32 devices in a mesh: dp: 8 (over z, x), row: 2 (over core), col: 2 (over y).
Axes of the slice: x: 2, y: 2, z: 4, core: 2. Of those that a mesh axis runs over, the one named last changes fastest.
Arguments:
- tokens: bfloat16 [8192, 2048], P('dp', ('row', 'col')), may hold values from -6 to 6
- teacher: bfloat16 [8192, 2048], P('dp', ('row', 'col')), may hold values from -6 to 6
- segments: int32 [8192], P('dp'), may hold values from 0 to 17, as said below
- valid_mask: int32 [8192], P('dp'), may hold values from 0 to 1, as said below
- query_weight: bfloat16 [2048, 2048], P('row', 'col'), may hold values from -0.1875 to 0.1875
- key_weight: bfloat16 [2048, 2048], P('row', 'col'), may hold values from -0.1875 to 0.1875
- value_weight: bfloat16 [2048, 2048], P('row', 'col'), may hold values from -0.125 to 0.125
- output_weight: bfloat16 [2048, 2048], P('col', 'row'), may hold values from -0.5 to 0.5
- gate_weight: bfloat16 [2048, 8192], P('row', 'col'), may hold values from -0.125 to 0.125
- up_weight: bfloat16 [2048, 8192], P('row', 'col'), may hold values from -0.125 to 0.125
- down_weight: bfloat16 [8192, 2048], P('col', 'row'), may hold values from -0.09375 to 0.09375
Outputs:
- output: bfloat16 [8192, 2048], P('dp', ('row', 'col'))
- loss: float32 [], replicated
- grad_tokens: float32 [8192, 2048], P('dp', ('row', 'col'))
- grad_query: float32 [2048, 2048], P('row', 'col')
- grad_key: float32 [2048, 2048], P('row', 'col')
- grad_value: float32 [2048, 2048], P('row', 'col')
- grad_output: float32 [2048, 2048], P('col', 'row')
- grad_gate: float32 [2048, 8192], P('row', 'col')
- grad_up: float32 [2048, 8192], P('row', 'col')
- grad_down: float32 [8192, 2048], P('col', 'row')
The draws below stay inside these ranges and needn't reach their ends.
Inputs may be any that keep to these rules, and one draw needn't show every extreme that they name: `segments`: within each sequence of 1024 tokens the segment numbers start at 0 and never fall; every segment but the last is a document of 60 to 800 tokens, and documents of exactly 60 and of exactly 800 tokens occur in every draw; the last segment of each sequence is padding of one or more tokens; some sequence in every draw reaches the largest segment number. `valid_mask`: 1 on the documents' tokens, 0 on each sequence's padding segment.
All inputs are finite; a program needn't handle non-finite values.
Results may differ from the reference program's by a relative error of at most 0.0095.
The reference program's roundings to bfloat16 on the way count: a program that leaves them out, or rounds other values in their place, can miss the bound.
Values may be sent and summed in bfloat16 or wider, within the bound.
A program may use at most 384 MiB of HBM per device.

```python
import math
import jax
import jax.numpy as jnp
from jax import lax

D = 2048
HEADS = 16
HEAD = 128
FF = 8192
LEN = 1024
DOC_MIN = 60
DOC_MAX = 800
TOKENS = 8192


def pack_layout(key):
    seq_total = TOKENS // LEN
    room = LEN // DOC_MIN + 2
    key_lengths, key_pick = jax.random.split(key)
    lengths = jax.random.randint(key_lengths, (seq_total, room), DOC_MIN, DOC_MAX + 1)
    chosen = jax.random.randint(key_pick, (), 0, seq_total)
    neighbour = (chosen + 1) % seq_total
    seq_ids = jnp.arange(seq_total)[:, None]
    doc_ids = jnp.arange(room)[None, :]
    lengths = jnp.where(seq_ids == chosen, DOC_MIN, lengths)
    lengths = jnp.where((seq_ids == neighbour) & (doc_ids == 0), DOC_MAX, lengths)
    finish = jnp.cumsum(lengths, axis=1)
    fitted = finish <= LEN - 1
    places = jnp.arange(LEN)
    passed = (finish[:, None, :] <= places[None, :, None]) & fitted[:, None, :]
    segment = jnp.sum(passed.astype(jnp.int32), axis=2)
    covered = jnp.max(jnp.where(fitted, finish, 0), axis=1)
    validity = (places[None, :] < covered[:, None]).astype(jnp.int32)
    return (segment.reshape(TOKENS).astype(jnp.int32), validity.reshape(TOKENS).astype(jnp.int32))


def draw_segments(key, part):
    layout = pack_layout(key)
    return layout[0]


def draw_valid_mask(key, part):
    layout = pack_layout(key)
    return layout[1]


def shard_levels(stream_key, extent, shards, low, top_value):
    gain = 1.0
    for dim, parts in shards:
        draws = jax.random.uniform(jax.random.fold_in(jax.random.fold_in(stream_key, 6), dim), (parts,), jnp.float32, low / len(shards), top_value / len(shards))
        gain = gain * jnp.repeat(jnp.exp(draws), extent[dim] // parts).reshape((-1,) + (1,) * (len(extent) - 1 - dim))
    return gain


def bell_draw(rng, shape, deviation, limit, cuts=(), kind=jnp.bfloat16):
    array = jax.random.normal(rng, shape, jnp.float32) * deviation
    if len(cuts) > 0:
        array = shard_levels(rng, shape, cuts, -0.22, 0.18) * array
    return jnp.clip(array, min=-limit, max=limit).astype(kind)


def setup_inputs(seed: int = 0) -> dict:
    streams_of = jax.random.split(jax.random.key(seed), 12)
    tokens = bell_draw(streams_of[0], (TOKENS, D), 1.0, 6.0, ((0, 8), (1, 4)))
    teacher = bell_draw(streams_of[1], (TOKENS, D), 1.0, 6.0, ((0, 8), (1, 4)))
    segments = draw_segments(jax.random.fold_in(streams_of[11], 71), 0)
    valid_mask = draw_valid_mask(jax.random.fold_in(streams_of[11], 71), 0)
    query_weight = bell_draw(streams_of[4], (D, D), (D // 2) ** -0.5, 0.1875, ((0, 2), (1, 2)))
    key_weight = bell_draw(streams_of[5], (D, D), (D // 2) ** -0.5, 0.1875, ((0, 2), (1, 2)))
    value_weight = bell_draw(streams_of[6], (D, D), D ** -0.5, 0.125, ((0, 2), (1, 2)))
    output_weight = bell_draw(streams_of[7], (D, D), (D // 16) ** -0.5, 0.5, ((0, 2), (1, 2)))
    gate_weight = bell_draw(streams_of[8], (D, FF), D ** -0.5, 0.125, ((0, 2), (1, 2)))
    up_weight = bell_draw(streams_of[9], (D, FF), D ** -0.5, 0.125, ((0, 2), (1, 2)))
    down_weight = bell_draw(streams_of[10], (FF, D), (FF // 2) ** -0.5, 0.09375, ((0, 2), (1, 2)))
    return {"tokens": tokens, "teacher": teacher, "segments": segments, "valid_mask": valid_mask, "query_weight": query_weight, "key_weight": key_weight, "value_weight": value_weight, "output_weight": output_weight, "gate_weight": gate_weight, "up_weight": up_weight, "down_weight": down_weight}


EPS = 1e-05
THETA = 10000.0
NEG = -1e+30

@jax.custom_vjp
def low(v):
    return lax.optimization_barrier(v.astype(jnp.bfloat16)).astype(jnp.float32)

@jax.custom_vjp
def low_back(v):
    return v

def low_keep(v):
    return (low(v), None)

def low_pass(kept, grad):
    return (grad,)

def back_keep(v):
    return (v, None)

def back_low(kept, grad):
    return (low(grad),)
low.defvjp(low_keep, low_pass)
low_back.defvjp(back_keep, back_low)

def product(left, right):
    return jnp.dot(left, right, precision=lax.Precision.HIGHEST, preferred_element_type=jnp.float32)

def normalize(operand):
    centre = operand - lax.optimization_barrier(jnp.mean(operand, axis=-1, keepdims=True))
    return centre * lax.rsqrt(lax.optimization_barrier(jnp.mean(centre * centre, axis=-1, keepdims=True)) + EPS)

def rope_tables(local_rows):
    half_width = HEAD // 2
    places = (jnp.arange(local_rows) % LEN).astype(jnp.float32)
    frequency = jnp.exp(jnp.arange(half_width).astype(jnp.float32) * (-2.0 * math.log(THETA) / HEAD))
    angles = places[:, None] * frequency[None, :]
    return (jnp.cos(angles), jnp.sin(angles))

def rotate(operand, cosine, sine_table):
    half_width = operand.shape[-1] // 2
    front_half = operand[..., :half_width]
    back_half = operand[..., half_width:]
    cosine = cosine[:, None, :]
    sine_table = sine_table[:, None, :]
    return jnp.concatenate([front_half * cosine - back_half * sine_table, back_half * cosine + front_half * sine_table], axis=-1)

def attend(queries, key_heads, value_heads, segment):
    block_rows = min(512, LEN)
    block_total = LEN // block_rows
    key_places = jnp.arange(LEN).astype(jnp.int32)
    factor = 1.0 / math.sqrt(HEAD)

    def one_block(block_index):
        offset = block_index * block_rows
        query_block = lax.dynamic_slice_in_dim(queries, offset, block_rows, 0)
        query_segs = lax.dynamic_slice_in_dim(segment, offset, block_rows, 0)
        query_places = offset + jnp.arange(block_rows).astype(jnp.int32)
        scores = jnp.einsum('qhd,khd->hqk', query_block, key_heads, precision=lax.Precision.HIGHEST) * factor
        scores = low_back(scores)
        allowed = (query_segs[:, None] == segment[None, :]) & (key_places[None, :] <= query_places[:, None])
        scores = jnp.where(allowed[None], scores, NEG)
        row_max = lax.optimization_barrier(jnp.max(scores, axis=-1, keepdims=True))
        shares = jnp.exp(scores - row_max)
        shares = shares / lax.optimization_barrier(jnp.sum(shares, axis=-1, keepdims=True))
        return jnp.einsum('hqk,khd->qhd', low(shares), value_heads, precision=lax.Precision.HIGHEST)
    blocks = lax.map(jax.checkpoint(one_block), jnp.arange(block_total, dtype=jnp.int32))
    return blocks.reshape(LEN, HEADS, HEAD)

def sequence(weights, seq_tokens, seq_teacher, segment, validity, cosine, sine_table):
    query_weight, key_weight, value_weight, output_weight, gate_weight, up_weight, down_weight = weights
    normed = low(normalize(seq_tokens))
    queries = low_back(product(normed, query_weight)).reshape(LEN, HEADS, HEAD)
    key_heads = low_back(product(normed, key_weight)).reshape(LEN, HEADS, HEAD)
    value_heads = low_back(product(normed, value_weight)).reshape(LEN, HEADS, HEAD)
    queries = low(rotate(queries, cosine, sine_table))
    key_heads = low(rotate(key_heads, cosine, sine_table))
    value_heads = low(value_heads)
    attended = attend(queries, key_heads, value_heads, segment).reshape(LEN, D)
    attended = low(low_back(attended))
    branch = low_back(product(attended, output_weight))
    hidden = seq_tokens + branch
    normed_two = low(normalize(hidden))
    gate_out = low_back(product(normed_two, gate_weight))
    up_out = low_back(product(normed_two, up_weight))
    act_low = low(jax.nn.silu(gate_out) * up_out)
    result = hidden + low_back(product(act_low, down_weight))
    error_term = result - seq_teacher
    return (result, 0.5 * jnp.sum(validity[:, None] * error_term * error_term))

def reference(tokens, teacher, segments, valid_mask, query_weight, key_weight, value_weight, output_weight, gate_weight, up_weight, down_weight):
    seq_total = TOKENS // LEN
    validity = valid_mask.astype(jnp.float32)
    token_total = jnp.sum(validity)
    cosine, sine_table = rope_tables(LEN)
    teacher_seqs = teacher.astype(jnp.float32).reshape(seq_total, LEN, D)
    segment_seqs = segments.reshape(seq_total, LEN)
    valid_seqs = validity.reshape(seq_total, LEN)
    checked = jax.checkpoint(sequence)

    def forward(tokens_f, weights):

        def scan_step(running, seq_items):
            seq_tokens, seq_teacher, segment, seq_valid = seq_items
            result, partial_sum = checked(weights, seq_tokens, seq_teacher, segment, seq_valid, cosine, sine_table)
            return (running + partial_sum, result)
        running, results = lax.scan(scan_step, jnp.zeros((), jnp.float32), (tokens_f.reshape(seq_total, LEN, D), teacher_seqs, segment_seqs, valid_seqs))
        return (results.reshape(TOKENS, D), running / token_total)
    weights = tuple((matrix.astype(jnp.float32) for matrix in (query_weight, key_weight, value_weight, output_weight, gate_weight, up_weight, down_weight)))
    (output, loss_value), pullback = jax.vjp(forward, tokens.astype(jnp.float32), weights)
    grad_tokens, grad_weights = pullback((jnp.zeros_like(output), jnp.ones_like(loss_value) * TOKENS))
    return (output.astype(jnp.bfloat16), loss_value, grad_tokens, grad_weights[0], grad_weights[1], grad_weights[2], grad_weights[3], grad_weights[4], grad_weights[5], grad_weights[6])
```

```python
import functools
import math

import jax
import jax.numpy as jnp
from jax import lax
from jax.experimental import pallas as pl
from jax.experimental.pallas import tpu as pltpu
from jax.sharding import PartitionSpec as P

D = 2048
HEAD = 128
LEN = 1024
EPS = 1e-05
THETA = 10000.0
NEG = -1e30
CHUNKS = 2

BF = jnp.bfloat16
F32 = jnp.float32


def rope_tables(places):
    half_width = HEAD // 2
    frequency = jnp.exp(
        jnp.arange(half_width).astype(F32) * (-2.0 * math.log(THETA) / HEAD)
    )
    angles = places.astype(F32)[:, None] * frequency[None, :]
    return (jnp.cos(angles), jnp.sin(angles))


def rotate(operand, cosine, sine_table):
    half_width = operand.shape[-1] // 2
    front_half = operand[..., :half_width]
    back_half = operand[..., half_width:]
    cosine = cosine[:, None, :]
    sine_table = sine_table[:, None, :]
    return jnp.concatenate(
        [
            front_half * cosine - back_half * sine_table,
            back_half * cosine + front_half * sine_table,
        ],
        axis=-1,
    )


def dot(left, right):
    return jnp.dot(left, right, preferred_element_type=F32)


def contract_rows(left, right):
    return lax.dot_general(left, right, (((0,), (0,)), ((), ())), preferred_element_type=F32)


def contract_cols(left, right):
    return lax.dot_general(left, right, (((1,), (1,)), ((), ())), preferred_element_type=F32)


def take(operand, index, size, axis):
    return lax.dynamic_slice_in_dim(operand, index * size, size, axis)


def swap_halves(operand, axis):
    half = operand.shape[axis] // 2
    return jnp.concatenate(
        [
            lax.slice_in_dim(operand, half, 2 * half, axis=axis),
            lax.slice_in_dim(operand, 0, half, axis=axis),
        ],
        axis=axis,
    )


def ordered(first, mine, other, axis):
    return jnp.concatenate(
        [jnp.where(first, mine, other), jnp.where(first, other, mine)], axis=axis
    )


def add_low(left, right):
    return (left.astype(F32) + right.astype(F32)).astype(BF)


MESH = pl.DeviceIdType.MESH


def line_kernel(sizes, spots, chunk, lag, ahead, deep, *refs):
    count = len(sizes)
    pieces = refs[:count]
    out = refs[count]
    held, got_in, got_mid, load, send_in, send_mid, send_out, send_side, in_sem, mid_sem, out_sem, side_sem, keep = refs[count + 1:]
    places = lax.axis_size("dp") // 2
    dp = lax.axis_index("dp")
    row = lax.axis_index("row")
    col = lax.axis_index("col")
    place, side = dp // 2, dp % 2
    half = places // 2
    low = place < half
    depth = jnp.where(low, place, places - 1 - place)
    is_mid = depth == half - 1
    is_end = depth == 0
    to_in = jnp.where(low, place + 1, place - 1)
    to_out = jnp.where(low, place - 1, place + 1)
    inner = (to_in * 2 + side, row, col)
    outer = (jnp.clip(to_out, 0, places - 1) * 2 + side, row, col)
    other = (dp + 1 - 2 * side, row, col)
    total_rows = held.shape[0]
    steps = total_rows // chunk

    loads = []
    for i in range(count):
        rows = sizes[i]
        at = pl.multiple_of(spots[i](row), 16)
        loads.append(pltpu.make_async_copy(pieces[i], held.at[pl.ds(at, rows)], load.at[i]))
        loads[-1].start()

    barrier = pltpu.get_barrier_semaphore()
    pl.semaphore_signal(barrier, inc=1, device_id=inner, device_id_type=MESH)
    pl.semaphore_signal(barrier, inc=1, device_id=other, device_id_type=MESH)

    @pl.when(jnp.logical_not(is_end))
    def _():
        pl.semaphore_signal(barrier, inc=1, device_id=outer, device_id_type=MESH)
        pl.semaphore_wait(barrier, 3)

    @pl.when(is_end)
    def _():
        pl.semaphore_wait(barrier, 2)

    for copy in loads:
        copy.wait()

    def at(t):
        return pl.ds(pl.multiple_of(t * chunk, chunk), chunk)

    def inward(t):
        return pltpu.make_async_remote_copy(
            src_ref=held.at[at(t)], dst_ref=got_in.at[at(t)], send_sem=send_in.at[t],
            recv_sem=in_sem.at[t], device_id=inner, device_id_type=MESH)

    def middle(t):
        return pltpu.make_async_remote_copy(
            src_ref=held.at[at(t)], dst_ref=got_mid.at[at(t)], send_sem=send_mid.at[t],
            recv_sem=mid_sem.at[t], device_id=inner, device_id_type=MESH)

    def outward(t, source):
        return pltpu.make_async_remote_copy(
            src_ref=source, dst_ref=out.at[side, at(t)], send_sem=send_out.at[t],
            recv_sem=out_sem.at[t], device_id=outer, device_id_type=MESH)

    def across(t, source):
        return pltpu.make_async_remote_copy(
            src_ref=source, dst_ref=out.at[side, at(t)], send_sem=send_side.at[t],
            recv_sem=side_sem.at[t], device_id=other, device_id_type=MESH)

    def store(t):
        return pltpu.make_async_copy(got_in.at[at(t)], out.at[side, at(t)], keep.at[t])

    def mid_loop(t, _):
        @pl.when(t < steps)
        def _():
            @pl.when(jnp.logical_not(is_end))
            def _():
                inward(t).wait_recv()
                held[at(t)] = (held[at(t)].astype(F32) + got_in[at(t)].astype(F32)).astype(BF)
            @pl.when(t >= deep)
            def _():
                middle(t - deep).wait_send()
            middle(t).start()

        @pl.when(t >= ahead)
        def _():
            u = t - ahead
            middle(u).wait_recv()
            got_in[at(u)] = (held[at(u)].astype(F32) + got_mid[at(u)].astype(F32)).astype(BF)
            store(u).start()
            @pl.when(u >= deep)
            def _():
                @pl.when(jnp.logical_not(is_end))
                def _():
                    outward(u - deep, got_in.at[at(u)]).wait_send()
                across(u - deep, got_in.at[at(u)]).wait_send()
            @pl.when(jnp.logical_not(is_end))
            def _():
                outward(u, got_in.at[at(u)]).start()
            across(u, got_in.at[at(u)]).start()
        return 0

    def far_loop(t, _):
        @pl.when(t < steps)
        def _():
            @pl.when(jnp.logical_not(is_end))
            def _():
                inward(t).wait_recv()
                held[at(t)] = (held[at(t)].astype(F32) + got_in[at(t)].astype(F32)).astype(BF)
            @pl.when(t >= deep)
            def _():
                inward(t - deep).wait_send()
            inward(t).start()

        @pl.when(t >= lag)
        def _():
            u = t - lag
            outward(u, out.at[side, at(u)]).wait_recv()
            @pl.when(u >= deep)
            def _():
                @pl.when(jnp.logical_not(is_end))
                def _():
                    outward(u - deep, out.at[side, at(u)]).wait_send()
                across(u - deep, out.at[side, at(u)]).wait_send()
            @pl.when(jnp.logical_not(is_end))
            def _():
                outward(u, out.at[side, at(u)]).start()
            across(u, out.at[side, at(u)]).start()
        return 0

    @pl.when(is_mid)
    def _():
        lax.fori_loop(0, steps + ahead, mid_loop, 0)
        def finish(t, _):
            store(t).wait()
            across(t, got_in.at[at(t)]).wait_recv()
            @pl.when(t >= steps - deep)
            def _():
                middle(t).wait_send()
                across(t, got_in.at[at(t)]).wait_send()
                @pl.when(jnp.logical_not(is_end))
                def _():
                    outward(t, got_in.at[at(t)]).wait_send()
            return 0
        lax.fori_loop(0, steps, finish, 0)

    @pl.when(jnp.logical_not(is_mid))
    def _():
        lax.fori_loop(0, steps + lag, far_loop, 0)
        def finish(t, _):
            across(t, out.at[side, at(t)]).wait_recv()
            @pl.when(t >= steps - deep)
            def _():
                inward(t).wait_send()
                across(t, out.at[side, at(t)]).wait_send()
                @pl.when(jnp.logical_not(is_end))
                def _():
                    outward(t, out.at[side, at(t)]).wait_send()
            return 0
        lax.fori_loop(0, steps, finish, 0)


def line_sum(pieces, spots, chunk, lag=8, ahead=2, deep=2):
    sizes = [p.shape[0] for p in pieces]
    rows, width = sum(sizes), pieces[0].shape[1]
    steps = rows // chunk
    dma = pltpu.SemaphoreType.DMA
    return pl.pallas_call(
        functools.partial(line_kernel, sizes, spots, chunk, lag, ahead, deep),
        out_shape=jax.ShapeDtypeStruct((2, rows, width), BF),
        in_specs=[pl.BlockSpec(memory_space=pl.ANY)] * len(pieces),
        out_specs=pl.BlockSpec(memory_space=pl.ANY),
        scratch_shapes=[pltpu.VMEM((rows, width), BF)] * 3 + [dma((len(pieces),))] + [dma((steps,))] * 9,
        compiler_params=pltpu.CompilerParams(collective_id=0, has_side_effects=True, vmem_limit_bytes=56 * 2**20),
        name="line_sum",
    )(*pieces)


def pack(operand, width):
    rows, columns = operand.shape
    if columns == width:
        return operand
    if columns > width:
        return jnp.concatenate(
            [operand[:, i : i + width] for i in range(0, columns, width)], axis=0
        )
    times = width // columns
    step = rows // times
    return jnp.concatenate([operand[i * step : (i + 1) * step] for i in range(times)], axis=1)


def unpack(operand, columns):
    rows, width = operand.shape
    if columns == width:
        return operand
    if columns > width:
        step = rows * width // columns
        return jnp.concatenate(
            [operand[i * step : (i + 1) * step] for i in range(columns // width)], axis=1
        )
    return jnp.concatenate(
        [operand[:, i : i + columns] for i in range(0, width, columns)], axis=0
    )


def butterfly(operand, axis):
    size = lax.axis_size(axis)
    step = 1
    while step < size:
        operand = operand + lax.ppermute(operand, axis, [(i, i ^ step) for i in range(size)])
        step *= 2
    return operand


def allowed_pairs(query_segs, query_places, key_segs, key_places):
    return (query_segs[:, None] == key_segs[None, :]) & (
        key_places[None, :] <= query_places[:, None]
    )


def attend(queries, key_heads, value_heads, allowed):
    scores = jnp.einsum("qhd,khd->hqk", queries, key_heads, preferred_element_type=F32)
    scores = jnp.where(allowed[None], scores * (1.0 / math.sqrt(HEAD)), NEG)
    row_max = jnp.max(scores, axis=-1, keepdims=True)
    shares = jnp.exp(scores - row_max)
    totals = jnp.sum(shares, axis=-1, keepdims=True)
    shares = (shares / totals).astype(BF)
    attended = jnp.einsum("hqk,khd->qhd", shares, value_heads, preferred_element_type=F32)
    return attended.astype(BF), row_max + jnp.log(totals)


def attend_back(queries, key_heads, value_heads, allowed, logsum, gradient):
    factor = 1.0 / math.sqrt(HEAD)
    scores = jnp.einsum("qhd,khd->hqk", queries, key_heads, preferred_element_type=F32)
    scores = jnp.where(allowed[None], scores * factor, NEG)
    shares = jnp.exp(scores - logsum)
    grad_shares = jnp.einsum("qhd,khd->hqk", gradient, value_heads, preferred_element_type=F32)
    centre = jnp.sum(shares * grad_shares, axis=-1, keepdims=True)
    grad_scores = (shares * (grad_shares - centre)).astype(BF)
    grad_q = jnp.einsum("hqk,khd->qhd", grad_scores, key_heads, preferred_element_type=F32)
    grad_k = jnp.einsum("hqk,qhd->khd", grad_scores, queries, preferred_element_type=F32)
    grad_v = jnp.einsum("hqk,qhd->khd", shares.astype(BF), gradient, preferred_element_type=F32)
    return grad_q * factor, grad_k * factor, grad_v


def moments(operand):
    average = jnp.mean(operand, axis=-1, keepdims=True)
    centre = operand - average
    factor = lax.rsqrt(jnp.mean(centre * centre, axis=-1, keepdims=True) + EPS)
    return average, factor


def normalize_back(gradient, normed, factor):
    mean = jnp.mean(gradient, axis=-1, keepdims=True)
    crossed = jnp.mean(gradient * normed, axis=-1, keepdims=True)
    return factor * (gradient - mean - normed * crossed)


def body(
    tokens,
    teacher,
    segments,
    valid_mask,
    query_weight,
    key_weight,
    value_weight,
    output_weight,
    gate_weight,
    up_weight,
    down_weight,
):
    rows = tokens.shape[0]
    cols = lax.axis_size("col")
    row = lax.axis_index("row")
    col = lax.axis_index("col")
    block = tokens.shape[1]
    half_width = block * cols
    wide = query_weight.shape[1] // 2
    hidden_units = gate_weight.shape[1] // 2
    local_heads = wide // HEAD
    span = rows // CHUNKS
    own = span // 2
    first_row = row == 0
    side = lax.axis_index("dp") % 2
    sides = [(i, i ^ 1) for i in range(lax.axis_size("dp"))]
    part_units = hidden_units // 2
    part_wide = wide // 2

    def swap(operand):
        return lax.ppermute(operand, "row", [(0, 1), (1, 0)])

    def own_columns(weight, size):
        kept, sent = take(weight, row, size, 1), take(weight, 1 - row, size, 1)
        return jnp.concatenate([kept, swap(sent)], axis=0)

    def own_rows(weight, size):
        kept, sent = take(weight, row, size, 0), take(weight, 1 - row, size, 0)
        return jnp.concatenate([kept, swap(sent)], axis=1)

    def cross(operand):
        return lax.ppermute(operand, "dp", sides)

    def gather_blocks(operand):
        if cols == 2:
            got = lax.ppermute(operand, "col", [(0, 1), (1, 0)])
            return ordered(col == 0, operand, got, 1)
        return lax.all_gather(operand, "col", axis=1, tiled=True)

    def sum_chips(mine, sent):
        if cols == 2:
            return mine + lax.ppermute(sent.astype(BF), "col", [(0, 1), (1, 0)]).astype(F32)
        return mine + (lax.psum(sent, "col") - sent)

    def both_cores(kept):
        return jnp.concatenate([kept, swap(swap_halves(kept, 1))], axis=0)

    def sum_cores(part):
        sent = swap_halves(part[own:], 1).astype(BF)
        return part[:own] + swap(sent).astype(F32)

    def local_order(vector):
        pieces = []
        for j in range(CHUNKS):
            piece = vector[j * span : (j + 1) * span]
            pieces.append(ordered(first_row, piece[:own], piece[own:], 0))
        return pieces

    validity = valid_mask.astype(F32)
    token_total = butterfly(jnp.sum(validity).reshape(1, 1), "dp")
    scale = (rows * lax.axis_size("dp")) / token_total
    segs = local_order(segments)
    places = local_order(jnp.arange(rows, dtype=jnp.int32))
    valids = [v[:own, None] for v in local_order(validity)]

    qkv_weight = own_columns(
        jnp.concatenate(
            [
                jnp.concatenate(
                    [
                        lax.slice_in_dim(w, h * wide, (h + 1) * wide, axis=1)
                        for w in (query_weight, key_weight, value_weight)
                    ],
                    axis=1,
                )
                for h in range(2)
            ],
            axis=1,
        ),
        3 * wide,
    )
    out_weight = own_rows(output_weight, wide)
    gates = own_columns(gate_weight, hidden_units)
    ups = own_columns(up_weight, hidden_units)
    downs = own_rows(down_weight, hidden_units)

    inputs, first_stats, low_first = [], [], []
    for j in range(CHUNKS):
        piece = tokens[j * span : (j + 1) * span]
        piece = ordered(first_row, piece[:own], piece[own:], 0)
        half = gather_blocks(piece)
        whole = jnp.concatenate([half, swap(swap_halves(half, 0))], axis=1)
        whole_f = whole.astype(F32)
        average, factor = moments(whole_f)
        inputs.append(whole[:own])
        first_stats.append((average[:own], factor[:own]))
        low_first.append(((whole_f - average) * factor).astype(BF))

    tables = [rope_tables(p) for p in places]
    query_heads, key_heads, value_heads = [], [], []
    attended, logsums = [], []
    hidden, second_stats, low_second = [], [], []
    for j in range(CHUNKS):
        raw = dot(low_first[j], qkv_weight).reshape(span, 3, local_heads, HEAD)
        query_heads.append(rotate(raw[:, 0], *tables[j]).astype(BF))
        key_heads.append(rotate(raw[:, 1], *tables[j]).astype(BF))
        value_heads.append(raw[:, 2].astype(BF))

    def keys_to(j):
        return (
            jnp.concatenate(key_heads[: j + 1], axis=0),
            jnp.concatenate(value_heads[: j + 1], axis=0),
            allowed_pairs(
                segs[j],
                places[j],
                jnp.concatenate(segs[: j + 1]),
                jnp.concatenate(places[: j + 1]),
            ),
        )

    for j in range(CHUNKS):
        keys, values, allowed = keys_to(j)
        heads, logsum = attend(query_heads[j], keys, values, allowed)
        attended.append(heads.reshape(span, wide))
        logsums.append(logsum)
        part = sum_cores(dot(attended[j], out_weight))
        hidden.append(inputs[j].astype(F32) + sum_chips(part, part))
        average, factor = moments(hidden[j])
        second_stats.append((average, factor))
        low_second.append(both_cores(((hidden[j] - average) * factor).astype(BF)))

    gate_outs, up_outs, acts = [], [], []
    outputs, grad_results, low_results = [], [], []
    error_sum = jnp.zeros((), F32)
    for j in range(CHUNKS):
        gate_outs.append(dot(low_second[j], gates))
        up_outs.append(dot(low_second[j], ups))
        acts.append((jax.nn.silu(gate_outs[j]) * up_outs[j]).astype(BF))
        part = sum_cores(dot(acts[j], downs))

        piece = teacher[j * span : (j + 1) * span]
        piece = ordered(first_row, piece[:own], piece[own:], 0)
        near, far = piece[:own].astype(F32), swap(piece[own:]).astype(F32)
        blocks = [jnp.where(col == b, near, 0.0) for b in range(cols)]
        blocks += [jnp.where(col == b, far, 0.0) for b in range(cols)]
        part = part - jnp.concatenate(blocks, axis=1)
        error = hidden[j] + sum_chips(part, part)

        near_error, far_error = take(error[:, :half_width], col, block, 1), take(
            error[:, half_width:], col, block, 1
        )
        near_out, far_out = near_error + near, far_error + far
        outputs.append(
            ordered(first_row, near_out.astype(BF), swap(far_out.astype(BF)), 0)
        )
        error_sum = error_sum + 0.5 * jnp.sum(
            valids[j] * (near_error * near_error + far_error * far_error)
        )
        grad_results.append(scale * valids[j] * error)
        low_results.append(both_cores(grad_results[j].astype(BF)))
    output = jnp.concatenate(outputs, axis=0)

    def with_side(mine, other):
        return jnp.concatenate([*mine, *other], axis=0)

    def split_rows(full):
        half = full.shape[0] // 2
        return full[:half], swap(full[half:])

    def split_cols(full):
        half = full.shape[1] // 2
        return full[:, :half], swap(full[:, half:])

    results = with_side(low_results, [cross(g) for g in low_results])
    act = with_side(
        [take(a, side, part_units, 1) for a in acts],
        [cross(take(a, 1 - side, part_units, 1)) for a in acts],
    )
    twos = with_side(low_second, [cross(a) for a in low_second])
    down_pair = split_cols(contract_rows(act, results).astype(BF))

    gate_backs, up_backs = [], []
    for j in range(CHUNKS):
        grad_act = contract_cols(low_results[j], downs)
        sigmoid = jax.nn.sigmoid(gate_outs[j])
        gate_backs.append(
            (
                grad_act * up_outs[j] * sigmoid * (1.0 + gate_outs[j] * (1.0 - sigmoid))
            ).astype(BF)
        )
        up_backs.append((grad_act * gate_outs[j] * sigmoid).astype(BF))

    def input_pair(lefts, rights, size):
        right = with_side(
            [take(g, side, size, 1) for g in rights],
            [cross(take(g, 1 - side, size, 1)) for g in rights],
        )
        return split_rows(contract_rows(lefts, right).astype(BF))

    gate_pair = input_pair(twos, gate_backs, part_units)
    up_pair = input_pair(twos, up_backs, part_units)

    grad_hiddens, low_hiddens = [], []
    for j in range(CHUNKS):
        part = sum_cores(contract_cols(gate_backs[j], gates) + contract_cols(up_backs[j], ups))
        gradient = sum_chips(part, part)
        average, factor = second_stats[j]
        normed = (hidden[j] - average) * factor
        grad_hiddens.append(grad_results[j] + normalize_back(gradient, normed, factor))
        low_hiddens.append(both_cores(grad_hiddens[j].astype(BF)))
    low_hidden = jnp.concatenate(low_hiddens, axis=0)

    grad_out = contract_rows(jnp.concatenate(attended, axis=0), low_hidden).astype(BF)
    grad_out = add_low(
        take(grad_out, side, part_wide, 0), cross(take(grad_out, 1 - side, part_wide, 0))
    )
    out_pair = split_cols(grad_out)
    grad_attended = contract_cols(low_hidden, out_weight).astype(BF)
    grad_attended = grad_attended.reshape(rows, local_heads, HEAD)
    grad_q, grad_k, grad_v = [], [], []
    for j in range(CHUNKS):
        keys, values, allowed = keys_to(j)
        parts = attend_back(
            query_heads[j],
            keys,
            values,
            allowed,
            logsums[j],
            grad_attended[j * span : (j + 1) * span],
        )
        grad_q.append(parts[0])
        for i in range(j + 1):
            at = slice(i * span, (i + 1) * span)
            if i == j:
                grad_k.append(parts[1][at])
                grad_v.append(parts[2][at])
            else:
                grad_k[i] = grad_k[i] + parts[1][at]
                grad_v[i] = grad_v[i] + parts[2][at]
    backs = []
    for j in range(CHUNKS):
        cosine, sine_table = tables[j]
        backs.append(
            jnp.concatenate(
                [
                    rotate(grad_q[j], cosine, -sine_table).reshape(span, wide),
                    rotate(grad_k[j], cosine, -sine_table).reshape(span, wide),
                    grad_v[j].reshape(span, wide),
                ],
                axis=1,
            ).astype(BF)
        )
    ones = with_side(low_first, [cross(a) for a in low_first])
    backs_wide = []
    for which in range(2):
        chosen = side if which == 0 else 1 - side
        backs_wide.append(
            [
                jnp.concatenate(
                    [
                        take(g[:, i * wide : (i + 1) * wide], chosen, part_wide, 1)
                        for i in range(3)
                    ],
                    axis=1,
                )
                for g in backs
            ]
        )
    qkv_pair = split_rows(
        contract_rows(
            ones, with_side(backs_wide[0], [cross(g) for g in backs_wide[1]])
        ).astype(BF)
    )
    three = [
        ordered(
            first_row,
            qkv_pair[0][:, i * part_wide : (i + 1) * part_wide],
            qkv_pair[1][:, i * part_wide : (i + 1) * part_wide],
            1,
        )
        for i in range(3)
    ]
    pieces, spots, starts = [], [], []
    total = 0
    for pair in (down_pair, gate_pair, up_pair, out_pair):
        packed = [pack(p, half_width) for p in pair]
        size = packed[0].shape[0]
        pieces += packed
        spots += [
            lambda r, total=total, size=size: total + r * size,
            lambda r, total=total, size=size: total + (1 - r) * size,
        ]
        starts.append((total, size))
        total += 2 * size
    for item in (jnp.concatenate(three[:2], axis=1), three[2]):
        packed = pack(item, half_width)
        size = packed.shape[0]
        pieces.append(packed)
        spots.append(lambda r, total=total: total + 0 * r)
        starts.append((total, size))
        total += size
    sums = line_sum(pieces, spots, chunk=min(256, total // 8))

    def blocks_of(which, columns):
        start, size = starts[which]
        return [
            unpack(sums[x, start + s * size : start + (s + 1) * size], columns)
            for s in range(2)
            for x in range(2)
        ]

    grad_down = jnp.concatenate(blocks_of(0, half_width), axis=0).astype(F32)
    grad_gate = jnp.concatenate(blocks_of(1, part_units), axis=1).astype(F32)
    grad_up = jnp.concatenate(blocks_of(2, part_units), axis=1).astype(F32)
    grad_output = jnp.concatenate(blocks_of(3, half_width), axis=0).astype(F32)
    three = [[], [], []]
    qk = [unpack(sums[x, starts[4][0] : starts[4][0] + starts[4][1]], 4 * part_wide) for x in range(2)]
    v = [unpack(sums[x, starts[5][0] : starts[5][0] + starts[5][1]], 2 * part_wide) for x in range(2)]
    for s in range(2):
        for x in range(2):
            at = s * part_wide
            three[0].append(qk[x][:, at : at + part_wide])
            three[1].append(qk[x][:, 2 * part_wide + at : 2 * part_wide + at + part_wide])
            three[2].append(v[x][:, at : at + part_wide])
    grad_query, grad_key, grad_value = (
        jnp.concatenate(t, axis=1).astype(F32) for t in three
    )
    grad_tokens = []
    for j in range(CHUNKS):
        part = sum_cores(contract_cols(backs[j], qkv_weight))
        gradient = sum_chips(part, part)
        average, factor = first_stats[j]
        normed = (inputs[j].astype(F32) - average) * factor
        grads = grad_hiddens[j] + normalize_back(gradient, normed, factor)
        near = take(grads[:, :half_width], col, block, 1)
        far = take(grads[:, half_width:], col, block, 1)
        grad_tokens.append(ordered(first_row, near, swap(far), 0))
    error_sum = error_sum.reshape(1, 1)
    for axis in ("row", "col", "dp"):
        error_sum = butterfly(error_sum, axis)
    loss_value = (error_sum / token_total)[0, 0]
    return (
        output,
        loss_value,
        jnp.concatenate(grad_tokens, axis=0),
        grad_query,
        grad_key,
        grad_value,
        grad_output,
        grad_gate,
        grad_up,
        grad_down,
    )


def solution(mesh):
    features = P("dp", ("row", "col"))
    into, back = P("row", "col"), P("col", "row")
    in_specs = (features, features, P("dp"), P("dp"), into, into, into, back, into, into, back)
    out_specs = (features, P(), features, into, into, into, back, into, into, back)
    return jax.shard_map(body, mesh=mesh, in_specs=in_specs, out_specs=out_specs, check_vma=False)
```

```python
import functools
import math

import jax
import jax.numpy as jnp
from jax import lax
from jax.experimental import pallas as pl
from jax.experimental.pallas import tpu as pltpu
from jax.sharding import PartitionSpec as P

D = 2048
HEAD = 128
LEN = 1024
EPS = 1e-05
THETA = 10000.0
NEG = -1e30

BF = jnp.bfloat16
F32 = jnp.float32


def rope_tables(places):
    half_width = HEAD // 2
    frequency = jnp.exp(
        jnp.arange(half_width).astype(F32) * (-2.0 * math.log(THETA) / HEAD)
    )
    angles = places.astype(F32)[:, None] * frequency[None, :]
    cosine, sine_table = jnp.cos(angles), jnp.sin(angles)
    return (
        jnp.concatenate([cosine, cosine], axis=1),
        jnp.concatenate([-sine_table, sine_table], axis=1),
    )


def dot(left, right):
    return jnp.dot(left, right, preferred_element_type=F32)


def contract_rows(left, right):
    return lax.dot_general(left, right, (((0,), (0,)), ((), ())), preferred_element_type=F32)


def contract_cols(left, right):
    return lax.dot_general(left, right, (((1,), (1,)), ((), ())), preferred_element_type=F32)


def take(operand, index, size, axis):
    return lax.dynamic_slice_in_dim(operand, index * size, size, axis)


def swap_halves(operand, axis):
    half = operand.shape[axis] // 2
    return jnp.concatenate(
        [
            lax.slice_in_dim(operand, half, 2 * half, axis=axis),
            lax.slice_in_dim(operand, 0, half, axis=axis),
        ],
        axis=axis,
    )


def ordered(first, mine, other, axis):
    return jnp.concatenate(
        [jnp.where(first, mine, other), jnp.where(first, other, mine)], axis=axis
    )


def add_low(left, right):
    return (left.astype(F32) + right.astype(F32)).astype(BF)


MESH = pl.DeviceIdType.MESH


def line_kernel(sizes, spots, chunk, lag, ahead, deep, *refs):
    count = len(sizes)
    pieces = refs[:count]
    out = refs[count]
    held, got_in, got_mid, load, send_in, send_mid, send_out, send_side, in_sem, mid_sem, out_sem, side_sem, keep = refs[count + 1:]
    places = lax.axis_size("dp") // 2
    dp = lax.axis_index("dp")
    row = lax.axis_index("row")
    col = lax.axis_index("col")
    place, side = dp // 2, dp % 2
    half = places // 2
    low = place < half
    depth = jnp.where(low, place, places - 1 - place)
    is_mid = depth == half - 1
    is_end = depth == 0
    to_in = jnp.where(low, place + 1, place - 1)
    to_out = jnp.where(low, place - 1, place + 1)
    inner = (to_in * 2 + side, row, col)
    outer = (jnp.clip(to_out, 0, places - 1) * 2 + side, row, col)
    other = (dp + 1 - 2 * side, row, col)
    total_rows = held.shape[0]
    steps = total_rows // chunk

    loads = []
    for i in range(count):
        rows = sizes[i]
        at = pl.multiple_of(spots[i](row), 16)
        loads.append(pltpu.make_async_copy(pieces[i], held.at[pl.ds(at, rows)], load.at[i]))
        loads[-1].start()

    barrier = pltpu.get_barrier_semaphore()
    pl.semaphore_signal(barrier, inc=1, device_id=inner, device_id_type=MESH)
    pl.semaphore_signal(barrier, inc=1, device_id=other, device_id_type=MESH)

    @pl.when(jnp.logical_not(is_end))
    def _():
        pl.semaphore_signal(barrier, inc=1, device_id=outer, device_id_type=MESH)
        pl.semaphore_wait(barrier, 3)

    @pl.when(is_end)
    def _():
        pl.semaphore_wait(barrier, 2)

    for copy in loads:
        copy.wait()

    def at(t):
        return pl.ds(pl.multiple_of(t * chunk, chunk), chunk)

    def inward(t):
        return pltpu.make_async_remote_copy(
            src_ref=held.at[at(t)], dst_ref=got_in.at[at(t)], send_sem=send_in.at[t],
            recv_sem=in_sem.at[t], device_id=inner, device_id_type=MESH)

    def middle(t):
        return pltpu.make_async_remote_copy(
            src_ref=held.at[at(t)], dst_ref=got_mid.at[at(t)], send_sem=send_mid.at[t],
            recv_sem=mid_sem.at[t], device_id=inner, device_id_type=MESH)

    def outward(t, source):
        return pltpu.make_async_remote_copy(
            src_ref=source, dst_ref=out.at[side, at(t)], send_sem=send_out.at[t],
            recv_sem=out_sem.at[t], device_id=outer, device_id_type=MESH)

    def across(t, source):
        return pltpu.make_async_remote_copy(
            src_ref=source, dst_ref=out.at[side, at(t)], send_sem=send_side.at[t],
            recv_sem=side_sem.at[t], device_id=other, device_id_type=MESH)

    def store(t):
        return pltpu.make_async_copy(got_in.at[at(t)], out.at[side, at(t)], keep.at[t])

    def mid_loop(t, _):
        @pl.when(t < steps)
        def _():
            @pl.when(jnp.logical_not(is_end))
            def _():
                inward(t).wait_recv()
                held[at(t)] = (held[at(t)].astype(F32) + got_in[at(t)].astype(F32)).astype(BF)
            @pl.when(t >= deep)
            def _():
                middle(t - deep).wait_send()
            middle(t).start()

        @pl.when(t >= ahead)
        def _():
            u = t - ahead
            middle(u).wait_recv()
            got_in[at(u)] = (held[at(u)].astype(F32) + got_mid[at(u)].astype(F32)).astype(BF)
            store(u).start()
            @pl.when(u >= deep)
            def _():
                @pl.when(jnp.logical_not(is_end))
                def _():
                    outward(u - deep, got_in.at[at(u)]).wait_send()
                across(u - deep, got_in.at[at(u)]).wait_send()
            @pl.when(jnp.logical_not(is_end))
            def _():
                outward(u, got_in.at[at(u)]).start()
            across(u, got_in.at[at(u)]).start()
        return 0

    def far_loop(t, _):
        @pl.when(t < steps)
        def _():
            @pl.when(jnp.logical_not(is_end))
            def _():
                inward(t).wait_recv()
                held[at(t)] = (held[at(t)].astype(F32) + got_in[at(t)].astype(F32)).astype(BF)
            @pl.when(t >= deep)
            def _():
                inward(t - deep).wait_send()
            inward(t).start()

        @pl.when(t >= lag)
        def _():
            u = t - lag
            outward(u, out.at[side, at(u)]).wait_recv()
            @pl.when(u >= deep)
            def _():
                @pl.when(jnp.logical_not(is_end))
                def _():
                    outward(u - deep, out.at[side, at(u)]).wait_send()
                across(u - deep, out.at[side, at(u)]).wait_send()
            @pl.when(jnp.logical_not(is_end))
            def _():
                outward(u, out.at[side, at(u)]).start()
            across(u, out.at[side, at(u)]).start()
        return 0

    @pl.when(is_mid)
    def _():
        lax.fori_loop(0, steps + ahead, mid_loop, 0)
        def finish(t, _):
            store(t).wait()
            across(t, got_in.at[at(t)]).wait_recv()
            @pl.when(t >= steps - deep)
            def _():
                middle(t).wait_send()
                across(t, got_in.at[at(t)]).wait_send()
                @pl.when(jnp.logical_not(is_end))
                def _():
                    outward(t, got_in.at[at(t)]).wait_send()
            return 0
        lax.fori_loop(0, steps, finish, 0)

    @pl.when(jnp.logical_not(is_mid))
    def _():
        lax.fori_loop(0, steps + lag, far_loop, 0)
        def finish(t, _):
            across(t, out.at[side, at(t)]).wait_recv()
            @pl.when(t >= steps - deep)
            def _():
                inward(t).wait_send()
                across(t, out.at[side, at(t)]).wait_send()
                @pl.when(jnp.logical_not(is_end))
                def _():
                    outward(t, out.at[side, at(t)]).wait_send()
            return 0
        lax.fori_loop(0, steps, finish, 0)


def line_sum(pieces, spots, chunk, lag=8, ahead=2, deep=2):
    sizes = [p.shape[0] for p in pieces]
    rows, width = sum(sizes), pieces[0].shape[1]
    steps = rows // chunk
    dma = pltpu.SemaphoreType.DMA
    return pl.pallas_call(
        functools.partial(line_kernel, sizes, spots, chunk, lag, ahead, deep),
        out_shape=jax.ShapeDtypeStruct((2, rows, width), BF),
        in_specs=[pl.BlockSpec(memory_space=pl.ANY)] * len(pieces),
        out_specs=pl.BlockSpec(memory_space=pl.ANY),
        scratch_shapes=[pltpu.VMEM((rows, width), BF)] * 3 + [dma((len(pieces),))] + [dma((steps,))] * 9,
        compiler_params=pltpu.CompilerParams(collective_id=0, has_side_effects=True, vmem_limit_bytes=56 * 2**20),
        name="line_sum",
    )(*pieces)


def pack(operand, width):
    rows, columns = operand.shape
    if columns == width:
        return operand
    if columns > width:
        return jnp.concatenate(
            [operand[:, i : i + width] for i in range(0, columns, width)], axis=0
        )
    times = width // columns
    step = rows // times
    return jnp.concatenate([operand[i * step : (i + 1) * step] for i in range(times)], axis=1)


def unpack(operand, columns):
    rows, width = operand.shape
    if columns == width:
        return operand
    if columns > width:
        step = rows * width // columns
        return jnp.concatenate(
            [operand[i * step : (i + 1) * step] for i in range(columns // width)], axis=1
        )
    return jnp.concatenate(
        [operand[:, i : i + columns] for i in range(0, width, columns)], axis=0
    )


def butterfly(operand, axis):
    size = lax.axis_size(axis)
    step = 1
    while step < size:
        operand = operand + lax.ppermute(operand, axis, [(i, i ^ step) for i in range(size)])
        step *= 2
    return operand


def turned(operand, cosine, sine_table):
    return operand * cosine + pltpu.roll(operand, HEAD // 2, 1) * sine_table


def allowed_pairs(spot_col, spot_row):
    return (spot_col[:, 0:1] == spot_row[0:1, :]) & (spot_row[1:2, :] <= spot_col[:, 1:2])


def attention_kernel(
    x_ref, own_ref, got_ref, out_own, out_got, cos_ref, sin_ref, col_ref, row_ref, *refs
):
    earlier, (q_out, k_out, v_out, att_out, lse_out, kept, sent) = refs[:-7], refs[-7:]
    half = x_ref.shape[1] // 2
    wide = out_own.shape[0]
    own = kept.shape[0]
    near, far = x_ref[:, :half], x_ref[:, half:]
    cosine, sine_table = cos_ref[...], sin_ref[...]
    for which, out in enumerate((q_out, k_out, v_out)):
        at = slice(which * wide, (which + 1) * wide)
        raw = dot(near, own_ref[:, at]) + dot(far, got_ref[:, at])
        for h in range(wide // HEAD):
            head = slice(h * HEAD, (h + 1) * HEAD)
            value = raw[:, head]
            if which < 2:
                value = turned(value, cosine, sine_table)
            out[:, head] = value.astype(BF)
    allowed = allowed_pairs(col_ref[...], row_ref[...])
    for h in range(wide // HEAD):
        head = slice(h * HEAD, (h + 1) * HEAD)
        keys, values = k_out[:, head], v_out[:, head]
        if earlier:
            keys = jnp.concatenate([earlier[0][:, head], keys], axis=0)
            values = jnp.concatenate([earlier[1][:, head], values], axis=0)
        scores = contract_cols(q_out[:, head], keys) * (1.0 / math.sqrt(HEAD))
        scores = jnp.where(allowed, scores, NEG)
        row_max = jnp.max(scores, axis=-1, keepdims=True)
        shares = jnp.exp(scores - row_max)
        totals = jnp.sum(shares, axis=-1, keepdims=True)
        shares = (shares / totals).astype(BF)
        att_out[:, head] = dot(shares, values).astype(BF)
        lse_out[:, head] = jnp.broadcast_to(row_max + jnp.log(totals), (2 * own, HEAD))
    near, far = dot(att_out[...], out_own[...]), dot(att_out[...], out_got[...])
    kept[:, :half] = near[:own]
    kept[:, half:] = far[:own]
    sent[:, :half] = far[own:].astype(BF)
    sent[:, half:] = near[own:].astype(BF)


def attention_back_kernel(
    g_ref, out_own, out_got, cos_ref, sin_ref, col_ref, row_ref, lse_ref, q_ref, k_ref, v_ref, *refs
):
    span, wide = q_ref.shape
    half = g_ref.shape[1] // 2
    factor = 1.0 / math.sqrt(HEAD)
    cosine, sine_table = cos_ref[...], -sin_ref[...]
    grads = contract_cols(g_ref[:, :half], out_own[...])
    grads = (grads + contract_cols(g_ref[:, half:], out_got[...])).astype(BF)
    allowed = allowed_pairs(col_ref[...], row_ref[...])
    last = len(refs) > 3
    for h in range(wide // HEAD):
        head = slice(h * HEAD, (h + 1) * HEAD)
        queries, gradient = q_ref[:, head], grads[:, head]
        keys, values = k_ref[:, head], v_ref[:, head]
        if last:
            keys = jnp.concatenate([refs[0][:, head], keys], axis=0)
            values = jnp.concatenate([refs[1][:, head], values], axis=0)
        scores = jnp.where(allowed, contract_cols(queries, keys) * factor, NEG)
        shares = jnp.exp(scores - lse_ref[:, h * HEAD : h * HEAD + 1])
        grad_shares = contract_cols(gradient, values)
        centre = jnp.sum(shares * grad_shares, axis=-1, keepdims=True)
        grad_scores = (shares * (grad_shares - centre)).astype(BF)
        grad_q = turned(dot(grad_scores, keys) * factor, cosine, sine_table)
        grad_k = contract_rows(grad_scores, queries) * factor
        grad_v = contract_rows(shares.astype(BF), gradient)
        if not last:
            q_out, k_out, v_out = refs
            q_out[:, head] = grad_q.astype(BF)
            k_out[:, head] = grad_k
            v_out[:, head] = grad_v
        else:
            cos_first, sin_first, k_part, v_part, first_out, back_out = refs[2:]
            back_out[:, head] = grad_q.astype(BF)
            at = slice(wide + h * HEAD, wide + (h + 1) * HEAD)
            back_out[:, at] = turned(grad_k[span:], cosine, sine_table).astype(BF)
            first = grad_k[:span] + k_part[:, head]
            first_out[:, head] = turned(first, cos_first[...], -sin_first[...]).astype(BF)
            at = slice(2 * wide + h * HEAD, 2 * wide + (h + 1) * HEAD)
            back_out[:, at] = grad_v[span:].astype(BF)
            at = slice(wide + h * HEAD, wide + (h + 1) * HEAD)
            first_out[:, at] = (grad_v[:span] + v_part[:, head]).astype(BF)


def in_vmem(kernel, name, out_shape, operands):
    return pl.pallas_call(
        kernel,
        out_shape=out_shape,
        in_specs=[pl.BlockSpec(memory_space=pltpu.VMEM)] * len(operands),
        out_specs=[pl.BlockSpec(memory_space=pltpu.VMEM)] * len(out_shape),
        compiler_params=pltpu.CompilerParams(vmem_limit_bytes=52 * 2**20),
        cost_estimate=pl.CostEstimate(
            flops=8 * 10**9, bytes_accessed=2 * 10**7, transcendentals=2 * 10**6
        ),
        name=name,
    )(*operands)


def moments(operand):
    average = jnp.mean(operand, axis=-1, keepdims=True)
    centre = operand - average
    factor = lax.rsqrt(jnp.mean(centre * centre, axis=-1, keepdims=True) + EPS)
    return average, factor


def normalize_back(gradient, normed, factor):
    mean = jnp.mean(gradient, axis=-1, keepdims=True)
    crossed = jnp.mean(gradient * normed, axis=-1, keepdims=True)
    return factor * (gradient - mean - normed * crossed)


def feed_forward_kernel(
    r_ref, x_ref, gate_own, gate_got, up_own, up_got, down_own, down_got,
    gate_out, up_out, act_keep, act_give, kept, sent, total, *, side_steps,
):
    step, last = pl.program_id(0), pl.num_programs(0) - 1
    half = x_ref.shape[1] // 2
    own = kept.shape[0]
    near, far = x_ref[:, :half], x_ref[:, half:]
    gate = dot(near, gate_own[...]) + dot(far, gate_got[...])
    up = dot(near, up_own[...]) + dot(far, up_got[...])
    gate_out[...] = gate
    up_out[...] = up
    act = (gate * jax.nn.sigmoid(gate) * up).astype(BF)
    mine = step // side_steps == r_ref[1]

    @pl.when(mine)
    def _():
        act_keep[...] = act

    @pl.when(jnp.logical_not(mine))
    def _():
        act_give[...] = act

    near, far = dot(act, down_own[...]), dot(act, down_got[...])

    @pl.when(step == 0)
    def _():
        total[:, :half] = near
        total[:, half:] = far

    @pl.when(step > 0)
    def _():
        total[:, :half] += near
        total[:, half:] += far

    @pl.when(step == last)
    def _():
        kept[...] = total[:own]
        sent[:, :half] = total[own:, half:].astype(BF)
        sent[:, half:] = total[own:, :half].astype(BF)


def feed_forward_back_kernel(
    r_ref, g_ref, gate_ref, up_ref, gate_own, gate_got, up_own, up_got, down_own, down_got,
    gate_keep, gate_give, up_keep, up_give, kept, sent, total, *, side_steps,
):
    step, last = pl.program_id(0), pl.num_programs(0) - 1
    half = g_ref.shape[1] // 2
    own = kept.shape[0]
    grad = contract_cols(g_ref[:, :half], down_own[...]) + contract_cols(
        g_ref[:, half:], down_got[...]
    )
    gate, up = gate_ref[...], up_ref[...]
    sigmoid = jax.nn.sigmoid(gate)
    gate_back = (grad * up * sigmoid * (1.0 + gate * (1.0 - sigmoid))).astype(BF)
    up_back = (grad * gate * sigmoid).astype(BF)
    mine = step // side_steps == r_ref[1]

    @pl.when(mine)
    def _():
        gate_keep[...] = gate_back
        up_keep[...] = up_back

    @pl.when(jnp.logical_not(mine))
    def _():
        gate_give[...] = gate_back
        up_give[...] = up_back

    near = contract_cols(gate_back, gate_own[...]) + contract_cols(up_back, up_own[...])
    far = contract_cols(gate_back, gate_got[...]) + contract_cols(up_back, up_got[...])

    @pl.when(step == 0)
    def _():
        total[:, :half] = near
        total[:, half:] = far

    @pl.when(step > 0)
    def _():
        total[:, :half] += near
        total[:, half:] += far

    @pl.when(step == last)
    def _():
        kept[...] = total[:own]
        sent[:, :half] = total[own:, half:].astype(BF)
        sent[:, half:] = total[own:, :half].astype(BF)


def feed_forward(back, where, operand, saved, weights, got, units, tile):
    span, width = operand.shape
    half, own, steps = width // 2, span // 2, units // tile
    side_steps = steps // 2
    gate, up, down = weights
    gate_got, up_got, down_got = got

    def mine(i, r):
        return (0, jnp.clip(i - r[1] * side_steps, 0, side_steps - 1))

    def other(i, r):
        return (0, jnp.clip(i - (1 - r[1]) * side_steps, 0, side_steps - 1))

    whole = pl.BlockSpec((span, width), lambda i, r: (0, 0))
    wide = pl.BlockSpec((span, tile), lambda i, r: (0, i))
    into_own = pl.BlockSpec((half, tile), lambda i, r: (0, r[0] * steps + i))
    into_got = pl.BlockSpec((half, tile), lambda i, r: (0, i))
    back_own = pl.BlockSpec((tile, half), lambda i, r: (r[0] * steps + i, 0))
    back_got = pl.BlockSpec((tile, half), lambda i, r: (i, 0))
    weight_specs = [into_own, into_got, into_own, into_got, back_own, back_got]
    keep, give = pl.BlockSpec((span, tile), mine), pl.BlockSpec((span, tile), other)
    ends = [pl.BlockSpec((own, width), lambda i, r: (0, 0))] * 2
    part = jax.ShapeDtypeStruct((span, units // 2), BF)
    full = jax.ShapeDtypeStruct((span, units), F32)
    end_shapes = [
        jax.ShapeDtypeStruct((own, width), F32),
        jax.ShapeDtypeStruct((own, width), BF),
    ]
    if back:
        kernel = feed_forward_back_kernel
        in_specs = [whole, wide, wide] + weight_specs
        out_specs = [keep, give, keep, give] + ends
        out_shape = [part] * 4 + end_shapes
    else:
        kernel = feed_forward_kernel
        in_specs = [whole] + weight_specs
        out_specs = [wide, wide, keep, give] + ends
        out_shape = [full] * 2 + [part] * 2 + end_shapes
    return pl.pallas_call(
        functools.partial(kernel, side_steps=side_steps),
        out_shape=out_shape,
        grid_spec=pltpu.PrefetchScalarGridSpec(
            num_scalar_prefetch=1,
            grid=(steps,),
            in_specs=in_specs,
            out_specs=out_specs,
            scratch_shapes=[pltpu.VMEM((span, width), F32)],
        ),
        compiler_params=pltpu.CompilerParams(vmem_limit_bytes=52 * 2**20),
        cost_estimate=pl.CostEstimate(
            flops=6 * span * width * units,
            bytes_accessed=6 * width * units + 12 * span * units,
            transcendentals=span * units,
        ),
        name="feed_forward_back" if back else "feed_forward",
    )(where, operand, *saved, gate, gate_got, up, up_got, down, down_got)


def widen(sums, shape, block, spot):
    rows, columns = block

    def kernel(in_ref, out_ref):
        out_ref[...] = in_ref[0].astype(F32)

    return pl.pallas_call(
        kernel,
        out_shape=jax.ShapeDtypeStruct(shape, F32),
        grid=(shape[1] // columns, shape[0] // rows),
        in_specs=[pl.BlockSpec((1, rows, columns), spot)],
        out_specs=pl.BlockSpec((rows, columns), lambda j, i: (i, j)),
        compiler_params=pltpu.CompilerParams(vmem_limit_bytes=32 * 2**20),
        cost_estimate=pl.CostEstimate(
            flops=0, bytes_accessed=6 * shape[0] * shape[1], transcendentals=0
        ),
        name="widen",
    )(sums)


def widen_four(sums, shape, starts, part):
    rows, columns = shape
    qk, v, o = (start // part for start in starts)

    def kernel(qk_a, qk_b, v_a, v_b, o_ref, q_out, k_out, v_out, o_out):
        step = pl.program_id(0)
        o_out[...] = o_ref[0].astype(F32)
        for core in range(2):
            for pair, out, at in ((0, q_out, 0), (1, k_out, 2)):
                for x, ref in enumerate((qk_a, qk_b)):
                    spot = (2 * core + x) * part
                    source = (at + core) * part
                    out[:, spot : spot + part] = ref[0, :, source : source + part].astype(F32)
        for high in range(2):

            @pl.when(step // 2 == high)
            def _():
                for core in range(2):
                    for x, ref in enumerate((v_a, v_b)):
                        spot = (2 * core + x) * part
                        source = (2 * high + core) * part
                        v_out[:, spot : spot + part] = ref[0, :, source : source + part].astype(F32)

    block = (1, part, columns)
    return pl.pallas_call(
        kernel,
        out_shape=[jax.ShapeDtypeStruct(shape, F32)] * 4,
        grid=(rows // part,),
        in_specs=[
            pl.BlockSpec(block, lambda i: (0, qk + i, 0)),
            pl.BlockSpec(block, lambda i: (1, qk + i, 0)),
            pl.BlockSpec(block, lambda i: (0, v + i % 2, 0)),
            pl.BlockSpec(block, lambda i: (1, v + i % 2, 0)),
            pl.BlockSpec(block, lambda i: (i % 2, o + i // 2, 0)),
        ],
        out_specs=[pl.BlockSpec((part, columns), lambda i: (i, 0))] * 4,
        compiler_params=pltpu.CompilerParams(vmem_limit_bytes=32 * 2**20),
        name="widen_four",
    )(sums, sums, sums, sums, sums)


def body(
    tokens,
    teacher,
    segments,
    valid_mask,
    query_weight,
    key_weight,
    value_weight,
    output_weight,
    gate_weight,
    up_weight,
    down_weight,
):
    rows = tokens.shape[0]
    cols = lax.axis_size("col")
    row = lax.axis_index("row")
    col = lax.axis_index("col")
    side = lax.axis_index("dp") % 2
    sides = [(i, i ^ 1) for i in range(lax.axis_size("dp"))]
    block = tokens.shape[1]
    half_width = block * cols
    wide = query_weight.shape[1] // 2
    units = gate_weight.shape[1] // 2
    part_units = units // 2
    part_wide = wide // 2
    tile = min(512, part_units)
    span = rows // 2
    own = span // 2
    first_row = row == 0
    where = jnp.stack([row, side]).astype(jnp.int32)
    tie = lax.optimization_barrier

    def swap(operand):
        return lax.ppermute(operand, "row", [(0, 1), (1, 0)])

    def cross(operand):
        return lax.ppermute(operand, "dp", sides)

    def gather_blocks(operand):
        if cols == 2:
            got = lax.ppermute(operand, "col", [(0, 1), (1, 0)])
            return ordered(col == 0, operand, got, 1)
        return lax.all_gather(operand, "col", axis=1, tiled=True)

    def from_chips(sent):
        if cols == 2:
            return lax.ppermute(sent.astype(BF), "col", [(0, 1), (1, 0)])
        sent = sent.astype(F32)
        return lax.psum(sent, "col") - sent

    def both_cores(kept):
        return jnp.concatenate([kept, swap(swap_halves(kept, 1))], axis=0)

    def from_cores(first, second):
        other = swap(swap_halves(jnp.concatenate([first, second], axis=0), 1))
        return [first, other[:own], second, other[own:]]

    def sum_cores(near, far):
        sent = jnp.concatenate([far[own:], near[own:]], axis=1).astype(BF)
        return jnp.concatenate([near[:own], far[:own]], axis=1) + swap(sent).astype(F32)

    def local_order(vector):
        pieces = []
        for j in range(2):
            piece = vector[j * span : (j + 1) * span]
            pieces.append(ordered(first_row, piece[:own], piece[own:], 0))
        return pieces

    blocks = []
    for j in range(2):
        piece = tokens[j * span : (j + 1) * span]
        blocks.append(gather_blocks(ordered(first_row, piece[:own], piece[own:], 0)))

    def columns_of(core):
        return jnp.concatenate(
            [take(w, core, wide, 1) for w in (query_weight, key_weight, value_weight)], axis=1
        )

    qkv_own, qkv_got = columns_of(row), swap(columns_of(1 - row))
    out_own = take(output_weight, row, wide, 0)
    out_got = swap(take(output_weight, 1 - row, wide, 0))
    weights = (gate_weight, up_weight, down_weight)

    validity = valid_mask.astype(F32)
    token_total = butterfly(jnp.sum(validity).reshape(1, 1), "dp")
    scale = (rows * lax.axis_size("dp")) / token_total
    segs = local_order(segments)
    places = local_order(jnp.arange(rows, dtype=jnp.int32))
    valids = [v[:own, None] for v in local_order(validity)]
    tables = [rope_tables(p) for p in places]
    spot_cols = [jnp.stack([g, p], axis=1) for g, p in zip(segs, places)]
    spot_rows = [
        jnp.stack([jnp.concatenate(segs[: j + 1]), jnp.concatenate(places[: j + 1])])
        for j in range(2)
    ]

    inputs, first_stats, low_first = [], [], []
    query_heads, key_heads, value_heads = [], [], []
    attended, logsums = [], []

    def first_norm(j, half):
        whole = jnp.concatenate([half, swap(swap_halves(half, 0))], axis=1)
        whole_f = whole.astype(F32)
        average, factor = moments(whole_f)
        inputs.append(whole[:own])
        first_stats.append((average[:own], factor[:own]))
        low_first.append(((whole_f - average) * factor).astype(BF))
        return low_first[j]

    def attention(j, operand):
        out = jax.ShapeDtypeStruct((span, wide), BF)
        q, k, v, heads, logsum, kept, sent = in_vmem(
            attention_kernel,
            "attention",
            [out] * 4
            + [
                jax.ShapeDtypeStruct((span, wide), F32),
                jax.ShapeDtypeStruct((own, 2 * half_width), F32),
                jax.ShapeDtypeStruct((own, 2 * half_width), BF),
            ],
            [operand, qkv_own, qkv_got, out_own, out_got, *tables[j], spot_cols[j], spot_rows[j]]
            + [x for pair in zip(key_heads, value_heads) for x in pair],
        )
        query_heads.append(q)
        key_heads.append(k)
        value_heads.append(v)
        attended.append(heads)
        logsums.append(logsum)
        return kept, sent

    hidden, second_stats, low_second = [], [], []

    def second_norm(j, part, got):
        hidden.append(inputs[j].astype(F32) + (part + got.astype(F32)))
        average, factor = moments(hidden[j])
        second_stats.append((average, factor))
        low_second.append(both_cores(((hidden[j] - average) * factor).astype(BF)))
        return low_second[j]

    saved, acts, act_gives = [], [], []

    def forward(operand, received):
        return feed_forward(False, where, operand, (), weights, received, units, tile)

    def after_forward(j, raw):
        gate_out, up_out, act_keep, act_give, kept, sent = raw
        saved.append((gate_out, up_out))
        acts.append(act_keep)
        act_gives.append(act_give)
        piece = teacher[j * span : (j + 1) * span]
        piece = ordered(first_row, piece[:own], piece[own:], 0)
        near, far = piece[:own].astype(F32), swap(piece[own:]).astype(F32)
        minus = [jnp.where(col == b, near, 0.0) for b in range(cols)]
        minus += [jnp.where(col == b, far, 0.0) for b in range(cols)]
        part = kept + swap(sent).astype(F32) - jnp.concatenate(minus, axis=1)
        return part, (near, far)

    outputs, errors, grad_results, low_results = [], [], [], []

    def loss_of(j, part, got, targets):
        near, far = targets
        error = hidden[j] + (part + got.astype(F32))
        near_error = take(error[:, :half_width], col, block, 1)
        far_error = take(error[:, half_width:], col, block, 1)
        outputs.append(
            ordered(
                first_row,
                (near_error + near).astype(BF),
                swap((far_error + far).astype(BF)),
                0,
            )
        )
        errors.append(
            0.5 * jnp.sum(valids[j] * (near_error * near_error + far_error * far_error))
        )
        grad_results.append(scale * valids[j] * error)
        low_results.append(both_cores(grad_results[j].astype(BF)))
        return low_results[j]

    def backward(j, operand, received):
        return feed_forward(True, where, operand, saved[j], weights, received, units, tile)

    grad_hiddens, low_hiddens = [], []

    def second_norm_back(j, part, got):
        gradient = part + got.astype(F32)
        average, factor = second_stats[j]
        normed = (hidden[j] - average) * factor
        grad_hiddens.append(grad_results[j] + normalize_back(gradient, normed, factor))
        low_hiddens.append(both_cores(grad_hiddens[j].astype(BF)))
        return low_hiddens[j]

    def attention_back(j, operand, extra):
        first = jax.ShapeDtypeStruct((span, wide), F32)
        shapes = [jax.ShapeDtypeStruct((span, wide), BF), first, first]
        if j == 1:
            shapes = [jax.ShapeDtypeStruct((span, n * wide), BF) for n in (2, 3)]
        return in_vmem(
            attention_back_kernel,
            "attention_back",
            shapes,
            [
                operand,
                out_own,
                out_got,
                *tables[j],
                spot_cols[j],
                spot_rows[j],
                logsums[j],
                query_heads[j],
                key_heads[j],
                value_heads[j],
                *extra,
            ],
        )

    def joined(pair):
        return pair[0] + swap(pair[1]).astype(F32)

    part_a = joined(attention(0, first_norm(0, blocks[0])))
    operand = first_norm(1, blocks[1])
    operand, part_a, low, mine, scale = tie(
        (operand, part_a, part_a.astype(BF), low_first[0][:own], scale)
    )
    got_a, first_a = from_chips(low), cross(mine)
    pair = attention(1, operand)
    pair, got_a, first_a = tie((pair, got_a, first_a))
    received = (
        swap(take(gate_weight, 1 - row, units, 1)),
        swap(take(up_weight, 1 - row, units, 1)),
        swap(take(down_weight, 1 - row, units, 0)),
    )
    part_b = joined(pair)
    two_a = second_norm(0, part_a, got_a)
    two_a, part_b, low, mine, received = tie(
        (two_a, part_b, part_b.astype(BF), low_first[1][:own], received)
    )
    got_b, first_b = from_chips(low), cross(mine)
    raw = forward(two_a, received)
    raw, got_b, first_b = tie((raw, got_b, first_b))
    part_a, targets_a = after_forward(0, raw)
    two_b = second_norm(1, part_b, got_b)
    two_b, part_a, low, mine = tie((two_b, part_a, part_a.astype(BF), two_a[:own]))
    got_a, cross_two_a = from_chips(low), cross(mine)
    raw = forward(two_b, received)
    raw, got_a, cross_two_a = tie((raw, got_a, cross_two_a))
    part_b, targets_b = after_forward(1, raw)
    low_a = loss_of(0, part_a, got_a, targets_a)
    low_a, part_b, low, mine = tie((low_a, part_b, part_b.astype(BF), two_b[:own]))
    got_b, cross_two_b = from_chips(low), cross(mine)
    raw = backward(0, low_a, received)
    raw, got_b, cross_two_b = tie((raw, got_b, cross_two_b))
    ups_a, part_a = raw[:4], joined(raw[4:])
    low_b = loss_of(1, part_b, got_b, targets_b)
    low_b, part_a, low, mine = tie((low_b, part_a, part_a.astype(BF), act_gives[0]))
    got_a, cross_act_a = from_chips(low), cross(mine)
    raw = backward(1, low_b, received)
    raw, got_a, cross_act_a = tie((raw, got_a, cross_act_a))
    ups_b, part_b = raw[:4], joined(raw[4:])
    hidden_a = second_norm_back(0, part_a, got_a)
    hidden_a, part_b, low, mine = tie((hidden_a, part_b, part_b.astype(BF), low_a[:own]))
    got_b, cross_low_a = from_chips(low), cross(mine)
    parts = attention_back(0, hidden_a, [])
    parts, got_b, cross_low_a = tie((parts, got_b, cross_low_a))
    hidden_b = second_norm_back(1, part_b, got_b)
    hidden_b, parts, mine = tie((hidden_b, parts, low_b[:own]))
    cross_low_b = cross(mine)
    first_back, back_b = attention_back(
        1, hidden_b, [key_heads[0], value_heads[0], *tables[0], *parts[1:]]
    )
    first_back, back_b, cross_low_b = tie((first_back, back_b, cross_low_b))
    backs = [jnp.concatenate([parts[0], first_back], axis=1), back_b]
    gate_gives = [u[1] for u in (ups_a, ups_b)]
    up_gives = [u[3] for u in (ups_a, ups_b)]

    def half_columns(operand, which):
        return jnp.concatenate(
            [take(operand[:, i * wide : (i + 1) * wide], which, part_wide, 1) for i in range(3)],
            axis=1,
        )

    def split_rows(full):
        half = full.shape[0] // 2
        return full[:half], swap(full[half:])

    def split_cols(full):
        half = full.shape[1] // 2
        return full[:, :half], swap(full[:, half:])

    def together(lefts, rights):
        return jnp.concatenate(lefts, axis=0), jnp.concatenate(rights, axis=0)

    def product(lefts, rights):
        return contract_rows(lefts, rights).astype(BF)

    back_gives = [half_columns(g, 1 - side) for g in backs]
    hiddens = together(attended, [hidden_a, hidden_b])
    error_sum = (errors[0] + errors[1]).reshape(1, 1)
    hiddens, act_give, backs, back_gives = tie((hiddens, act_gives[1], backs, back_gives))
    cross_act_b = cross(act_give)
    last_parts = [
        sum_cores(contract_cols(g, qkv_own), contract_cols(g, qkv_got)) for g in backs
    ]
    grad_out = product(*hiddens)
    last_parts, grad_out, cross_act_b, error_sum = tie(
        (last_parts, grad_out, cross_act_b, error_sum)
    )
    downs = together(
        [*acts, cross_act_a, cross_act_b], [low_a, low_b, *from_cores(cross_low_a, cross_low_b)]
    )
    downs, gate_gives = tie((downs, gate_gives))
    cross_gates = [cross(g) for g in gate_gives]
    grad_down = product(*downs)
    error_sum = butterfly(error_sum, "row")
    cross_gates, grad_down, error_sum = tie((cross_gates, grad_down, error_sum))
    down_pair = split_cols(grad_down)
    twos = [two_a, two_b, *from_cores(cross_two_a, cross_two_b)]
    gates = together(twos, [ups_a[0], ups_b[0], *cross_gates])
    out_give = take(grad_out, 1 - side, part_wide, 0)
    gates, up_gives = tie((gates, up_gives))
    cross_ups = [cross(g) for g in up_gives]
    grad_gate = product(*gates)
    error_sum = butterfly(error_sum, "col")
    grad_gate, cross_ups, error_sum = tie((grad_gate, cross_ups, error_sum))
    gate_pair = split_rows(grad_gate)
    ups = together(twos, [ups_a[2], ups_b[2], *cross_ups])
    ups, out_give, back_gives = tie((ups, out_give, back_gives))
    grad_out_got = cross(out_give)
    cross_backs = [cross(g) for g in back_gives]
    grad_up = product(*ups)
    error_sum = butterfly(error_sum, "dp")
    grad_up, grad_out_got, cross_backs, error_sum = tie(
        (grad_up, grad_out_got, cross_backs, error_sum)
    )
    up_pair = split_rows(grad_up)
    out_pair = split_cols(add_low(take(grad_out, side, part_wide, 0), grad_out_got))
    qkv_pair = split_rows(
        product(
            *together(
                [*low_first, *from_cores(first_a, first_b)],
                [*[half_columns(g, side) for g in backs], *cross_backs],
            )
        )
    )
    three = [
        ordered(
            first_row,
            qkv_pair[0][:, i * part_wide : (i + 1) * part_wide],
            qkv_pair[1][:, i * part_wide : (i + 1) * part_wide],
            1,
        )
        for i in range(3)
    ]
    pieces, spots, starts = [], [], []
    total = 0
    for pair in (down_pair, gate_pair, up_pair, out_pair):
        packed = [pack(p, half_width) for p in pair]
        size = packed[0].shape[0]
        pieces += packed
        spots += [
            lambda r, total=total, size=size: total + r * size,
            lambda r, total=total, size=size: total + (1 - r) * size,
        ]
        starts.append((total, size))
        total += 2 * size
    for item in (jnp.concatenate(three[:2], axis=1), three[2]):
        packed = pack(item, half_width)
        size = packed.shape[0]
        pieces.append(packed)
        spots.append(lambda r, total=total: total + 0 * r)
        starts.append((total, size))
        total += size
    last_gots = [from_chips(p) for p in last_parts]
    sums = line_sum(pieces, spots, chunk=min(256, total // 8))
    sums, last_parts, last_gots = tie((sums, last_parts, last_gots))

    if cols == 2:
        tall = min(1024, starts[0][1])

        def rows_of(start, size, step):
            def spot(j, i):
                s, rest = i // (2 * step), i % (2 * step)
                return (rest // step, (start + s * size) // tall + rest % step, 0)

            return spot

        def columns_at(start):
            return lambda j, i: (j % 2, (start + (j // 2) * half_width) // tall + i, 0)

        grad_down = widen(
            sums,
            down_weight.shape,
            (tall, half_width),
            rows_of(*starts[0], part_units // tall),
        )
        grad_gate, grad_up = (
            widen(sums, gate_weight.shape, (tall, part_units), columns_at(starts[n][0]))
            for n in (1, 2)
        )
        grad_query, grad_key, grad_value, grad_output = widen_four(
            sums, query_weight.shape, [starts[n][0] for n in (4, 5, 3)], part_wide
        )
    else:

        def blocks_of(which, columns):
            start, size = starts[which]
            return [
                unpack(sums[x, start + s * size : start + (s + 1) * size], columns)
                for s in range(2)
                for x in range(2)
            ]

        grad_down = jnp.concatenate(blocks_of(0, half_width), axis=0).astype(F32)
        grad_gate = jnp.concatenate(blocks_of(1, part_units), axis=1).astype(F32)
        grad_up = jnp.concatenate(blocks_of(2, part_units), axis=1).astype(F32)
        grad_output = jnp.concatenate(blocks_of(3, half_width), axis=0).astype(F32)
        three = [[], [], []]
        qk, v = (
            [unpack(sums[x, starts[n][0] : starts[n][0] + starts[n][1]], k * part_wide) for x in range(2)]
            for n, k in ((4, 4), (5, 2))
        )
        for s in range(2):
            for x in range(2):
                at = s * part_wide
                three[0].append(qk[x][:, at : at + part_wide])
                three[1].append(qk[x][:, 2 * part_wide + at : 2 * part_wide + at + part_wide])
                three[2].append(v[x][:, at : at + part_wide])
        grad_query, grad_key, grad_value = (
            jnp.concatenate(t, axis=1).astype(F32) for t in three
        )

    grad_tokens = []
    for j in range(2):
        gradient = last_parts[j] + last_gots[j].astype(F32)
        average, factor = first_stats[j]
        normed = (inputs[j].astype(F32) - average) * factor
        grads = grad_hiddens[j] + normalize_back(gradient, normed, factor)
        near = take(grads[:, :half_width], col, block, 1)
        far = take(grads[:, half_width:], col, block, 1)
        grad_tokens.append(ordered(first_row, near, swap(far), 0))
    loss_value = (error_sum / token_total)[0, 0]
    return (
        jnp.concatenate(outputs, axis=0),
        loss_value,
        jnp.concatenate(grad_tokens, axis=0),
        grad_query,
        grad_key,
        grad_value,
        grad_output,
        grad_gate,
        grad_up,
        grad_down,
    )


def solution(mesh):
    features = P("dp", ("row", "col"))
    into, back = P("row", "col"), P("col", "row")
    in_specs = (features, features, P("dp"), P("dp"), into, into, into, back, into, into, back)
    out_specs = (features, P(), features, into, into, into, back, into, into, back)
    return jax.shard_map(body, mesh=mesh, in_specs=in_specs, out_specs=out_specs, check_vma=False)
```

```python
import functools
import math

import jax
import jax.numpy as jnp
from jax import lax
from jax.experimental import pallas as pl
from jax.experimental.pallas import tpu as pltpu
from jax.sharding import PartitionSpec as P

D = 2048
HEAD = 128
LEN = 1024
EPS = 1e-05
THETA = 10000.0
NEG = -1e30

BF = jnp.bfloat16
F32 = jnp.float32


def rope_tables(places):
    half_width = HEAD // 2
    frequency = jnp.exp(
        jnp.arange(half_width).astype(F32) * (-2.0 * math.log(THETA) / HEAD)
    )
    angles = places.astype(F32)[:, None] * frequency[None, :]
    cosine, sine_table = jnp.cos(angles), jnp.sin(angles)
    return (
        jnp.concatenate([cosine, cosine], axis=1),
        jnp.concatenate([-sine_table, sine_table], axis=1),
    )


def dot(left, right):
    return jnp.dot(left, right, preferred_element_type=F32)


def contract_rows(left, right):
    return lax.dot_general(left, right, (((0,), (0,)), ((), ())), preferred_element_type=F32)


def contract_cols(left, right):
    return lax.dot_general(left, right, (((1,), (1,)), ((), ())), preferred_element_type=F32)


def take(operand, index, size, axis):
    return lax.dynamic_slice_in_dim(operand, index * size, size, axis)


def swap_halves(operand, axis):
    half = operand.shape[axis] // 2
    return jnp.concatenate(
        [
            lax.slice_in_dim(operand, half, 2 * half, axis=axis),
            lax.slice_in_dim(operand, 0, half, axis=axis),
        ],
        axis=axis,
    )


def ordered(first, mine, other, axis):
    return jnp.concatenate(
        [jnp.where(first, mine, other), jnp.where(first, other, mine)], axis=axis
    )


def add_low(left, right):
    return (left.astype(F32) + right.astype(F32)).astype(BF)


MESH = pl.DeviceIdType.MESH


def line_kernel(sizes, spots, given, chunk, lag, ahead, deep, *refs):
    count = len(sizes)
    pieces, gives = refs[:count], refs[count : count + given]
    out = refs[count + given]
    held, got_in, got_mid, got_give, load, send_in, send_mid, send_out, send_side, in_sem, mid_sem, out_sem, side_sem, keep, send_give, give_sem = refs[count + given + 1:]
    places = lax.axis_size("dp") // 2
    dp = lax.axis_index("dp")
    row = lax.axis_index("row")
    col = lax.axis_index("col")
    place, side = dp // 2, dp % 2
    half = places // 2
    low = place < half
    depth = jnp.where(low, place, places - 1 - place)
    is_mid = depth == half - 1
    is_end = depth == 0
    to_in = jnp.where(low, place + 1, place - 1)
    to_out = jnp.where(low, place - 1, place + 1)
    inner = (to_in * 2 + side, row, col)
    outer = (jnp.clip(to_out, 0, places - 1) * 2 + side, row, col)
    other = (dp + 1 - 2 * side, row, col)
    total_rows = held.shape[0]
    steps = total_rows // chunk
    base = total_rows - sum(sizes[count - given :])
    first = base // chunk

    loads = []
    for i in range(count):
        rows = sizes[i]
        at = pl.multiple_of(spots[i](row), 16)
        loads.append(pltpu.make_async_copy(pieces[i], held.at[pl.ds(at, rows)], load.at[i]))
        loads[-1].start()

    barrier = pltpu.get_barrier_semaphore()
    pl.semaphore_signal(barrier, inc=1, device_id=inner, device_id_type=MESH)
    pl.semaphore_signal(barrier, inc=1, device_id=other, device_id_type=MESH)

    @pl.when(jnp.logical_not(is_end))
    def _():
        pl.semaphore_signal(barrier, inc=1, device_id=outer, device_id_type=MESH)
        pl.semaphore_wait(barrier, 3)

    @pl.when(is_end)
    def _():
        pl.semaphore_wait(barrier, 2)

    given_copies = []
    for i in range(given):
        spot = pl.multiple_of(spots[count - given + i](row) - base, 16)
        given_copies.append(
            pltpu.make_async_remote_copy(
                src_ref=gives[i], dst_ref=got_give.at[pl.ds(spot, sizes[count - given + i])],
                send_sem=send_give.at[i], recv_sem=give_sem.at[i],
                device_id=other, device_id_type=MESH))
        given_copies[-1].start()
    for copy in loads:
        copy.wait()

    def add_given(t):
        @pl.when(t == first)
        def _():
            for copy in given_copies:
                copy.wait()

        @pl.when(t >= first)
        def _():
            held[at(t)] = (
                held[at(t)].astype(F32) + got_give[at(t - first)].astype(F32)
            ).astype(BF)

    def at(t):
        return pl.ds(pl.multiple_of(t * chunk, chunk), chunk)

    def inward(t):
        return pltpu.make_async_remote_copy(
            src_ref=held.at[at(t)], dst_ref=got_in.at[at(t)], send_sem=send_in.at[t],
            recv_sem=in_sem.at[t], device_id=inner, device_id_type=MESH)

    def middle(t):
        return pltpu.make_async_remote_copy(
            src_ref=held.at[at(t)], dst_ref=got_mid.at[at(t)], send_sem=send_mid.at[t],
            recv_sem=mid_sem.at[t], device_id=inner, device_id_type=MESH)

    def outward(t, source):
        return pltpu.make_async_remote_copy(
            src_ref=source, dst_ref=out.at[side, at(t)], send_sem=send_out.at[t],
            recv_sem=out_sem.at[t], device_id=outer, device_id_type=MESH)

    def across(t, source):
        return pltpu.make_async_remote_copy(
            src_ref=source, dst_ref=out.at[side, at(t)], send_sem=send_side.at[t],
            recv_sem=side_sem.at[t], device_id=other, device_id_type=MESH)

    def store(t):
        return pltpu.make_async_copy(got_in.at[at(t)], out.at[side, at(t)], keep.at[t])

    def mid_loop(t, _):
        @pl.when(t < steps)
        def _():
            add_given(t)

            @pl.when(jnp.logical_not(is_end))
            def _():
                inward(t).wait_recv()
                held[at(t)] = (held[at(t)].astype(F32) + got_in[at(t)].astype(F32)).astype(BF)
            @pl.when(t >= deep)
            def _():
                middle(t - deep).wait_send()
            middle(t).start()

        @pl.when(t >= ahead)
        def _():
            u = t - ahead
            middle(u).wait_recv()
            got_in[at(u)] = (held[at(u)].astype(F32) + got_mid[at(u)].astype(F32)).astype(BF)
            store(u).start()
            @pl.when(u >= deep)
            def _():
                @pl.when(jnp.logical_not(is_end))
                def _():
                    outward(u - deep, got_in.at[at(u)]).wait_send()
                across(u - deep, got_in.at[at(u)]).wait_send()
            @pl.when(jnp.logical_not(is_end))
            def _():
                outward(u, got_in.at[at(u)]).start()
            across(u, got_in.at[at(u)]).start()
        return 0

    def far_loop(t, _):
        @pl.when(t < steps)
        def _():
            add_given(t)

            @pl.when(jnp.logical_not(is_end))
            def _():
                inward(t).wait_recv()
                held[at(t)] = (held[at(t)].astype(F32) + got_in[at(t)].astype(F32)).astype(BF)
            @pl.when(t >= deep)
            def _():
                inward(t - deep).wait_send()
            inward(t).start()

        @pl.when(t >= lag)
        def _():
            u = t - lag
            outward(u, out.at[side, at(u)]).wait_recv()
            @pl.when(u >= deep)
            def _():
                @pl.when(jnp.logical_not(is_end))
                def _():
                    outward(u - deep, out.at[side, at(u)]).wait_send()
                across(u - deep, out.at[side, at(u)]).wait_send()
            @pl.when(jnp.logical_not(is_end))
            def _():
                outward(u, out.at[side, at(u)]).start()
            across(u, out.at[side, at(u)]).start()
        return 0

    @pl.when(is_mid)
    def _():
        lax.fori_loop(0, steps + ahead, mid_loop, 0)
        def finish(t, _):
            store(t).wait()
            across(t, got_in.at[at(t)]).wait_recv()
            @pl.when(t >= steps - deep)
            def _():
                middle(t).wait_send()
                across(t, got_in.at[at(t)]).wait_send()
                @pl.when(jnp.logical_not(is_end))
                def _():
                    outward(t, got_in.at[at(t)]).wait_send()
            return 0
        lax.fori_loop(0, steps, finish, 0)

    @pl.when(jnp.logical_not(is_mid))
    def _():
        lax.fori_loop(0, steps + lag, far_loop, 0)
        def finish(t, _):
            across(t, out.at[side, at(t)]).wait_recv()
            @pl.when(t >= steps - deep)
            def _():
                inward(t).wait_send()
                across(t, out.at[side, at(t)]).wait_send()
                @pl.when(jnp.logical_not(is_end))
                def _():
                    outward(t, out.at[side, at(t)]).wait_send()
            return 0
        lax.fori_loop(0, steps, finish, 0)


def line_sum(pieces, spots, gives, chunk, lag=8, ahead=2, deep=2):
    sizes = [p.shape[0] for p in pieces]
    rows, width = sum(sizes), pieces[0].shape[1]
    steps = rows // chunk
    given_rows = sum(g.shape[0] for g in gives)
    dma = pltpu.SemaphoreType.DMA
    return pl.pallas_call(
        functools.partial(line_kernel, sizes, spots, len(gives), chunk, lag, ahead, deep),
        out_shape=jax.ShapeDtypeStruct((2, rows, width), BF),
        in_specs=[pl.BlockSpec(memory_space=pl.ANY)] * (len(pieces) + len(gives)),
        out_specs=pl.BlockSpec(memory_space=pl.ANY),
        scratch_shapes=[pltpu.VMEM((rows, width), BF)] * 3
        + [pltpu.VMEM((given_rows, width), BF)]
        + [dma((len(pieces),))]
        + [dma((steps,))] * 9
        + [dma((len(gives),))] * 2,
        compiler_params=pltpu.CompilerParams(
            collective_id=0, has_side_effects=True, vmem_limit_bytes=58 * 2**20
        ),
        name="line_sum",
    )(*pieces, *gives)


def pack(operand, width):
    rows, columns = operand.shape
    if columns == width:
        return operand
    if columns > width:
        return jnp.concatenate(
            [operand[:, i : i + width] for i in range(0, columns, width)], axis=0
        )
    times = width // columns
    step = rows // times
    return jnp.concatenate([operand[i * step : (i + 1) * step] for i in range(times)], axis=1)


def unpack(operand, columns):
    rows, width = operand.shape
    if columns == width:
        return operand
    if columns > width:
        step = rows * width // columns
        return jnp.concatenate(
            [operand[i * step : (i + 1) * step] for i in range(columns // width)], axis=1
        )
    return jnp.concatenate(
        [operand[:, i : i + columns] for i in range(0, width, columns)], axis=0
    )


def hop(operand, axis, step):
    size = lax.axis_size(axis)
    return operand + lax.ppermute(operand, axis, [(i, i ^ step) for i in range(size)])


def turned(operand, cosine, sine_table):
    return operand * cosine + pltpu.roll(operand, HEAD // 2, 1) * sine_table


def allowed_pairs(spot_col, spot_row):
    return (spot_col[:, 0:1] == spot_row[0:1, :]) & (spot_row[1:2, :] <= spot_col[:, 1:2])


def attention_kernel(
    x_ref, own_ref, got_ref, out_own, out_got, cos_ref, sin_ref, col_ref, row_ref, *refs
):
    earlier, (q_out, k_out, v_out, att_out, lse_out, kept, sent) = refs[:-7], refs[-7:]
    half = x_ref.shape[1] // 2
    wide = out_own.shape[0]
    own = kept.shape[0]
    near, far = x_ref[:, :half], x_ref[:, half:]
    cosine, sine_table = cos_ref[...], sin_ref[...]
    for which, out in enumerate((q_out, k_out, v_out)):
        at = slice(which * wide, (which + 1) * wide)
        raw = dot(near, own_ref[:, at]) + dot(far, got_ref[:, at])
        for h in range(wide // HEAD):
            head = slice(h * HEAD, (h + 1) * HEAD)
            value = raw[:, head]
            if which < 2:
                value = turned(value, cosine, sine_table)
            out[:, head] = value.astype(BF)
    allowed = allowed_pairs(col_ref[...], row_ref[...])
    for h in range(wide // HEAD):
        head = slice(h * HEAD, (h + 1) * HEAD)
        keys, values = k_out[:, head], v_out[:, head]
        if earlier:
            keys = jnp.concatenate([earlier[0][:, head], keys], axis=0)
            values = jnp.concatenate([earlier[1][:, head], values], axis=0)
        scores = contract_cols(q_out[:, head], keys) * (1.0 / math.sqrt(HEAD))
        scores = jnp.where(allowed, scores, NEG)
        row_max = jnp.max(scores, axis=-1, keepdims=True)
        shares = jnp.exp(scores - row_max)
        totals = jnp.sum(shares, axis=-1, keepdims=True)
        shares = (shares / totals).astype(BF)
        att_out[:, head] = dot(shares, values).astype(BF)
        lse_out[:, head] = jnp.broadcast_to(row_max + jnp.log(totals), (2 * own, HEAD))
    near, far = dot(att_out[...], out_own[...]), dot(att_out[...], out_got[...])
    kept[:, :half] = near[:own]
    kept[:, half:] = far[:own]
    sent[:, :half] = far[own:].astype(BF)
    sent[:, half:] = near[own:].astype(BF)


def attention_back_kernel(
    g_ref, out_own, out_got, cos_ref, sin_ref, col_ref, row_ref, lse_ref, q_ref, k_ref, v_ref, *refs
):
    span, wide = q_ref.shape
    half = g_ref.shape[1] // 2
    factor = 1.0 / math.sqrt(HEAD)
    cosine, sine_table = cos_ref[...], -sin_ref[...]
    grads = contract_cols(g_ref[:, :half], out_own[...])
    grads = (grads + contract_cols(g_ref[:, half:], out_got[...])).astype(BF)
    allowed = allowed_pairs(col_ref[...], row_ref[...])
    last = len(refs) > 3
    for h in range(wide // HEAD):
        head = slice(h * HEAD, (h + 1) * HEAD)
        queries, gradient = q_ref[:, head], grads[:, head]
        keys, values = k_ref[:, head], v_ref[:, head]
        if last:
            keys = jnp.concatenate([refs[0][:, head], keys], axis=0)
            values = jnp.concatenate([refs[1][:, head], values], axis=0)
        scores = jnp.where(allowed, contract_cols(queries, keys) * factor, NEG)
        shares = jnp.exp(scores - lse_ref[:, h * HEAD : h * HEAD + 1])
        grad_shares = contract_cols(gradient, values)
        centre = jnp.sum(shares * grad_shares, axis=-1, keepdims=True)
        grad_scores = (shares * (grad_shares - centre)).astype(BF)
        grad_q = turned(dot(grad_scores, keys) * factor, cosine, sine_table)
        grad_k = contract_rows(grad_scores, queries) * factor
        grad_v = contract_rows(shares.astype(BF), gradient)
        if not last:
            q_out, k_out, v_out = refs
            q_out[:, head] = grad_q.astype(BF)
            k_out[:, head] = grad_k
            v_out[:, head] = grad_v
        else:
            cos_first, sin_first, k_part, v_part, first_out, back_out = refs[2:]
            back_out[:, head] = grad_q.astype(BF)
            at = slice(wide + h * HEAD, wide + (h + 1) * HEAD)
            back_out[:, at] = turned(grad_k[span:], cosine, sine_table).astype(BF)
            first = grad_k[:span] + k_part[:, head]
            first_out[:, head] = turned(first, cos_first[...], -sin_first[...]).astype(BF)
            at = slice(2 * wide + h * HEAD, 2 * wide + (h + 1) * HEAD)
            back_out[:, at] = grad_v[span:].astype(BF)
            at = slice(wide + h * HEAD, wide + (h + 1) * HEAD)
            first_out[:, at] = (grad_v[:span] + v_part[:, head]).astype(BF)


def last_kernel(a_ref, b_ref, own_ref, got_ref, kept_a, sent_a, kept_b, sent_b):
    half = own_ref.shape[0]
    own = kept_a.shape[0]
    for ref, kept, sent in ((a_ref, kept_a, sent_a), (b_ref, kept_b, sent_b)):
        near, far = contract_cols(ref[...], own_ref[...]), contract_cols(ref[...], got_ref[...])
        kept[:, :half] = near[:own]
        kept[:, half:] = far[:own]
        sent[:, :half] = far[own:].astype(BF)
        sent[:, half:] = near[own:].astype(BF)


def in_vmem(kernel, name, out_shape, operands):
    return pl.pallas_call(
        kernel,
        out_shape=out_shape,
        in_specs=[pl.BlockSpec(memory_space=pltpu.VMEM)] * len(operands),
        out_specs=[pl.BlockSpec(memory_space=pltpu.VMEM)] * len(out_shape),
        compiler_params=pltpu.CompilerParams(vmem_limit_bytes=52 * 2**20),
        cost_estimate=pl.CostEstimate(
            flops=8 * 10**9, bytes_accessed=2 * 10**7, transcendentals=2 * 10**6
        ),
        name=name,
    )(*operands)


def moments(operand):
    average = jnp.mean(operand, axis=-1, keepdims=True)
    centre = operand - average
    factor = lax.rsqrt(jnp.mean(centre * centre, axis=-1, keepdims=True) + EPS)
    return average, factor


def normalize_back(gradient, normed, factor):
    mean = jnp.mean(gradient, axis=-1, keepdims=True)
    crossed = jnp.mean(gradient * normed, axis=-1, keepdims=True)
    return factor * (gradient - mean - normed * crossed)


def feed_forward_kernel(
    r_ref, x_ref, gate_own, gate_got, up_own, up_got, down_own, down_got,
    gate_out, up_out, act_keep, act_give, kept, sent, total, *, side_steps,
):
    step, last = pl.program_id(0), pl.num_programs(0) - 1
    half = x_ref.shape[1] // 2
    own = kept.shape[0]
    near, far = x_ref[:, :half], x_ref[:, half:]
    gate = dot(near, gate_own[...]) + dot(far, gate_got[...])
    up = dot(near, up_own[...]) + dot(far, up_got[...])
    gate_out[...] = gate
    up_out[...] = up
    act = (gate * jax.nn.sigmoid(gate) * up).astype(BF)
    mine = step // side_steps == r_ref[1]

    @pl.when(mine)
    def _():
        act_keep[...] = act

    @pl.when(jnp.logical_not(mine))
    def _():
        act_give[...] = act

    near, far = dot(act, down_own[...]), dot(act, down_got[...])

    @pl.when(step == 0)
    def _():
        total[:, :half] = near
        total[:, half:] = far

    @pl.when(step > 0)
    def _():
        total[:, :half] += near
        total[:, half:] += far

    @pl.when(step == last)
    def _():
        kept[...] = total[:own]
        sent[:, :half] = total[own:, half:].astype(BF)
        sent[:, half:] = total[own:, :half].astype(BF)


def feed_forward_back_kernel(
    r_ref, g_ref, gate_ref, up_ref, gate_own, gate_got, up_own, up_got, down_own, down_got,
    gate_keep, gate_give, up_keep, up_give, kept, sent, total, *, side_steps,
):
    step, last = pl.program_id(0), pl.num_programs(0) - 1
    half = g_ref.shape[1] // 2
    own = kept.shape[0]
    grad = contract_cols(g_ref[:, :half], down_own[...]) + contract_cols(
        g_ref[:, half:], down_got[...]
    )
    gate, up = gate_ref[...], up_ref[...]
    sigmoid = jax.nn.sigmoid(gate)
    gate_back = (grad * up * sigmoid * (1.0 + gate * (1.0 - sigmoid))).astype(BF)
    up_back = (grad * gate * sigmoid).astype(BF)
    mine = step // side_steps == r_ref[1]

    @pl.when(mine)
    def _():
        gate_keep[...] = gate_back
        up_keep[...] = up_back

    @pl.when(jnp.logical_not(mine))
    def _():
        gate_give[...] = gate_back
        up_give[...] = up_back

    near = contract_cols(gate_back, gate_own[...]) + contract_cols(up_back, up_own[...])
    far = contract_cols(gate_back, gate_got[...]) + contract_cols(up_back, up_got[...])

    @pl.when(step == 0)
    def _():
        total[:, :half] = near
        total[:, half:] = far

    @pl.when(step > 0)
    def _():
        total[:, :half] += near
        total[:, half:] += far

    @pl.when(step == last)
    def _():
        kept[...] = total[:own]
        sent[:, :half] = total[own:, half:].astype(BF)
        sent[:, half:] = total[own:, :half].astype(BF)


def feed_forward(back, where, operand, saved, weights, got, units, tile):
    span, width = operand.shape
    half, own, steps = width // 2, span // 2, units // tile
    side_steps = steps // 2
    gate, up, down = weights
    gate_got, up_got, down_got = got

    def mine(i, r):
        return (0, jnp.clip(i - r[1] * side_steps, 0, side_steps - 1))

    def other(i, r):
        return (0, jnp.clip(i - (1 - r[1]) * side_steps, 0, side_steps - 1))

    whole = pl.BlockSpec((span, width), lambda i, r: (0, 0))
    wide = pl.BlockSpec((span, tile), lambda i, r: (0, i))
    into_own = pl.BlockSpec((half, tile), lambda i, r: (0, r[0] * steps + i))
    into_got = pl.BlockSpec((half, tile), lambda i, r: (0, i))
    back_own = pl.BlockSpec((tile, half), lambda i, r: (r[0] * steps + i, 0))
    back_got = pl.BlockSpec((tile, half), lambda i, r: (i, 0))
    weight_specs = [into_own, into_got, into_own, into_got, back_own, back_got]
    keep, give = pl.BlockSpec((span, tile), mine), pl.BlockSpec((span, tile), other)
    ends = [pl.BlockSpec((own, width), lambda i, r: (0, 0))] * 2
    part = jax.ShapeDtypeStruct((span, units // 2), BF)
    full = jax.ShapeDtypeStruct((span, units), F32)
    end_shapes = [
        jax.ShapeDtypeStruct((own, width), F32),
        jax.ShapeDtypeStruct((own, width), BF),
    ]
    if back:
        kernel = feed_forward_back_kernel
        in_specs = [whole, wide, wide] + weight_specs
        out_specs = [keep, give, keep, give] + ends
        out_shape = [part] * 4 + end_shapes
    else:
        kernel = feed_forward_kernel
        in_specs = [whole] + weight_specs
        out_specs = [wide, wide, keep, give] + ends
        out_shape = [full] * 2 + [part] * 2 + end_shapes
    return pl.pallas_call(
        functools.partial(kernel, side_steps=side_steps),
        out_shape=out_shape,
        grid_spec=pltpu.PrefetchScalarGridSpec(
            num_scalar_prefetch=1,
            grid=(steps,),
            in_specs=in_specs,
            out_specs=out_specs,
            scratch_shapes=[pltpu.VMEM((span, width), F32)],
        ),
        compiler_params=pltpu.CompilerParams(vmem_limit_bytes=52 * 2**20),
        cost_estimate=pl.CostEstimate(
            flops=6 * span * width * units,
            bytes_accessed=6 * width * units + 12 * span * units,
            transcendentals=span * units,
        ),
        name="feed_forward_back" if back else "feed_forward",
    )(where, operand, *saved, gate, gate_got, up, up_got, down, down_got)


def widen_three(sums, down_shape, into_shape, size):
    def kernel(in_ref, *outs):
        for n, out in enumerate(outs):

            @pl.when(pl.program_id(0) // 4 == n)
            def _():
                out[...] = in_ref[0].astype(F32)

    def spot(n):
        if n == 0:
            return lambda t: (jnp.clip(t, 0, 3), 0)
        return lambda t: (0, jnp.clip(t - 4 * n, 0, 3))

    return pl.pallas_call(
        kernel,
        out_shape=[jax.ShapeDtypeStruct(x, F32) for x in (down_shape, into_shape, into_shape)],
        grid=(12,),
        in_specs=[pl.BlockSpec((1, size, size), lambda t: (t % 2, t // 2, 0))],
        out_specs=[pl.BlockSpec((size, size), spot(n)) for n in range(3)],
        compiler_params=pltpu.CompilerParams(vmem_limit_bytes=48 * 2**20),
        name="widen_three",
    )(sums)


def widen_four(sums, shape, starts, part):
    rows, columns = shape
    qk, v, o = (start // part for start in starts)

    def kernel(qk_a, qk_b, v_a, v_b, o_ref, q_out, k_out, v_out, o_out):
        step = pl.program_id(0)
        o_out[...] = o_ref[0].astype(F32)
        for core in range(2):
            for pair, out, at in ((0, q_out, 0), (1, k_out, 2)):
                for x, ref in enumerate((qk_a, qk_b)):
                    spot = (2 * core + x) * part
                    source = (at + core) * part
                    out[:, spot : spot + part] = ref[0, :, source : source + part].astype(F32)
        for high in range(2):

            @pl.when(step // 2 == high)
            def _():
                for core in range(2):
                    for x, ref in enumerate((v_a, v_b)):
                        spot = (2 * core + x) * part
                        source = (2 * high + core) * part
                        v_out[:, spot : spot + part] = ref[0, :, source : source + part].astype(F32)

    block = (1, part, columns)
    return pl.pallas_call(
        kernel,
        out_shape=[jax.ShapeDtypeStruct(shape, F32)] * 4,
        grid=(rows // part,),
        in_specs=[
            pl.BlockSpec(block, lambda i: (0, qk + i, 0)),
            pl.BlockSpec(block, lambda i: (1, qk + i, 0)),
            pl.BlockSpec(block, lambda i: (0, v + i % 2, 0)),
            pl.BlockSpec(block, lambda i: (1, v + i % 2, 0)),
            pl.BlockSpec(block, lambda i: (i % 2, o + i // 2, 0)),
        ],
        out_specs=[pl.BlockSpec((part, columns), lambda i: (i, 0))] * 4,
        compiler_params=pltpu.CompilerParams(vmem_limit_bytes=32 * 2**20),
        name="widen_four",
    )(sums, sums, sums, sums, sums)


def body(
    tokens,
    teacher,
    segments,
    valid_mask,
    query_weight,
    key_weight,
    value_weight,
    output_weight,
    gate_weight,
    up_weight,
    down_weight,
):
    rows = tokens.shape[0]
    cols = lax.axis_size("col")
    row = lax.axis_index("row")
    col = lax.axis_index("col")
    side = lax.axis_index("dp") % 2
    sides = [(i, i ^ 1) for i in range(lax.axis_size("dp"))]
    block = tokens.shape[1]
    half_width = block * cols
    wide = query_weight.shape[1] // 2
    units = gate_weight.shape[1] // 2
    part_units = units // 2
    part_wide = wide // 2
    tile = min(512, part_units)
    span = rows // 2
    own = span // 2
    first_row = row == 0
    where = jnp.stack([row, side]).astype(jnp.int32)
    tie = lax.optimization_barrier

    def swap(operand):
        return lax.ppermute(operand, "row", [(0, 1), (1, 0)])

    def cross(operand):
        return lax.ppermute(operand, "dp", sides)

    def gather_blocks(operand):
        if cols == 2:
            got = lax.ppermute(operand, "col", [(0, 1), (1, 0)])
            return ordered(col == 0, operand, got, 1)
        return lax.all_gather(operand, "col", axis=1, tiled=True)

    def from_chips(sent):
        if cols == 2:
            return lax.ppermute(sent.astype(BF), "col", [(0, 1), (1, 0)])
        sent = sent.astype(F32)
        return lax.psum(sent, "col") - sent

    def both_cores(kept):
        return jnp.concatenate([kept, swap(swap_halves(kept, 1))], axis=0)

    def from_cores(first, second):
        other = swap(swap_halves(jnp.concatenate([first, second], axis=0), 1))
        return [first, other[:own], second, other[own:]]

    def sum_cores(near, far):
        sent = jnp.concatenate([far[own:], near[own:]], axis=1).astype(BF)
        return jnp.concatenate([near[:own], far[:own]], axis=1) + swap(sent).astype(F32)

    def local_order(vector):
        pieces = []
        for j in range(2):
            piece = vector[j * span : (j + 1) * span]
            pieces.append(ordered(first_row, piece[:own], piece[own:], 0))
        return pieces

    blocks = []
    for j in range(2):
        piece = tokens[j * span : (j + 1) * span]
        blocks.append(gather_blocks(ordered(first_row, piece[:own], piece[own:], 0)))

    def columns_of(core):
        return jnp.concatenate(
            [take(w, core, wide, 1) for w in (query_weight, key_weight, value_weight)], axis=1
        )

    qkv_own, qkv_got = columns_of(row), swap(columns_of(1 - row))
    out_own = take(output_weight, row, wide, 0)
    out_got = swap(take(output_weight, 1 - row, wide, 0))
    weights = (gate_weight, up_weight, down_weight)

    validity = valid_mask.astype(F32)
    token_total = jnp.sum(validity).reshape(1, 1)
    hops = [(axis, 1 << k) for axis in ("dp", "row", "col") for k in range(10)]
    hops = [(axis, step) for axis, step in hops if step < lax.axis_size(axis)]
    token_hops = [h for h in hops if h[0] == "dp"]
    segs = local_order(segments)
    places = local_order(jnp.arange(rows, dtype=jnp.int32))
    valids = [v[:own, None] for v in local_order(validity)]
    tables = [rope_tables(p) for p in places]
    spot_cols = [jnp.stack([g, p], axis=1) for g, p in zip(segs, places)]
    spot_rows = [
        jnp.stack([jnp.concatenate(segs[: j + 1]), jnp.concatenate(places[: j + 1])])
        for j in range(2)
    ]

    inputs, first_stats, low_first = [], [], []
    query_heads, key_heads, value_heads = [], [], []
    attended, logsums = [], []

    def first_norm(j, half):
        whole = jnp.concatenate([half, swap(swap_halves(half, 0))], axis=1)
        whole_f = whole.astype(F32)
        average, factor = moments(whole_f)
        inputs.append(whole[:own])
        first_stats.append((average[:own], factor[:own]))
        low_first.append(((whole_f - average) * factor).astype(BF))
        return low_first[j]

    def attention(j, operand):
        out = jax.ShapeDtypeStruct((span, wide), BF)
        q, k, v, heads, logsum, kept, sent = in_vmem(
            attention_kernel,
            "attention",
            [out] * 4
            + [
                jax.ShapeDtypeStruct((span, wide), F32),
                jax.ShapeDtypeStruct((own, 2 * half_width), F32),
                jax.ShapeDtypeStruct((own, 2 * half_width), BF),
            ],
            [operand, qkv_own, qkv_got, out_own, out_got, *tables[j], spot_cols[j], spot_rows[j]]
            + [x for pair in zip(key_heads, value_heads) for x in pair],
        )
        query_heads.append(q)
        key_heads.append(k)
        value_heads.append(v)
        attended.append(heads)
        logsums.append(logsum)
        return kept, sent

    hidden, second_stats, low_second = [], [], []

    def second_norm(j, part, got):
        hidden.append(inputs[j].astype(F32) + (part + got.astype(F32)))
        average, factor = moments(hidden[j])
        second_stats.append((average, factor))
        low_second.append(both_cores(((hidden[j] - average) * factor).astype(BF)))
        return low_second[j]

    saved, acts, act_gives = [], [], []

    def forward(operand, received):
        return feed_forward(False, where, operand, (), weights, received, units, tile)

    def after_forward(j, raw):
        gate_out, up_out, act_keep, act_give, kept, sent = raw
        saved.append((gate_out, up_out))
        acts.append(act_keep)
        act_gives.append(act_give)
        piece = teacher[j * span : (j + 1) * span]
        piece = ordered(first_row, piece[:own], piece[own:], 0)
        near, far = piece[:own].astype(F32), swap(piece[own:]).astype(F32)
        minus = [jnp.where(col == b, near, 0.0) for b in range(cols)]
        minus += [jnp.where(col == b, far, 0.0) for b in range(cols)]
        part = kept + swap(sent).astype(F32) - jnp.concatenate(minus, axis=1)
        return part, (near, far)

    outputs, errors, grad_results, low_results = [], [], [], []

    def loss_of(j, part, got, targets):
        near, far = targets
        error = hidden[j] + (part + got.astype(F32))
        near_error = take(error[:, :half_width], col, block, 1)
        far_error = take(error[:, half_width:], col, block, 1)
        outputs.append(
            ordered(
                first_row,
                (near_error + near).astype(BF),
                swap((far_error + far).astype(BF)),
                0,
            )
        )
        errors.append(
            0.5 * jnp.sum(valids[j] * (near_error * near_error + far_error * far_error))
        )
        grad_results.append(scale * valids[j] * error)
        low_results.append(both_cores(grad_results[j].astype(BF)))
        return low_results[j]

    def backward(j, operand, received):
        return feed_forward(True, where, operand, saved[j], weights, received, units, tile)

    grad_hiddens, low_hiddens = [], []

    def second_norm_back(j, part, got):
        gradient = part + got.astype(F32)
        average, factor = second_stats[j]
        normed = (hidden[j] - average) * factor
        grad_hiddens.append(grad_results[j] + normalize_back(gradient, normed, factor))
        low_hiddens.append(both_cores(grad_hiddens[j].astype(BF)))
        return low_hiddens[j]

    def attention_back(j, operand, extra):
        first = jax.ShapeDtypeStruct((span, wide), F32)
        shapes = [jax.ShapeDtypeStruct((span, wide), BF), first, first]
        if j == 1:
            shapes = [jax.ShapeDtypeStruct((span, n * wide), BF) for n in (2, 3)]
        return in_vmem(
            attention_back_kernel,
            "attention_back",
            shapes,
            [
                operand,
                out_own,
                out_got,
                *tables[j],
                spot_cols[j],
                spot_rows[j],
                logsums[j],
                query_heads[j],
                key_heads[j],
                value_heads[j],
                *extra,
            ],
        )

    def joined(pair):
        return pair[0] + swap(pair[1]).astype(F32)

    part_a = joined(attention(0, first_norm(0, blocks[0])))
    operand = first_norm(1, blocks[1])
    operand, part_a, low, token_total, core = tie(
        (operand, part_a, part_a.astype(BF), token_total, 1 - row)
    )
    got_a = from_chips(low)
    token_total = hop(token_total, *token_hops[0])
    pair = attention(1, operand)
    received = (
        swap(take(gate_weight, core, units, 1)),
        swap(take(up_weight, core, units, 1)),
        swap(take(down_weight, core, units, 0)),
    )
    pair, got_a, token_total, received = tie((pair, got_a, token_total, received))
    part_b = joined(pair)
    two_a = second_norm(0, part_a, got_a)
    two_a, part_b, low, mine, token_total = tie(
        (two_a, part_b, part_b.astype(BF), two_a[:own], token_total)
    )
    token_total = hop(token_total, *token_hops[1])
    got_b, cross_two_a = from_chips(low), cross(mine)
    raw = forward(two_a, received)
    raw, got_b, cross_two_a, token_total = tie((raw, got_b, cross_two_a, token_total))
    part_a, targets_a = after_forward(0, raw)
    two_b = second_norm(1, part_b, got_b)
    two_b, part_a, low, mine, token_total = tie(
        (two_b, part_a, part_a.astype(BF), two_b[:own], token_total)
    )
    for step in token_hops[2:]:
        token_total = hop(token_total, *step)
    got_a, cross_two_b = from_chips(low), cross(mine)
    raw = forward(two_b, received)
    raw, got_a, cross_two_b, token_total = tie((raw, got_a, cross_two_b, token_total))
    scale = (rows * lax.axis_size("dp")) / token_total
    part_b, targets_b = after_forward(1, raw)
    low_a = loss_of(0, part_a, got_a, targets_a)
    low_a, part_b, low, mine = tie((low_a, part_b, part_b.astype(BF), act_gives[0]))
    got_b, cross_act_a = from_chips(low), cross(mine)
    raw = backward(0, low_a, received)
    raw, got_b, cross_act_a = tie((raw, got_b, cross_act_a))
    ups_a, part_a = raw[:4], joined(raw[4:])
    low_b = loss_of(1, part_b, got_b, targets_b)
    low_b, part_a, low, mine, error_sum = tie(
        (
            low_b,
            part_a,
            part_a.astype(BF),
            act_gives[1],
            (errors[0] + errors[1]).reshape(1, 1),
        )
    )
    error_sum = hop(error_sum, *hops[0])
    got_a, cross_act_b = from_chips(low), cross(mine)
    raw = backward(1, low_b, received)
    raw, got_a, cross_act_b, error_sum = tie((raw, got_a, cross_act_b, error_sum))
    ups_b, part_b = raw[:4], joined(raw[4:])
    hidden_a = second_norm_back(0, part_a, got_a)
    hidden_a, part_b, low, mine = tie((hidden_a, part_b, part_b.astype(BF), low_a[:own]))
    error_sum = hop(error_sum, *hops[1])
    got_b, cross_low_a = from_chips(low), cross(mine)
    parts = attention_back(0, hidden_a, [])
    parts, got_b, cross_low_a, error_sum = tie((parts, got_b, cross_low_a, error_sum))
    hidden_b = second_norm_back(1, part_b, got_b)
    hidden_b, parts, mine, error_sum = tie((hidden_b, parts, low_b[:own], error_sum))
    error_sum = hop(error_sum, *hops[2])
    cross_low_b = cross(mine)
    first_back, back_b = attention_back(
        1, hidden_b, [key_heads[0], value_heads[0], *tables[0], *parts[1:]]
    )
    first_back, back_b, cross_low_b, error_sum = tie(
        (first_back, back_b, cross_low_b, error_sum)
    )
    backs = [jnp.concatenate([parts[0], first_back], axis=1), back_b]
    gate_gives = [u[1] for u in (ups_a, ups_b)]
    up_gives = [u[3] for u in (ups_a, ups_b)]

    def split_rows(full):
        half = full.shape[0] // 2
        return full[:half], swap(full[half:])

    def split_cols(full):
        half = full.shape[1] // 2
        return full[:, :half], swap(full[:, half:])

    def together(lefts, rights):
        return jnp.concatenate(lefts, axis=0), jnp.concatenate(rights, axis=0)

    def product(lefts, rights):
        return contract_rows(lefts, rights).astype(BF)

    hiddens = together(attended, [hidden_a, hidden_b])
    firsts = together(low_first, backs)
    backs, mine, gate_gives = tie((backs, gate_gives[0], gate_gives))
    cross_gate_a = cross(mine)
    for step in hops[3:]:
        error_sum = hop(error_sum, *step)
    ends = [jax.ShapeDtypeStruct((own, 2 * half_width), t) for t in (F32, BF)]
    raw = in_vmem(last_kernel, "first_norm_back", ends * 2, [*backs, qkv_own, qkv_got])
    raw, cross_gate_a, error_sum = tie((raw, cross_gate_a, error_sum))
    last_parts = [joined(raw[:2]), joined(raw[2:])]
    downs = together(
        [*acts, cross_act_a, cross_act_b], [low_a, low_b, *from_cores(cross_low_a, cross_low_b)]
    )
    downs, mine = tie((downs, gate_gives[1]))
    cross_gate_b = cross(mine)
    grad_down = product(*downs)
    grad_down, cross_gate_b, up_gives = tie((grad_down, cross_gate_b, up_gives))
    down_pair = split_cols(grad_down)
    cross_up_a = cross(up_gives[0])
    grad_qkv = product(*firsts)
    grad_qkv, cross_up_a, up_gives, hiddens = tie((grad_qkv, cross_up_a, up_gives, hiddens))
    qkv_pair = split_rows(grad_qkv)
    out_pair = split_cols(product(*hiddens))
    twos = [two_a, two_b, *from_cores(cross_two_a, cross_two_b)]
    gates = together(twos, [ups_a[0], ups_b[0], cross_gate_a, cross_gate_b])
    gates, mine, qkv_pair, out_pair = tie((gates, up_gives[1], qkv_pair, out_pair))
    cross_up_b = cross(mine)
    grad_gate = product(*gates)
    grad_gate, cross_up_b = tie((grad_gate, cross_up_b))
    gate_pair = split_rows(grad_gate)
    up_pair = split_rows(
        product(*together(twos, [ups_a[2], ups_b[2], cross_up_a, cross_up_b]))
    )

    def halves(pair, which):
        three = [
            ordered(
                first_row,
                *(take(p[:, i * wide : (i + 1) * wide], which, part_wide, 1) for p in pair),
                1,
            )
            for i in range(3)
        ]
        return [pack(jnp.concatenate(three[:2], axis=1), half_width), pack(three[2], half_width)]

    pieces, spots, starts = [], [], []
    total = 0
    out_mine = [take(p, side, part_wide, 0) for p in out_pair]
    out_give = [take(p, 1 - side, part_wide, 0) for p in out_pair]
    for pair in (down_pair, gate_pair, up_pair, out_mine):
        packed = [pack(p, half_width) for p in pair]
        size = packed[0].shape[0]
        pieces += packed
        spots += [
            lambda r, total=total, size=size: total + r * size,
            lambda r, total=total, size=size: total + (1 - r) * size,
        ]
        starts.append((total, size))
        total += 2 * size
    for packed in halves(qkv_pair, side):
        size = packed.shape[0]
        pieces.append(packed)
        spots.append(lambda r, total=total: total + 0 * r)
        starts.append((total, size))
        total += size
    gives = [pack(p, half_width) for p in out_give] + halves(qkv_pair, 1 - side)
    last_gots = [from_chips(p) for p in last_parts]
    sums = line_sum(pieces, spots, gives, chunk=min(256, total // 8))
    sums, last_parts, last_gots = tie((sums, last_parts, last_gots))

    if cols == 2 and part_units == half_width:
        grad_down, grad_gate, grad_up = widen_three(
            sums, down_weight.shape, gate_weight.shape, half_width
        )
        grad_query, grad_key, grad_value, grad_output = widen_four(
            sums, query_weight.shape, [starts[n][0] for n in (4, 5, 3)], part_wide
        )
    else:

        def blocks_of(which, columns):
            start, size = starts[which]
            return [
                unpack(sums[x, start + s * size : start + (s + 1) * size], columns)
                for s in range(2)
                for x in range(2)
            ]

        grad_down = jnp.concatenate(blocks_of(0, half_width), axis=0).astype(F32)
        grad_gate = jnp.concatenate(blocks_of(1, part_units), axis=1).astype(F32)
        grad_up = jnp.concatenate(blocks_of(2, part_units), axis=1).astype(F32)
        grad_output = jnp.concatenate(blocks_of(3, half_width), axis=0).astype(F32)
        three = [[], [], []]
        qk, v = (
            [unpack(sums[x, starts[n][0] : starts[n][0] + starts[n][1]], k * part_wide) for x in range(2)]
            for n, k in ((4, 4), (5, 2))
        )
        for s in range(2):
            for x in range(2):
                at = s * part_wide
                three[0].append(qk[x][:, at : at + part_wide])
                three[1].append(qk[x][:, 2 * part_wide + at : 2 * part_wide + at + part_wide])
                three[2].append(v[x][:, at : at + part_wide])
        grad_query, grad_key, grad_value = (
            jnp.concatenate(t, axis=1).astype(F32) for t in three
        )

    grad_tokens = []
    for j in range(2):
        gradient = last_parts[j] + last_gots[j].astype(F32)
        average, factor = first_stats[j]
        normed = (inputs[j].astype(F32) - average) * factor
        grads = grad_hiddens[j] + normalize_back(gradient, normed, factor)
        near = take(grads[:, :half_width], col, block, 1)
        far = take(grads[:, half_width:], col, block, 1)
        grad_tokens.append(ordered(first_row, near, swap(far), 0))
    loss_value = (error_sum / token_total)[0, 0]
    return (
        jnp.concatenate(outputs, axis=0),
        loss_value,
        jnp.concatenate(grad_tokens, axis=0),
        grad_query,
        grad_key,
        grad_value,
        grad_output,
        grad_gate,
        grad_up,
        grad_down,
    )


def solution(mesh):
    features = P("dp", ("row", "col"))
    into, back = P("row", "col"), P("col", "row")
    in_specs = (features, features, P("dp"), P("dp"), into, into, into, back, into, into, back)
    out_specs = (features, P(), features, into, into, into, back, into, into, back)
    return jax.shard_map(body, mesh=mesh, in_specs=in_specs, out_specs=out_specs, check_vma=False)
```

```python
import functools
import math

import jax
import jax.numpy as jnp
from jax import lax
from jax.experimental import pallas as pl
from jax.experimental.pallas import tpu as pltpu
from jax.sharding import PartitionSpec as P

D = 2048
HEAD = 128
LEN = 1024
EPS = 1e-05
THETA = 10000.0
NEG = -1e30

BF = jnp.bfloat16
F32 = jnp.float32


def rope_tables(places):
    half_width = HEAD // 2
    frequency = jnp.exp(
        jnp.arange(half_width).astype(F32) * (-2.0 * math.log(THETA) / HEAD)
    )
    angles = places.astype(F32)[:, None] * frequency[None, :]
    cosine, sine_table = jnp.cos(angles), jnp.sin(angles)
    return (
        jnp.concatenate([cosine, cosine], axis=1),
        jnp.concatenate([-sine_table, sine_table], axis=1),
    )


def dot(left, right):
    return jnp.dot(left, right, preferred_element_type=F32)


def contract_rows(left, right):
    return lax.dot_general(left, right, (((0,), (0,)), ((), ())), preferred_element_type=F32)


def contract_cols(left, right):
    return lax.dot_general(left, right, (((1,), (1,)), ((), ())), preferred_element_type=F32)


def take(operand, index, size, axis):
    return lax.dynamic_slice_in_dim(operand, index * size, size, axis)


def swap_halves(operand, axis):
    half = operand.shape[axis] // 2
    return jnp.concatenate(
        [
            lax.slice_in_dim(operand, half, 2 * half, axis=axis),
            lax.slice_in_dim(operand, 0, half, axis=axis),
        ],
        axis=axis,
    )


def ordered(first, mine, other, axis):
    return jnp.concatenate(
        [jnp.where(first, mine, other), jnp.where(first, other, mine)], axis=axis
    )


def add_low(left, right):
    return (left.astype(F32) + right.astype(F32)).astype(BF)


MESH = pl.DeviceIdType.MESH


def line_kernel(sizes, spots, given, chunk, lag, ahead, deep, *refs):
    count = len(sizes)
    pieces, gives = refs[:count], refs[count : count + given]
    out = refs[count + given]
    held, got_in, got_mid, got_give, load, send_in, send_mid, send_out, send_side, in_sem, mid_sem, out_sem, side_sem, keep, send_give, give_sem = refs[count + given + 1:]
    places = lax.axis_size("dp") // 2
    dp = lax.axis_index("dp")
    row = lax.axis_index("row")
    col = lax.axis_index("col")
    place, side = dp // 2, dp % 2
    half = places // 2
    low = place < half
    depth = jnp.where(low, place, places - 1 - place)
    is_mid = depth == half - 1
    is_end = depth == 0
    to_in = jnp.where(low, place + 1, place - 1)
    to_out = jnp.where(low, place - 1, place + 1)
    inner = (to_in * 2 + side, row, col)
    outer = (jnp.clip(to_out, 0, places - 1) * 2 + side, row, col)
    other = (dp + 1 - 2 * side, row, col)
    total_rows = held.shape[0]
    steps = total_rows // chunk
    base = total_rows - sum(sizes[count - given :])
    first = base // chunk

    loads = []
    for i in range(count):
        rows = sizes[i]
        at = pl.multiple_of(spots[i](row), 16)
        loads.append(pltpu.make_async_copy(pieces[i], held.at[pl.ds(at, rows)], load.at[i]))
        loads[-1].start()

    barrier = pltpu.get_barrier_semaphore()
    pl.semaphore_signal(barrier, inc=1, device_id=inner, device_id_type=MESH)
    pl.semaphore_signal(barrier, inc=1, device_id=other, device_id_type=MESH)

    @pl.when(jnp.logical_not(is_end))
    def _():
        pl.semaphore_signal(barrier, inc=1, device_id=outer, device_id_type=MESH)
        pl.semaphore_wait(barrier, 3)

    @pl.when(is_end)
    def _():
        pl.semaphore_wait(barrier, 2)

    given_copies = []
    for i in range(given):
        spot = pl.multiple_of(spots[count - given + i](row) - base, 16)
        given_copies.append(
            pltpu.make_async_remote_copy(
                src_ref=gives[i], dst_ref=got_give.at[pl.ds(spot, sizes[count - given + i])],
                send_sem=send_give.at[i], recv_sem=give_sem.at[i],
                device_id=other, device_id_type=MESH))
        given_copies[-1].start()
    for copy in loads:
        copy.wait()

    def add_given(t):
        @pl.when(t == first)
        def _():
            for copy in given_copies:
                copy.wait()

        @pl.when(t >= first)
        def _():
            held[at(t)] = (
                held[at(t)].astype(F32) + got_give[at(t - first)].astype(F32)
            ).astype(BF)

    def at(t):
        return pl.ds(pl.multiple_of(t * chunk, chunk), chunk)

    def inward(t):
        return pltpu.make_async_remote_copy(
            src_ref=held.at[at(t)], dst_ref=got_in.at[at(t)], send_sem=send_in.at[t],
            recv_sem=in_sem.at[t], device_id=inner, device_id_type=MESH)

    def middle(t):
        return pltpu.make_async_remote_copy(
            src_ref=held.at[at(t)], dst_ref=got_mid.at[at(t)], send_sem=send_mid.at[t],
            recv_sem=mid_sem.at[t], device_id=inner, device_id_type=MESH)

    def outward(t, source):
        return pltpu.make_async_remote_copy(
            src_ref=source, dst_ref=out.at[side, at(t)], send_sem=send_out.at[t],
            recv_sem=out_sem.at[t], device_id=outer, device_id_type=MESH)

    def across(t, source):
        return pltpu.make_async_remote_copy(
            src_ref=source, dst_ref=out.at[side, at(t)], send_sem=send_side.at[t],
            recv_sem=side_sem.at[t], device_id=other, device_id_type=MESH)

    def store(t):
        return pltpu.make_async_copy(got_in.at[at(t)], out.at[side, at(t)], keep.at[t])

    def mid_loop(t, _):
        @pl.when(t < steps)
        def _():
            add_given(t)

            @pl.when(jnp.logical_not(is_end))
            def _():
                inward(t).wait_recv()
                held[at(t)] = (held[at(t)].astype(F32) + got_in[at(t)].astype(F32)).astype(BF)
            @pl.when(t >= deep)
            def _():
                middle(t - deep).wait_send()
            middle(t).start()

        @pl.when(t >= ahead)
        def _():
            u = t - ahead
            middle(u).wait_recv()
            got_in[at(u)] = (held[at(u)].astype(F32) + got_mid[at(u)].astype(F32)).astype(BF)
            store(u).start()
            @pl.when(u >= deep)
            def _():
                @pl.when(jnp.logical_not(is_end))
                def _():
                    outward(u - deep, got_in.at[at(u)]).wait_send()
                across(u - deep, got_in.at[at(u)]).wait_send()
            @pl.when(jnp.logical_not(is_end))
            def _():
                outward(u, got_in.at[at(u)]).start()
            across(u, got_in.at[at(u)]).start()
        return 0

    def far_loop(t, _):
        @pl.when(t < steps)
        def _():
            add_given(t)

            @pl.when(jnp.logical_not(is_end))
            def _():
                inward(t).wait_recv()
                held[at(t)] = (held[at(t)].astype(F32) + got_in[at(t)].astype(F32)).astype(BF)
            @pl.when(t >= deep)
            def _():
                inward(t - deep).wait_send()
            inward(t).start()

        @pl.when(t >= lag)
        def _():
            u = t - lag
            outward(u, out.at[side, at(u)]).wait_recv()
            @pl.when(u >= deep)
            def _():
                @pl.when(jnp.logical_not(is_end))
                def _():
                    outward(u - deep, out.at[side, at(u)]).wait_send()
                across(u - deep, out.at[side, at(u)]).wait_send()
            @pl.when(jnp.logical_not(is_end))
            def _():
                outward(u, out.at[side, at(u)]).start()
            across(u, out.at[side, at(u)]).start()
        return 0

    @pl.when(is_mid)
    def _():
        lax.fori_loop(0, steps + ahead, mid_loop, 0)
        def finish(t, _):
            store(t).wait()
            across(t, got_in.at[at(t)]).wait_recv()
            @pl.when(t >= steps - deep)
            def _():
                middle(t).wait_send()
                across(t, got_in.at[at(t)]).wait_send()
                @pl.when(jnp.logical_not(is_end))
                def _():
                    outward(t, got_in.at[at(t)]).wait_send()
            return 0
        lax.fori_loop(0, steps, finish, 0)

    @pl.when(jnp.logical_not(is_mid))
    def _():
        lax.fori_loop(0, steps + lag, far_loop, 0)
        def finish(t, _):
            across(t, out.at[side, at(t)]).wait_recv()
            @pl.when(t >= steps - deep)
            def _():
                inward(t).wait_send()
                across(t, out.at[side, at(t)]).wait_send()
                @pl.when(jnp.logical_not(is_end))
                def _():
                    outward(t, out.at[side, at(t)]).wait_send()
            return 0
        lax.fori_loop(0, steps, finish, 0)


def line_sum(pieces, spots, gives, chunk, lag=8, ahead=2, deep=2):
    sizes = [p.shape[0] for p in pieces]
    rows, width = sum(sizes), pieces[0].shape[1]
    steps = rows // chunk
    given_rows = sum(g.shape[0] for g in gives)
    dma = pltpu.SemaphoreType.DMA
    return pl.pallas_call(
        functools.partial(line_kernel, sizes, spots, len(gives), chunk, lag, ahead, deep),
        out_shape=jax.ShapeDtypeStruct((2, rows, width), BF),
        in_specs=[pl.BlockSpec(memory_space=pl.ANY)] * (len(pieces) + len(gives)),
        out_specs=pl.BlockSpec(memory_space=pl.ANY),
        scratch_shapes=[pltpu.VMEM((rows, width), BF)] * 3
        + [pltpu.VMEM((given_rows, width), BF)]
        + [dma((len(pieces),))]
        + [dma((steps,))] * 9
        + [dma((len(gives),))] * 2,
        compiler_params=pltpu.CompilerParams(
            collective_id=0, has_side_effects=True, vmem_limit_bytes=58 * 2**20
        ),
        name="line_sum",
    )(*pieces, *gives)


def pack(operand, width):
    rows, columns = operand.shape
    if columns == width:
        return operand
    if columns > width:
        return jnp.concatenate(
            [operand[:, i : i + width] for i in range(0, columns, width)], axis=0
        )
    times = width // columns
    step = rows // times
    return jnp.concatenate([operand[i * step : (i + 1) * step] for i in range(times)], axis=1)


def unpack(operand, columns):
    rows, width = operand.shape
    if columns == width:
        return operand
    if columns > width:
        step = rows * width // columns
        return jnp.concatenate(
            [operand[i * step : (i + 1) * step] for i in range(columns // width)], axis=1
        )
    return jnp.concatenate(
        [operand[:, i : i + columns] for i in range(0, width, columns)], axis=0
    )


def hop(operand, axis, step):
    size = lax.axis_size(axis)
    return operand + lax.ppermute(operand, axis, [(i, i ^ step) for i in range(size)])


def turned(operand, cosine, sine_table):
    return operand * cosine + pltpu.roll(operand, HEAD // 2, 1) * sine_table


def allowed_pairs(spot_col, spot_row):
    return (spot_col[:, 0:1] == spot_row[0:1, :]) & (spot_row[1:2, :] <= spot_col[:, 1:2])


def attention_kernel(
    x_ref, own_ref, got_ref, out_own, out_got, cos_ref, sin_ref, col_ref, row_ref, *refs
):
    earlier, (q_out, k_out, v_out, att_out, lse_out, kept, sent) = refs[:-7], refs[-7:]
    half = x_ref.shape[1] // 2
    wide = out_own.shape[0]
    own = kept.shape[0]
    near, far = x_ref[:, :half], x_ref[:, half:]
    cosine, sine_table = cos_ref[...], sin_ref[...]
    for which, out in enumerate((q_out, k_out, v_out)):
        at = slice(which * wide, (which + 1) * wide)
        raw = dot(near, own_ref[:, at]) + dot(far, got_ref[:, at])
        for h in range(wide // HEAD):
            head = slice(h * HEAD, (h + 1) * HEAD)
            value = raw[:, head]
            if which < 2:
                value = turned(value, cosine, sine_table)
            out[:, head] = value.astype(BF)
    allowed = allowed_pairs(col_ref[...], row_ref[...])
    for h in range(wide // HEAD):
        head = slice(h * HEAD, (h + 1) * HEAD)
        keys, values = k_out[:, head], v_out[:, head]
        if earlier:
            keys = jnp.concatenate([earlier[0][:, head], keys], axis=0)
            values = jnp.concatenate([earlier[1][:, head], values], axis=0)
        scores = contract_cols(q_out[:, head], keys) * (1.0 / math.sqrt(HEAD))
        scores = jnp.where(allowed, scores, NEG)
        row_max = jnp.max(scores, axis=-1, keepdims=True)
        shares = jnp.exp(scores - row_max)
        totals = jnp.sum(shares, axis=-1, keepdims=True)
        shares = (shares / totals).astype(BF)
        att_out[:, head] = dot(shares, values).astype(BF)
        lse_out[:, head] = jnp.broadcast_to(row_max + jnp.log(totals), (2 * own, HEAD))
    near, far = dot(att_out[...], out_own[...]), dot(att_out[...], out_got[...])
    kept[:, :half] = near[:own]
    kept[:, half:] = far[:own]
    sent[:, :half] = far[own:].astype(BF)
    sent[:, half:] = near[own:].astype(BF)


def attention_back_kernel(
    own_rows, other_rows, out_own, out_got, cos_ref, sin_ref, col_ref, row_ref,
    lse_ref, q_ref, k_ref, v_ref, *refs
):
    span, wide = q_ref.shape
    g_ref = jnp.concatenate([own_rows[...], other_rows[...]], axis=0)
    half = g_ref.shape[1] // 2
    factor = 1.0 / math.sqrt(HEAD)
    cosine, sine_table = cos_ref[...], -sin_ref[...]
    grads = contract_cols(g_ref[:, :half], out_own[...])
    grads = (grads + contract_cols(g_ref[:, half:], out_got[...])).astype(BF)
    allowed = allowed_pairs(col_ref[...], row_ref[...])
    last = len(refs) > 3
    for h in range(wide // HEAD):
        head = slice(h * HEAD, (h + 1) * HEAD)
        queries, gradient = q_ref[:, head], grads[:, head]
        keys, values = k_ref[:, head], v_ref[:, head]
        if last:
            keys = jnp.concatenate([refs[0][:, head], keys], axis=0)
            values = jnp.concatenate([refs[1][:, head], values], axis=0)
        scores = jnp.where(allowed, contract_cols(queries, keys) * factor, NEG)
        shares = jnp.exp(scores - lse_ref[:, h * HEAD : h * HEAD + 1])
        grad_shares = contract_cols(gradient, values)
        centre = jnp.sum(shares * grad_shares, axis=-1, keepdims=True)
        grad_scores = (shares * (grad_shares - centre)).astype(BF)
        grad_q = turned(dot(grad_scores, keys) * factor, cosine, sine_table)
        grad_k = contract_rows(grad_scores, queries) * factor
        grad_v = contract_rows(shares.astype(BF), gradient)
        if not last:
            q_out, k_out, v_out = refs
            q_out[:, head] = grad_q.astype(BF)
            k_out[:, head] = grad_k
            v_out[:, head] = grad_v
        else:
            cos_first, sin_first, k_part, v_part, first_out, back_out = refs[2:]
            back_out[:, head] = grad_q.astype(BF)
            at = slice(wide + h * HEAD, wide + (h + 1) * HEAD)
            back_out[:, at] = turned(grad_k[span:], cosine, sine_table).astype(BF)
            first = grad_k[:span] + k_part[:, head]
            first_out[:, head] = turned(first, cos_first[...], -sin_first[...]).astype(BF)
            at = slice(2 * wide + h * HEAD, 2 * wide + (h + 1) * HEAD)
            back_out[:, at] = grad_v[span:].astype(BF)
            at = slice(wide + h * HEAD, wide + (h + 1) * HEAD)
            first_out[:, at] = (grad_v[:span] + v_part[:, head]).astype(BF)


def last_kernel(a_ref, b_ref, own_ref, got_ref, kept_a, sent_a, kept_b, sent_b):
    half = own_ref.shape[0]
    own = kept_a.shape[0]
    for ref, kept, sent in ((a_ref, kept_a, sent_a), (b_ref, kept_b, sent_b)):
        near, far = contract_cols(ref[...], own_ref[...]), contract_cols(ref[...], got_ref[...])
        kept[:, :half] = near[:own]
        kept[:, half:] = far[:own]
        sent[:, :half] = far[own:].astype(BF)
        sent[:, half:] = near[own:].astype(BF)


def in_vmem(kernel, name, out_shape, operands):
    return pl.pallas_call(
        kernel,
        out_shape=out_shape,
        in_specs=[pl.BlockSpec(memory_space=pltpu.VMEM)] * len(operands),
        out_specs=[pl.BlockSpec(memory_space=pltpu.VMEM)] * len(out_shape),
        compiler_params=pltpu.CompilerParams(vmem_limit_bytes=52 * 2**20),
        cost_estimate=pl.CostEstimate(
            flops=8 * 10**9, bytes_accessed=2 * 10**7, transcendentals=2 * 10**6
        ),
        name=name,
    )(*operands)


def moments(operand):
    average = jnp.mean(operand, axis=-1, keepdims=True)
    centre = operand - average
    factor = lax.rsqrt(jnp.mean(centre * centre, axis=-1, keepdims=True) + EPS)
    return average, factor


def normalize_back(gradient, normed, factor):
    mean = jnp.mean(gradient, axis=-1, keepdims=True)
    crossed = jnp.mean(gradient * normed, axis=-1, keepdims=True)
    return factor * (gradient - mean - normed * crossed)


def feed_forward_kernel(
    r_ref, own_rows, other_rows, gate_own, gate_got, up_own, up_got, down_own, down_got,
    gate_out, up_out, act_keep, act_give, kept, sent, total, x_ref, *, side_steps,
):
    step, last = pl.program_id(0), pl.num_programs(0) - 1
    half = x_ref.shape[1] // 2
    own = kept.shape[0]

    @pl.when(step == 0)
    def _():
        x_ref[:own] = own_rows[...]
        x_ref[own:] = other_rows[...]

    near, far = x_ref[:, :half], x_ref[:, half:]
    gate = dot(near, gate_own[...]) + dot(far, gate_got[...])
    up = dot(near, up_own[...]) + dot(far, up_got[...])
    gate_out[...] = gate
    up_out[...] = up
    act = (gate * jax.nn.sigmoid(gate) * up).astype(BF)
    mine = step // side_steps == r_ref[1]

    @pl.when(mine)
    def _():
        act_keep[...] = act

    @pl.when(jnp.logical_not(mine))
    def _():
        act_give[...] = act

    near, far = dot(act, down_own[...]), dot(act, down_got[...])

    @pl.when(step == 0)
    def _():
        total[:, :half] = near
        total[:, half:] = far

    @pl.when(step > 0)
    def _():
        total[:, :half] += near
        total[:, half:] += far

    @pl.when(step == last)
    def _():
        kept[...] = total[:own]
        sent[:, :half] = total[own:, half:].astype(BF)
        sent[:, half:] = total[own:, :half].astype(BF)


def feed_forward_back_kernel(
    r_ref, own_rows, other_rows, gate_ref, up_ref,
    gate_own, gate_got, up_own, up_got, down_own, down_got,
    gate_keep, gate_give, up_keep, up_give, kept, sent, total, g_ref, *, side_steps,
):
    step, last = pl.program_id(0), pl.num_programs(0) - 1
    half = g_ref.shape[1] // 2
    own = kept.shape[0]

    @pl.when(step == 0)
    def _():
        g_ref[:own] = own_rows[...]
        g_ref[own:] = other_rows[...]

    grad = contract_cols(g_ref[:, :half], down_own[...]) + contract_cols(
        g_ref[:, half:], down_got[...]
    )
    gate, up = gate_ref[...], up_ref[...]
    sigmoid = jax.nn.sigmoid(gate)
    gate_back = (grad * up * sigmoid * (1.0 + gate * (1.0 - sigmoid))).astype(BF)
    up_back = (grad * gate * sigmoid).astype(BF)
    mine = step // side_steps == r_ref[1]

    @pl.when(mine)
    def _():
        gate_keep[...] = gate_back
        up_keep[...] = up_back

    @pl.when(jnp.logical_not(mine))
    def _():
        gate_give[...] = gate_back
        up_give[...] = up_back

    near = contract_cols(gate_back, gate_own[...]) + contract_cols(up_back, up_own[...])
    far = contract_cols(gate_back, gate_got[...]) + contract_cols(up_back, up_got[...])

    @pl.when(step == 0)
    def _():
        total[:, :half] = near
        total[:, half:] = far

    @pl.when(step > 0)
    def _():
        total[:, :half] += near
        total[:, half:] += far

    @pl.when(step == last)
    def _():
        kept[...] = total[:own]
        sent[:, :half] = total[own:, half:].astype(BF)
        sent[:, half:] = total[own:, :half].astype(BF)


def feed_forward(back, where, operand, saved, weights, got, units, tile):
    own, width = operand[0].shape
    half, span, steps = width // 2, 2 * own, units // tile
    side_steps = steps // 2
    gate, up, down = weights
    gate_got, up_got, down_got = got

    def mine(i, r):
        return (0, jnp.clip(i - r[1] * side_steps, 0, side_steps - 1))

    def other(i, r):
        return (0, jnp.clip(i - (1 - r[1]) * side_steps, 0, side_steps - 1))

    whole = pl.BlockSpec((own, width), lambda i, r: (0, 0))
    wide = pl.BlockSpec((span, tile), lambda i, r: (0, i))
    into_own = pl.BlockSpec((half, tile), lambda i, r: (0, r[0] * steps + i))
    into_got = pl.BlockSpec((half, tile), lambda i, r: (0, i))
    back_own = pl.BlockSpec((tile, half), lambda i, r: (r[0] * steps + i, 0))
    back_got = pl.BlockSpec((tile, half), lambda i, r: (i, 0))
    weight_specs = [into_own, into_got, into_own, into_got, back_own, back_got]
    keep, give = pl.BlockSpec((span, tile), mine), pl.BlockSpec((span, tile), other)
    ends = [pl.BlockSpec((own, width), lambda i, r: (0, 0))] * 2
    part = jax.ShapeDtypeStruct((span, units // 2), BF)
    full = jax.ShapeDtypeStruct((span, units), F32)
    end_shapes = [
        jax.ShapeDtypeStruct((own, width), F32),
        jax.ShapeDtypeStruct((own, width), BF),
    ]
    if back:
        kernel = feed_forward_back_kernel
        in_specs = [whole, whole, wide, wide] + weight_specs
        out_specs = [keep, give, keep, give] + ends
        out_shape = [part] * 4 + end_shapes
    else:
        kernel = feed_forward_kernel
        in_specs = [whole, whole] + weight_specs
        out_specs = [wide, wide, keep, give] + ends
        out_shape = [full] * 2 + [part] * 2 + end_shapes
    return pl.pallas_call(
        functools.partial(kernel, side_steps=side_steps),
        out_shape=out_shape,
        grid_spec=pltpu.PrefetchScalarGridSpec(
            num_scalar_prefetch=1,
            grid=(steps,),
            in_specs=in_specs,
            out_specs=out_specs,
            scratch_shapes=[pltpu.VMEM((span, width), F32), pltpu.VMEM((span, width), BF)],
        ),
        compiler_params=pltpu.CompilerParams(vmem_limit_bytes=52 * 2**20),
        cost_estimate=pl.CostEstimate(
            flops=6 * span * width * units,
            bytes_accessed=6 * width * units + 12 * span * units,
            transcendentals=span * units,
        ),
        name="feed_forward_back" if back else "feed_forward",
    )(where, *operand, *saved, gate, gate_got, up, up_got, down, down_got)


def widen_three(sums, down_shape, into_shape, size):
    def kernel(in_ref, *outs):
        for n, out in enumerate(outs):

            @pl.when(pl.program_id(0) // 4 == n)
            def _():
                out[...] = in_ref[0].astype(F32)

    def spot(n):
        if n == 0:
            return lambda t: (jnp.clip(t, 0, 3), 0)
        return lambda t: (0, jnp.clip(t - 4 * n, 0, 3))

    return pl.pallas_call(
        kernel,
        out_shape=[jax.ShapeDtypeStruct(x, F32) for x in (down_shape, into_shape, into_shape)],
        grid=(12,),
        in_specs=[pl.BlockSpec((1, size, size), lambda t: (t % 2, t // 2, 0))],
        out_specs=[pl.BlockSpec((size, size), spot(n)) for n in range(3)],
        compiler_params=pltpu.CompilerParams(vmem_limit_bytes=48 * 2**20),
        name="widen_three",
    )(sums)


def widen_four(sums, shape, starts, part):
    rows, columns = shape
    qk, v, o = (start // part for start in starts)

    def kernel(qk_a, qk_b, v_a, v_b, o_ref, q_out, k_out, v_out, o_out):
        step = pl.program_id(0)
        o_out[...] = o_ref[0].astype(F32)
        for core in range(2):
            for pair, out, at in ((0, q_out, 0), (1, k_out, 2)):
                for x, ref in enumerate((qk_a, qk_b)):
                    spot = (2 * core + x) * part
                    source = (at + core) * part
                    out[:, spot : spot + part] = ref[0, :, source : source + part].astype(F32)
        for high in range(2):

            @pl.when(step // 2 == high)
            def _():
                for core in range(2):
                    for x, ref in enumerate((v_a, v_b)):
                        spot = (2 * core + x) * part
                        source = (2 * high + core) * part
                        v_out[:, spot : spot + part] = ref[0, :, source : source + part].astype(F32)

    block = (1, part, columns)
    return pl.pallas_call(
        kernel,
        out_shape=[jax.ShapeDtypeStruct(shape, F32)] * 4,
        grid=(rows // part,),
        in_specs=[
            pl.BlockSpec(block, lambda i: (0, qk + i, 0)),
            pl.BlockSpec(block, lambda i: (1, qk + i, 0)),
            pl.BlockSpec(block, lambda i: (0, v + i % 2, 0)),
            pl.BlockSpec(block, lambda i: (1, v + i % 2, 0)),
            pl.BlockSpec(block, lambda i: (i % 2, o + i // 2, 0)),
        ],
        out_specs=[pl.BlockSpec((part, columns), lambda i: (i, 0))] * 4,
        compiler_params=pltpu.CompilerParams(vmem_limit_bytes=32 * 2**20),
        name="widen_four",
    )(sums, sums, sums, sums, sums)


def body(
    tokens,
    teacher,
    segments,
    valid_mask,
    query_weight,
    key_weight,
    value_weight,
    output_weight,
    gate_weight,
    up_weight,
    down_weight,
):
    rows = tokens.shape[0]
    cols = lax.axis_size("col")
    row = lax.axis_index("row")
    col = lax.axis_index("col")
    side = lax.axis_index("dp") % 2
    sides = [(i, i ^ 1) for i in range(lax.axis_size("dp"))]
    block = tokens.shape[1]
    half_width = block * cols
    wide = query_weight.shape[1] // 2
    units = gate_weight.shape[1] // 2
    part_units = units // 2
    part_wide = wide // 2
    tile = min(512, part_units)
    span = rows // 2
    own = span // 2
    first_row = row == 0
    where = jnp.stack([row, side]).astype(jnp.int32)
    tie = lax.optimization_barrier

    def swap(operand):
        return lax.ppermute(operand, "row", [(0, 1), (1, 0)])

    def cross(operand):
        return lax.ppermute(operand, "dp", sides)

    def gather_blocks(operand):
        if cols == 2:
            got = lax.ppermute(operand, "col", [(0, 1), (1, 0)])
            return ordered(col == 0, operand, got, 1)
        return lax.all_gather(operand, "col", axis=1, tiled=True)

    def from_chips(sent):
        if cols == 2:
            return lax.ppermute(sent.astype(BF), "col", [(0, 1), (1, 0)])
        sent = sent.astype(F32)
        return lax.psum(sent, "col") - sent

    def both_cores(kept):
        return [kept, swap(swap_halves(kept, 1))]

    def from_cores(first, second):
        other = swap(swap_halves(jnp.concatenate([first, second], axis=0), 1))
        return [first, other[:own], second, other[own:]]

    def sum_cores(near, far):
        sent = jnp.concatenate([far[own:], near[own:]], axis=1).astype(BF)
        return jnp.concatenate([near[:own], far[:own]], axis=1) + swap(sent).astype(F32)

    def local_order(vector):
        pieces = []
        for j in range(2):
            piece = vector[j * span : (j + 1) * span]
            pieces.append(ordered(first_row, piece[:own], piece[own:], 0))
        return pieces

    blocks = []
    for j in range(2):
        piece = tokens[j * span : (j + 1) * span]
        blocks.append(gather_blocks(ordered(first_row, piece[:own], piece[own:], 0)))

    targets = []
    for j in range(2):
        piece = teacher[j * span : (j + 1) * span]
        piece = ordered(first_row, piece[:own], piece[own:], 0)
        targets.append((piece[:own], swap(piece[own:])))
    slices = [take(w, 1 - row, units, 1) for w in (gate_weight, up_weight)]
    blocks[0], slices, targets = tie((blocks[0], slices, targets))

    def columns_of(core):
        return jnp.concatenate(
            [take(w, core, wide, 1) for w in (query_weight, key_weight, value_weight)], axis=1
        )

    qkv_own, qkv_got = columns_of(row), swap(columns_of(1 - row))
    out_own = take(output_weight, row, wide, 0)
    out_got = swap(take(output_weight, 1 - row, wide, 0))
    weights = (gate_weight, up_weight, down_weight)

    validity = valid_mask.astype(F32)
    token_total = jnp.sum(validity).reshape(1, 1)
    hops = [(axis, 1 << k) for axis in ("dp", "row", "col") for k in range(10)]
    hops = [(axis, step) for axis, step in hops if step < lax.axis_size(axis)]
    token_hops = [h for h in hops if h[0] == "dp"]
    segs = local_order(segments)
    places = local_order(jnp.arange(rows, dtype=jnp.int32))
    valids = [v[:own, None] for v in local_order(validity)]
    tables = [rope_tables(p) for p in places]
    spot_cols = [jnp.stack([g, p], axis=1) for g, p in zip(segs, places)]
    spot_rows = [
        jnp.stack([jnp.concatenate(segs[: j + 1]), jnp.concatenate(places[: j + 1])])
        for j in range(2)
    ]

    inputs, first_stats, low_first = [], [], []
    query_heads, key_heads, value_heads = [], [], []
    attended, logsums = [], []

    def first_norm(j, half):
        whole = jnp.concatenate([half, swap(swap_halves(half, 0))], axis=1)
        whole_f = whole.astype(F32)
        average, factor = moments(whole_f)
        inputs.append(whole[:own])
        first_stats.append((average[:own], factor[:own]))
        low_first.append(((whole_f - average) * factor).astype(BF))
        return low_first[j]

    def attention(j, operand):
        out = jax.ShapeDtypeStruct((span, wide), BF)
        q, k, v, heads, logsum, kept, sent = in_vmem(
            attention_kernel,
            "attention",
            [out] * 4
            + [
                jax.ShapeDtypeStruct((span, wide), F32),
                jax.ShapeDtypeStruct((own, 2 * half_width), F32),
                jax.ShapeDtypeStruct((own, 2 * half_width), BF),
            ],
            [operand, qkv_own, qkv_got, out_own, out_got, *tables[j], spot_cols[j], spot_rows[j]]
            + [x for pair in zip(key_heads, value_heads) for x in pair],
        )
        query_heads.append(q)
        key_heads.append(k)
        value_heads.append(v)
        attended.append(heads)
        logsums.append(logsum)
        return kept, sent

    hidden, second_stats, low_second = [], [], []

    def second_norm(j, part, got):
        hidden.append(inputs[j].astype(F32) + (part + got.astype(F32)))
        average, factor = moments(hidden[j])
        second_stats.append((average, factor))
        low_second.append(both_cores(((hidden[j] - average) * factor).astype(BF)))
        return low_second[j]

    saved, acts, act_gives = [], [], []

    def forward(operand, received):
        return feed_forward(False, where, operand, (), weights, received, units, tile)

    def after_forward(j, raw):
        gate_out, up_out, act_keep, act_give, kept, sent = raw
        saved.append((gate_out, up_out))
        acts.append(act_keep)
        act_gives.append(act_give)
        near, far = (t.astype(F32) for t in targets[j])
        minus = [jnp.where(col == b, near, 0.0) for b in range(cols)]
        minus += [jnp.where(col == b, far, 0.0) for b in range(cols)]
        part = kept + swap(sent).astype(F32) - jnp.concatenate(minus, axis=1)
        return part, (near, far)

    outputs, errors, grad_results, low_results = [], [], [], []

    def loss_of(j, part, got, targets):
        near, far = targets
        error = hidden[j] + (part + got.astype(F32))
        near_error = take(error[:, :half_width], col, block, 1)
        far_error = take(error[:, half_width:], col, block, 1)
        outputs.append(
            ordered(
                first_row,
                (near_error + near).astype(BF),
                swap((far_error + far).astype(BF)),
                0,
            )
        )
        errors.append(
            0.5 * jnp.sum(valids[j] * (near_error * near_error + far_error * far_error))
        )
        grad_results.append(scale * valids[j] * error)
        low_results.append(both_cores(grad_results[j].astype(BF)))
        return low_results[j]

    def backward(j, operand, received):
        return feed_forward(True, where, operand, saved[j], weights, received, units, tile)

    grad_hiddens, low_hiddens = [], []

    def second_norm_back(j, part, got):
        gradient = part + got.astype(F32)
        average, factor = second_stats[j]
        normed = (hidden[j] - average) * factor
        grad_hiddens.append(grad_results[j] + normalize_back(gradient, normed, factor))
        low_hiddens.append(both_cores(grad_hiddens[j].astype(BF)))
        return low_hiddens[j]

    def attention_back(j, operand, extra):
        first = jax.ShapeDtypeStruct((span, wide), F32)
        shapes = [jax.ShapeDtypeStruct((span, wide), BF), first, first]
        if j == 1:
            shapes = [jax.ShapeDtypeStruct((span, n * wide), BF) for n in (2, 3)]
        return in_vmem(
            attention_back_kernel,
            "attention_back",
            shapes,
            [
                *operand,
                out_own,
                out_got,
                *tables[j],
                spot_cols[j],
                spot_rows[j],
                logsums[j],
                query_heads[j],
                key_heads[j],
                value_heads[j],
                *extra,
            ],
        )

    def joined(pair):
        return pair[0] + swap(pair[1]).astype(F32)

    part_a = joined(attention(0, first_norm(0, blocks[0])))
    operand = first_norm(1, blocks[1])
    operand, part_a, low, token_total, core, slices = tie(
        (operand, part_a, part_a.astype(BF), token_total, 1 - row, slices)
    )
    got_a = from_chips(low)
    token_total = hop(token_total, *token_hops[0])
    pair = attention(1, operand)
    received = (
        swap(slices[0]),
        swap(slices[1]),
        swap(take(down_weight, core, units, 0)),
    )
    pair, got_a, token_total, received = tie((pair, got_a, token_total, received))
    part_b = joined(pair)
    two_a = second_norm(0, part_a, got_a)
    two_a, part_b, low, mine, token_total = tie(
        (two_a, part_b, part_b.astype(BF), two_a[0], token_total)
    )
    token_total = hop(token_total, *token_hops[1])
    got_b, cross_two_a = from_chips(low), cross(mine)
    raw = forward(two_a, received)
    raw, got_b, cross_two_a, token_total = tie((raw, got_b, cross_two_a, token_total))
    part_a, targets_a = after_forward(0, raw)
    two_b = second_norm(1, part_b, got_b)
    two_b, part_a, low, mine, token_total = tie(
        (two_b, part_a, part_a.astype(BF), two_b[0], token_total)
    )
    for step in token_hops[2:]:
        token_total = hop(token_total, *step)
    got_a, cross_two_b = from_chips(low), cross(mine)
    raw = forward(two_b, received)
    raw, got_a, cross_two_b, token_total = tie((raw, got_a, cross_two_b, token_total))
    scale = (rows * lax.axis_size("dp")) / token_total
    part_b, targets_b = after_forward(1, raw)
    low_a = loss_of(0, part_a, got_a, targets_a)
    low_a, part_b, low, mine = tie((low_a, part_b, part_b.astype(BF), act_gives[0]))
    got_b, cross_act_a = from_chips(low), cross(mine)
    raw = backward(0, low_a, received)
    raw, got_b, cross_act_a = tie((raw, got_b, cross_act_a))
    ups_a, part_a = raw[:4], joined(raw[4:])
    low_b = loss_of(1, part_b, got_b, targets_b)
    low_b, part_a, low, mine, error_sum = tie(
        (
            low_b,
            part_a,
            part_a.astype(BF),
            act_gives[1],
            (errors[0] + errors[1]).reshape(1, 1),
        )
    )
    error_sum = hop(error_sum, *hops[0])
    got_a, cross_act_b = from_chips(low), cross(mine)
    raw = backward(1, low_b, received)
    raw, got_a, cross_act_b, error_sum = tie((raw, got_a, cross_act_b, error_sum))
    ups_b, part_b = raw[:4], joined(raw[4:])
    hidden_a = second_norm_back(0, part_a, got_a)
    hidden_a, part_b, low, mine = tie((hidden_a, part_b, part_b.astype(BF), low_a[0]))
    error_sum = hop(error_sum, *hops[1])
    got_b, cross_low_a = from_chips(low), cross(mine)
    parts = attention_back(0, hidden_a, [])
    parts, got_b, cross_low_a, error_sum = tie((parts, got_b, cross_low_a, error_sum))
    hidden_b = second_norm_back(1, part_b, got_b)
    hidden_b, parts, mine, error_sum = tie((hidden_b, parts, low_b[0], error_sum))
    error_sum = hop(error_sum, *hops[2])
    cross_low_b = cross(mine)
    first_back, back_b = attention_back(
        1, hidden_b, [key_heads[0], value_heads[0], *tables[0], *parts[1:]]
    )
    first_back, back_b, cross_low_b, error_sum = tie(
        (first_back, back_b, cross_low_b, error_sum)
    )
    backs = [jnp.concatenate([parts[0], first_back], axis=1), back_b]
    gate_gives = [u[1] for u in (ups_a, ups_b)]
    up_gives = [u[3] for u in (ups_a, ups_b)]

    def split_rows(full):
        half = full.shape[0] // 2
        return full[:half], swap(full[half:])

    def split_cols(full):
        half = full.shape[1] // 2
        return full[:, :half], swap(full[:, half:])

    def together(lefts, rights):
        return jnp.concatenate(lefts, axis=0), jnp.concatenate(rights, axis=0)

    def product(lefts, rights):
        return contract_rows(lefts, rights).astype(BF)

    hiddens = together(attended, [*hidden_a, *hidden_b])
    firsts = together(low_first, backs)
    backs, mine, gate_gives = tie((backs, gate_gives[0], gate_gives))
    cross_gate_a = cross(mine)
    for step in hops[3:]:
        error_sum = hop(error_sum, *step)
    ends = [jax.ShapeDtypeStruct((own, 2 * half_width), t) for t in (F32, BF)]
    raw = in_vmem(last_kernel, "first_norm_back", ends * 2, [*backs, qkv_own, qkv_got])
    raw, cross_gate_a, error_sum = tie((raw, cross_gate_a, error_sum))
    last_parts = [joined(raw[:2]), joined(raw[2:])]
    downs = together(
        [*acts, cross_act_a, cross_act_b], [*low_a, *low_b, *from_cores(cross_low_a, cross_low_b)]
    )
    downs, mine = tie((downs, gate_gives[1]))
    cross_gate_b = cross(mine)
    grad_down = product(*downs)
    grad_down, cross_gate_b, up_gives = tie((grad_down, cross_gate_b, up_gives))
    down_pair = split_cols(grad_down)
    cross_up_a = cross(up_gives[0])
    grad_qkv = product(*firsts)
    grad_qkv, cross_up_a, up_gives, hiddens = tie((grad_qkv, cross_up_a, up_gives, hiddens))
    qkv_pair = split_rows(grad_qkv)
    out_pair = split_cols(product(*hiddens))
    twos = [*two_a, *two_b, *from_cores(cross_two_a, cross_two_b)]
    gates = together(twos, [ups_a[0], ups_b[0], cross_gate_a, cross_gate_b])
    gates, mine, qkv_pair, out_pair = tie((gates, up_gives[1], qkv_pair, out_pair))
    cross_up_b = cross(mine)
    grad_gate = product(*gates)
    grad_gate, cross_up_b = tie((grad_gate, cross_up_b))
    gate_pair = split_rows(grad_gate)
    up_pair = split_rows(
        product(*together(twos, [ups_a[2], ups_b[2], cross_up_a, cross_up_b]))
    )

    def halves(pair, which):
        three = [
            ordered(
                first_row,
                *(take(p[:, i * wide : (i + 1) * wide], which, part_wide, 1) for p in pair),
                1,
            )
            for i in range(3)
        ]
        return [pack(jnp.concatenate(three[:2], axis=1), half_width), pack(three[2], half_width)]

    pieces, spots, starts = [], [], []
    total = 0
    out_mine = [take(p, side, part_wide, 0) for p in out_pair]
    out_give = [take(p, 1 - side, part_wide, 0) for p in out_pair]
    for pair in (down_pair, gate_pair, up_pair, out_mine):
        packed = [pack(p, half_width) for p in pair]
        size = packed[0].shape[0]
        pieces += packed
        spots += [
            lambda r, total=total, size=size: total + r * size,
            lambda r, total=total, size=size: total + (1 - r) * size,
        ]
        starts.append((total, size))
        total += 2 * size
    for packed in halves(qkv_pair, side):
        size = packed.shape[0]
        pieces.append(packed)
        spots.append(lambda r, total=total: total + 0 * r)
        starts.append((total, size))
        total += size
    gives = [pack(p, half_width) for p in out_give] + halves(qkv_pair, 1 - side)
    last_gots = [from_chips(p) for p in last_parts]
    sums = line_sum(pieces, spots, gives, chunk=min(256, total // 8))
    sums, last_parts, last_gots = tie((sums, last_parts, last_gots))

    if cols == 2 and part_units == half_width:
        grad_down, grad_gate, grad_up = widen_three(
            sums, down_weight.shape, gate_weight.shape, half_width
        )
        grad_query, grad_key, grad_value, grad_output = widen_four(
            sums, query_weight.shape, [starts[n][0] for n in (4, 5, 3)], part_wide
        )
    else:

        def blocks_of(which, columns):
            start, size = starts[which]
            return [
                unpack(sums[x, start + s * size : start + (s + 1) * size], columns)
                for s in range(2)
                for x in range(2)
            ]

        grad_down = jnp.concatenate(blocks_of(0, half_width), axis=0).astype(F32)
        grad_gate = jnp.concatenate(blocks_of(1, part_units), axis=1).astype(F32)
        grad_up = jnp.concatenate(blocks_of(2, part_units), axis=1).astype(F32)
        grad_output = jnp.concatenate(blocks_of(3, half_width), axis=0).astype(F32)
        three = [[], [], []]
        qk, v = (
            [unpack(sums[x, starts[n][0] : starts[n][0] + starts[n][1]], k * part_wide) for x in range(2)]
            for n, k in ((4, 4), (5, 2))
        )
        for s in range(2):
            for x in range(2):
                at = s * part_wide
                three[0].append(qk[x][:, at : at + part_wide])
                three[1].append(qk[x][:, 2 * part_wide + at : 2 * part_wide + at + part_wide])
                three[2].append(v[x][:, at : at + part_wide])
        grad_query, grad_key, grad_value = (
            jnp.concatenate(t, axis=1).astype(F32) for t in three
        )

    grad_tokens = []
    for j in range(2):
        gradient = last_parts[j] + last_gots[j].astype(F32)
        average, factor = first_stats[j]
        normed = (inputs[j].astype(F32) - average) * factor
        grads = grad_hiddens[j] + normalize_back(gradient, normed, factor)
        near = take(grads[:, :half_width], col, block, 1)
        far = take(grads[:, half_width:], col, block, 1)
        grad_tokens.append(ordered(first_row, near, swap(far), 0))
    loss_value = (error_sum / token_total)[0, 0]
    return (
        jnp.concatenate(outputs, axis=0),
        loss_value,
        jnp.concatenate(grad_tokens, axis=0),
        grad_query,
        grad_key,
        grad_value,
        grad_output,
        grad_gate,
        grad_up,
        grad_down,
    )


def solution(mesh):
    features = P("dp", ("row", "col"))
    into, back = P("row", "col"), P("col", "row")
    in_specs = (features, features, P("dp"), P("dp"), into, into, into, back, into, into, back)
    out_specs = (features, P(), features, into, into, into, back, into, into, back)
    return jax.shard_map(body, mesh=mesh, in_specs=in_specs, out_specs=out_specs, check_vma=False)
```

```python
import functools
import math

import jax
import jax.numpy as jnp
from jax import lax
from jax.experimental import pallas as pl
from jax.experimental.pallas import tpu as pltpu
from jax.sharding import PartitionSpec as P

D = 2048
HEAD = 128
LEN = 1024
EPS = 1e-05
THETA = 10000.0
NEG = -1e30

BF = jnp.bfloat16
F32 = jnp.float32


def rope_tables(places):
    half_width = HEAD // 2
    frequency = jnp.exp(
        jnp.arange(half_width).astype(F32) * (-2.0 * math.log(THETA) / HEAD)
    )
    angles = places.astype(F32)[:, None] * frequency[None, :]
    cosine, sine_table = jnp.cos(angles), jnp.sin(angles)
    return (
        jnp.concatenate([cosine, cosine], axis=1),
        jnp.concatenate([-sine_table, sine_table], axis=1),
    )


def dot(left, right):
    return jnp.dot(left, right, preferred_element_type=F32)


def contract_rows(left, right):
    return lax.dot_general(left, right, (((0,), (0,)), ((), ())), preferred_element_type=F32)


def contract_cols(left, right):
    return lax.dot_general(left, right, (((1,), (1,)), ((), ())), preferred_element_type=F32)


def take(operand, index, size, axis):
    return lax.dynamic_slice_in_dim(operand, index * size, size, axis)


def swap_halves(operand, axis):
    half = operand.shape[axis] // 2
    return jnp.concatenate(
        [
            lax.slice_in_dim(operand, half, 2 * half, axis=axis),
            lax.slice_in_dim(operand, 0, half, axis=axis),
        ],
        axis=axis,
    )


def ordered(first, mine, other, axis):
    return jnp.concatenate(
        [jnp.where(first, mine, other), jnp.where(first, other, mine)], axis=axis
    )


def add_low(left, right):
    return (left.astype(F32) + right.astype(F32)).astype(BF)


MESH = pl.DeviceIdType.MESH


def line_kernel(sizes, spots, given, chunk, lag, ahead, deep, *refs):
    count = len(sizes)
    pieces, gives = refs[:count], refs[count : count + given]
    out = refs[count + given]
    held, got_in, got_mid, got_give, load, send_in, send_mid, send_out, send_side, in_sem, mid_sem, out_sem, side_sem, keep, send_give, give_sem = refs[count + given + 1:]
    places = lax.axis_size("dp") // 2
    dp = lax.axis_index("dp")
    row = lax.axis_index("row")
    col = lax.axis_index("col")
    place, side = dp // 2, dp % 2
    half = places // 2
    low = place < half
    depth = jnp.where(low, place, places - 1 - place)
    is_mid = depth == half - 1
    is_end = depth == 0
    to_in = jnp.where(low, place + 1, place - 1)
    to_out = jnp.where(low, place - 1, place + 1)
    inner = (to_in * 2 + side, row, col)
    outer = (jnp.clip(to_out, 0, places - 1) * 2 + side, row, col)
    other = (dp + 1 - 2 * side, row, col)
    total_rows = held.shape[0]
    steps = total_rows // chunk
    base = total_rows - sum(sizes[count - given :])
    first = base // chunk

    loads = []
    for i in range(count):
        rows = sizes[i]
        at = pl.multiple_of(spots[i](row), 16)
        loads.append(pltpu.make_async_copy(pieces[i], held.at[pl.ds(at, rows)], load.at[i]))
        loads[-1].start()

    barrier = pltpu.get_barrier_semaphore()
    pl.semaphore_signal(barrier, inc=1, device_id=inner, device_id_type=MESH)
    pl.semaphore_signal(barrier, inc=1, device_id=other, device_id_type=MESH)

    @pl.when(jnp.logical_not(is_end))
    def _():
        pl.semaphore_signal(barrier, inc=1, device_id=outer, device_id_type=MESH)
        pl.semaphore_wait(barrier, 3)

    @pl.when(is_end)
    def _():
        pl.semaphore_wait(barrier, 2)

    given_copies = []
    for i in range(given):
        spot = pl.multiple_of(spots[count - given + i](row) - base, 16)
        given_copies.append(
            pltpu.make_async_remote_copy(
                src_ref=gives[i], dst_ref=got_give.at[pl.ds(spot, sizes[count - given + i])],
                send_sem=send_give.at[i], recv_sem=give_sem.at[i],
                device_id=other, device_id_type=MESH))
        given_copies[-1].start()
    for copy in loads:
        copy.wait()

    def add_given(t):
        @pl.when(t == first)
        def _():
            for copy in given_copies:
                copy.wait()

        @pl.when(t >= first)
        def _():
            held[at(t)] = (
                held[at(t)].astype(F32) + got_give[at(t - first)].astype(F32)
            ).astype(BF)

    def at(t):
        return pl.ds(pl.multiple_of(t * chunk, chunk), chunk)

    def inward(t):
        return pltpu.make_async_remote_copy(
            src_ref=held.at[at(t)], dst_ref=got_in.at[at(t)], send_sem=send_in.at[t],
            recv_sem=in_sem.at[t], device_id=inner, device_id_type=MESH)

    def middle(t):
        return pltpu.make_async_remote_copy(
            src_ref=held.at[at(t)], dst_ref=got_mid.at[at(t)], send_sem=send_mid.at[t],
            recv_sem=mid_sem.at[t], device_id=inner, device_id_type=MESH)

    def outward(t, source):
        return pltpu.make_async_remote_copy(
            src_ref=source, dst_ref=out.at[side, at(t)], send_sem=send_out.at[t],
            recv_sem=out_sem.at[t], device_id=outer, device_id_type=MESH)

    def across(t, source):
        return pltpu.make_async_remote_copy(
            src_ref=source, dst_ref=out.at[side, at(t)], send_sem=send_side.at[t],
            recv_sem=side_sem.at[t], device_id=other, device_id_type=MESH)

    def store(t):
        return pltpu.make_async_copy(got_in.at[at(t)], out.at[side, at(t)], keep.at[t])

    def mid_loop(t, _):
        @pl.when(t < steps)
        def _():
            add_given(t)

            @pl.when(jnp.logical_not(is_end))
            def _():
                inward(t).wait_recv()
                held[at(t)] = (held[at(t)].astype(F32) + got_in[at(t)].astype(F32)).astype(BF)
            @pl.when(t >= deep)
            def _():
                middle(t - deep).wait_send()
            middle(t).start()

        @pl.when(t >= ahead)
        def _():
            u = t - ahead
            middle(u).wait_recv()
            got_in[at(u)] = (held[at(u)].astype(F32) + got_mid[at(u)].astype(F32)).astype(BF)
            store(u).start()
            @pl.when(u >= deep)
            def _():
                @pl.when(jnp.logical_not(is_end))
                def _():
                    outward(u - deep, got_in.at[at(u)]).wait_send()
                across(u - deep, got_in.at[at(u)]).wait_send()
            @pl.when(jnp.logical_not(is_end))
            def _():
                outward(u, got_in.at[at(u)]).start()
            across(u, got_in.at[at(u)]).start()
        return 0

    def far_loop(t, _):
        @pl.when(t < steps)
        def _():
            add_given(t)

            @pl.when(jnp.logical_not(is_end))
            def _():
                inward(t).wait_recv()
                held[at(t)] = (held[at(t)].astype(F32) + got_in[at(t)].astype(F32)).astype(BF)
            @pl.when(t >= deep)
            def _():
                inward(t - deep).wait_send()
            inward(t).start()

        @pl.when(t >= lag)
        def _():
            u = t - lag
            outward(u, out.at[side, at(u)]).wait_recv()
            @pl.when(u >= deep)
            def _():
                @pl.when(jnp.logical_not(is_end))
                def _():
                    outward(u - deep, out.at[side, at(u)]).wait_send()
                across(u - deep, out.at[side, at(u)]).wait_send()
            @pl.when(jnp.logical_not(is_end))
            def _():
                outward(u, out.at[side, at(u)]).start()
            across(u, out.at[side, at(u)]).start()
        return 0

    @pl.when(is_mid)
    def _():
        lax.fori_loop(0, steps + ahead, mid_loop, 0)
        def finish(t, _):
            store(t).wait()
            across(t, got_in.at[at(t)]).wait_recv()
            @pl.when(t >= steps - deep)
            def _():
                middle(t).wait_send()
                across(t, got_in.at[at(t)]).wait_send()
                @pl.when(jnp.logical_not(is_end))
                def _():
                    outward(t, got_in.at[at(t)]).wait_send()
            return 0
        lax.fori_loop(0, steps, finish, 0)

    @pl.when(jnp.logical_not(is_mid))
    def _():
        lax.fori_loop(0, steps + lag, far_loop, 0)
        def finish(t, _):
            across(t, out.at[side, at(t)]).wait_recv()
            @pl.when(t >= steps - deep)
            def _():
                inward(t).wait_send()
                across(t, out.at[side, at(t)]).wait_send()
                @pl.when(jnp.logical_not(is_end))
                def _():
                    outward(t, out.at[side, at(t)]).wait_send()
            return 0
        lax.fori_loop(0, steps, finish, 0)


def line_sum(pieces, spots, gives, chunk, lag=8, ahead=2, deep=2):
    sizes = [p.shape[0] for p in pieces]
    rows, width = sum(sizes), pieces[0].shape[1]
    steps = rows // chunk
    given_rows = sum(g.shape[0] for g in gives)
    dma = pltpu.SemaphoreType.DMA
    return pl.pallas_call(
        functools.partial(line_kernel, sizes, spots, len(gives), chunk, lag, ahead, deep),
        out_shape=jax.ShapeDtypeStruct((2, rows, width), BF),
        in_specs=[pl.BlockSpec(memory_space=pl.ANY)] * (len(pieces) + len(gives)),
        out_specs=pl.BlockSpec(memory_space=pl.ANY),
        scratch_shapes=[pltpu.VMEM((rows, width), BF)] * 3
        + [pltpu.VMEM((given_rows, width), BF)]
        + [dma((len(pieces),))]
        + [dma((steps,))] * 9
        + [dma((len(gives),))] * 2,
        compiler_params=pltpu.CompilerParams(
            collective_id=0, has_side_effects=True, vmem_limit_bytes=58 * 2**20
        ),
        name="line_sum",
    )(*pieces, *gives)


def pack(operand, width):
    rows, columns = operand.shape
    if columns == width:
        return operand
    if columns > width:
        return jnp.concatenate(
            [operand[:, i : i + width] for i in range(0, columns, width)], axis=0
        )
    times = width // columns
    step = rows // times
    return jnp.concatenate([operand[i * step : (i + 1) * step] for i in range(times)], axis=1)


def unpack(operand, columns):
    rows, width = operand.shape
    if columns == width:
        return operand
    if columns > width:
        step = rows * width // columns
        return jnp.concatenate(
            [operand[i * step : (i + 1) * step] for i in range(columns // width)], axis=1
        )
    return jnp.concatenate(
        [operand[:, i : i + columns] for i in range(0, width, columns)], axis=0
    )


def hop(operand, axis, step):
    size = lax.axis_size(axis)
    return operand + lax.ppermute(operand, axis, [(i, i ^ step) for i in range(size)])


def turned(operand, cosine, sine_table):
    return operand * cosine + pltpu.roll(operand, HEAD // 2, 1) * sine_table


def allowed_pairs(spot_col, spot_row):
    return (spot_col[:, 0:1] == spot_row[0:1, :]) & (spot_row[1:2, :] <= spot_col[:, 1:2])


def attention_kernel(
    x_ref, own_ref, got_ref, out_own, out_got, cos_ref, sin_ref, col_ref, row_ref, *refs
):
    earlier, (q_out, k_out, v_out, att_out, lse_out, kept, sent) = refs[:-7], refs[-7:]
    half = x_ref.shape[1] // 2
    wide = out_own.shape[0]
    own = kept.shape[0]
    near, far = x_ref[:, :half], x_ref[:, half:]
    cosine, sine_table = cos_ref[...], sin_ref[...]
    for which, out in enumerate((q_out, k_out, v_out)):
        at = slice(which * wide, (which + 1) * wide)
        raw = dot(near, own_ref[:, at]) + dot(far, got_ref[:, at])
        for h in range(wide // HEAD):
            head = slice(h * HEAD, (h + 1) * HEAD)
            value = raw[:, head]
            if which < 2:
                value = turned(value, cosine, sine_table)
            out[:, head] = value.astype(BF)
    allowed = allowed_pairs(col_ref[...], row_ref[...])
    for h in range(wide // HEAD):
        head = slice(h * HEAD, (h + 1) * HEAD)
        keys, values = k_out[:, head], v_out[:, head]
        if earlier:
            keys = jnp.concatenate([earlier[0][:, head], keys], axis=0)
            values = jnp.concatenate([earlier[1][:, head], values], axis=0)
        scores = contract_cols(q_out[:, head], keys) * (1.0 / math.sqrt(HEAD))
        scores = jnp.where(allowed, scores, NEG)
        row_max = jnp.max(scores, axis=-1, keepdims=True)
        shares = jnp.exp(scores - row_max)
        totals = jnp.sum(shares, axis=-1, keepdims=True)
        shares = (shares / totals).astype(BF)
        att_out[:, head] = dot(shares, values).astype(BF)
        lse_out[:, head] = jnp.broadcast_to(row_max + jnp.log(totals), (2 * own, HEAD))
    near, far = dot(att_out[...], out_own[...]), dot(att_out[...], out_got[...])
    kept[:, :half] = near[:own]
    kept[:, half:] = far[:own]
    sent[:, :half] = far[own:].astype(BF)
    sent[:, half:] = near[own:].astype(BF)


def attention_back_kernel(
    own_rows, other_rows, out_own, out_got, cos_ref, sin_ref, col_ref, row_ref,
    lse_ref, q_ref, k_ref, v_ref, *refs
):
    span, wide = q_ref.shape
    g_ref = jnp.concatenate([own_rows[...], other_rows[...]], axis=0)
    half = g_ref.shape[1] // 2
    factor = 1.0 / math.sqrt(HEAD)
    cosine, sine_table = cos_ref[...], -sin_ref[...]
    grads = contract_cols(g_ref[:, :half], out_own[...])
    grads = (grads + contract_cols(g_ref[:, half:], out_got[...])).astype(BF)
    allowed = allowed_pairs(col_ref[...], row_ref[...])
    last = len(refs) > 3
    for h in range(wide // HEAD):
        head = slice(h * HEAD, (h + 1) * HEAD)
        queries, gradient = q_ref[:, head], grads[:, head]
        keys, values = k_ref[:, head], v_ref[:, head]
        if last:
            keys = jnp.concatenate([refs[0][:, head], keys], axis=0)
            values = jnp.concatenate([refs[1][:, head], values], axis=0)
        scores = jnp.where(allowed, contract_cols(queries, keys) * factor, NEG)
        shares = jnp.exp(scores - lse_ref[:, h * HEAD : h * HEAD + 1])
        grad_shares = contract_cols(gradient, values)
        centre = jnp.sum(shares * grad_shares, axis=-1, keepdims=True)
        grad_scores = (shares * (grad_shares - centre)).astype(BF)
        grad_q = turned(dot(grad_scores, keys) * factor, cosine, sine_table)
        grad_k = contract_rows(grad_scores, queries) * factor
        grad_v = contract_rows(shares.astype(BF), gradient)
        if not last:
            q_out, k_out, v_out = refs
            q_out[:, head] = grad_q.astype(BF)
            k_out[:, head] = grad_k
            v_out[:, head] = grad_v
        else:
            cos_first, sin_first, k_part, v_part, first_out, back_out = refs[2:]
            back_out[:, head] = grad_q.astype(BF)
            at = slice(wide + h * HEAD, wide + (h + 1) * HEAD)
            back_out[:, at] = turned(grad_k[span:], cosine, sine_table).astype(BF)
            first = grad_k[:span] + k_part[:, head]
            first_out[:, head] = turned(first, cos_first[...], -sin_first[...]).astype(BF)
            at = slice(2 * wide + h * HEAD, 2 * wide + (h + 1) * HEAD)
            back_out[:, at] = grad_v[span:].astype(BF)
            at = slice(wide + h * HEAD, wide + (h + 1) * HEAD)
            first_out[:, at] = (grad_v[:span] + v_part[:, head]).astype(BF)


def last_kernel(a_ref, b_ref, own_ref, got_ref, kept_a, sent_a, kept_b, sent_b):
    half = own_ref.shape[0]
    own = kept_a.shape[0]
    for ref, kept, sent in ((a_ref, kept_a, sent_a), (b_ref, kept_b, sent_b)):
        near, far = contract_cols(ref[...], own_ref[...]), contract_cols(ref[...], got_ref[...])
        kept[:, :half] = near[:own]
        kept[:, half:] = far[:own]
        sent[:, :half] = far[own:].astype(BF)
        sent[:, half:] = near[own:].astype(BF)


def in_vmem(kernel, name, out_shape, operands, flops=8 * 10**9):
    return pl.pallas_call(
        kernel,
        out_shape=out_shape,
        in_specs=[pl.BlockSpec(memory_space=pltpu.VMEM)] * len(operands),
        out_specs=[pl.BlockSpec(memory_space=pltpu.VMEM)] * len(out_shape),
        compiler_params=pltpu.CompilerParams(vmem_limit_bytes=52 * 2**20),
        cost_estimate=pl.CostEstimate(
            flops=flops, bytes_accessed=flops // 400, transcendentals=flops // 4000
        ),
        name=name,
    )(*operands)


def moments(operand):
    average = jnp.mean(operand, axis=-1, keepdims=True)
    centre = operand - average
    factor = lax.rsqrt(jnp.mean(centre * centre, axis=-1, keepdims=True) + EPS)
    return average, factor


def normalize_back(gradient, normed, factor):
    mean = jnp.mean(gradient, axis=-1, keepdims=True)
    crossed = jnp.mean(gradient * normed, axis=-1, keepdims=True)
    return factor * (gradient - mean - normed * crossed)


def feed_forward_kernel(
    r_ref, own_rows, other_rows, gate_own, gate_got, up_own, up_got, down_own, down_got,
    gate_out, up_out, act_keep, act_give, kept, sent, total, x_ref, *, side_steps,
):
    step, last = pl.program_id(0), pl.num_programs(0) - 1
    half = x_ref.shape[1] // 2
    own = kept.shape[0]

    @pl.when(step == 0)
    def _():
        x_ref[:own] = own_rows[...]
        x_ref[own:] = other_rows[...]

    near, far = x_ref[:, :half], x_ref[:, half:]
    gate = dot(near, gate_own[...]) + dot(far, gate_got[...])
    up = dot(near, up_own[...]) + dot(far, up_got[...])
    gate_out[...] = gate
    up_out[...] = up
    act = (gate * jax.nn.sigmoid(gate) * up).astype(BF)
    mine = step // side_steps == r_ref[1]

    @pl.when(mine)
    def _():
        act_keep[...] = act

    @pl.when(jnp.logical_not(mine))
    def _():
        act_give[...] = act

    near, far = dot(act, down_own[...]), dot(act, down_got[...])

    @pl.when(step == 0)
    def _():
        total[:, :half] = near
        total[:, half:] = far

    @pl.when(step > 0)
    def _():
        total[:, :half] += near
        total[:, half:] += far

    @pl.when(step == last)
    def _():
        kept[...] = total[:own]
        sent[:, :half] = total[own:, half:].astype(BF)
        sent[:, half:] = total[own:, :half].astype(BF)


def feed_forward_back_kernel(
    r_ref, own_rows, other_rows, gate_ref, up_ref,
    gate_own, gate_got, up_own, up_got, down_own, down_got,
    gate_keep, gate_give, up_keep, up_give, kept, sent, total, g_ref, *, side_steps,
):
    step, last = pl.program_id(0), pl.num_programs(0) - 1
    half = g_ref.shape[1] // 2
    own = kept.shape[0]

    @pl.when(step == 0)
    def _():
        g_ref[:own] = own_rows[...]
        g_ref[own:] = other_rows[...]

    grad = contract_cols(g_ref[:, :half], down_own[...]) + contract_cols(
        g_ref[:, half:], down_got[...]
    )
    gate, up = gate_ref[...], up_ref[...]
    sigmoid = jax.nn.sigmoid(gate)
    gate_back = (grad * up * sigmoid * (1.0 + gate * (1.0 - sigmoid))).astype(BF)
    up_back = (grad * gate * sigmoid).astype(BF)
    mine = step // side_steps == r_ref[1]

    @pl.when(mine)
    def _():
        gate_keep[...] = gate_back
        up_keep[...] = up_back

    @pl.when(jnp.logical_not(mine))
    def _():
        gate_give[...] = gate_back
        up_give[...] = up_back

    near = contract_cols(gate_back, gate_own[...]) + contract_cols(up_back, up_own[...])
    far = contract_cols(gate_back, gate_got[...]) + contract_cols(up_back, up_got[...])

    @pl.when(step == 0)
    def _():
        total[:, :half] = near
        total[:, half:] = far

    @pl.when(step > 0)
    def _():
        total[:, :half] += near
        total[:, half:] += far

    @pl.when(step == last)
    def _():
        kept[...] = total[:own]
        sent[:, :half] = total[own:, half:].astype(BF)
        sent[:, half:] = total[own:, :half].astype(BF)


def feed_forward(back, where, operand, saved, weights, got, units, tile):
    own, width = operand[0].shape
    half, span, steps = width // 2, 2 * own, units // tile
    side_steps = steps // 2
    gate, up, down = weights
    gate_got, up_got, down_got = got

    def mine(i, r):
        return (0, jnp.clip(i - r[1] * side_steps, 0, side_steps - 1))

    def other(i, r):
        return (0, jnp.clip(i - (1 - r[1]) * side_steps, 0, side_steps - 1))

    whole = pl.BlockSpec((own, width), lambda i, r: (0, 0))
    wide = pl.BlockSpec((span, tile), lambda i, r: (0, i))
    into_own = pl.BlockSpec((half, tile), lambda i, r: (0, r[0] * steps + i))
    into_got = pl.BlockSpec((half, tile), lambda i, r: (0, i))
    back_own = pl.BlockSpec((tile, half), lambda i, r: (r[0] * steps + i, 0))
    back_got = pl.BlockSpec((tile, half), lambda i, r: (i, 0))
    weight_specs = [into_own, into_got, into_own, into_got, back_own, back_got]
    keep, give = pl.BlockSpec((span, tile), mine), pl.BlockSpec((span, tile), other)
    ends = [pl.BlockSpec((own, width), lambda i, r: (0, 0))] * 2
    part = jax.ShapeDtypeStruct((span, units // 2), BF)
    full = jax.ShapeDtypeStruct((span, units), F32)
    end_shapes = [
        jax.ShapeDtypeStruct((own, width), F32),
        jax.ShapeDtypeStruct((own, width), BF),
    ]
    if back:
        kernel = feed_forward_back_kernel
        in_specs = [whole, whole, wide, wide] + weight_specs
        out_specs = [keep, give, keep, give] + ends
        out_shape = [part] * 4 + end_shapes
    else:
        kernel = feed_forward_kernel
        in_specs = [whole, whole] + weight_specs
        out_specs = [wide, wide, keep, give] + ends
        out_shape = [full] * 2 + [part] * 2 + end_shapes
    return pl.pallas_call(
        functools.partial(kernel, side_steps=side_steps),
        out_shape=out_shape,
        grid_spec=pltpu.PrefetchScalarGridSpec(
            num_scalar_prefetch=1,
            grid=(steps,),
            in_specs=in_specs,
            out_specs=out_specs,
            scratch_shapes=[pltpu.VMEM((span, width), F32), pltpu.VMEM((span, width), BF)],
        ),
        compiler_params=pltpu.CompilerParams(vmem_limit_bytes=52 * 2**20),
        cost_estimate=pl.CostEstimate(
            flops=6 * span * width * units,
            bytes_accessed=6 * width * units + 12 * span * units,
            transcendentals=span * units,
        ),
        name="feed_forward_back" if back else "feed_forward",
    )(where, *operand, *saved, gate, gate_got, up, up_got, down, down_got)


def widen_three(sums, down_shape, into_shape, size):
    def kernel(in_ref, *outs):
        for n, out in enumerate(outs):

            @pl.when(pl.program_id(0) // 4 == n)
            def _():
                out[...] = in_ref[0].astype(F32)

    def spot(n):
        if n == 0:
            return lambda t: (jnp.clip(t, 0, 3), 0)
        return lambda t: (0, jnp.clip(t - 4 * n, 0, 3))

    return pl.pallas_call(
        kernel,
        out_shape=[jax.ShapeDtypeStruct(x, F32) for x in (down_shape, into_shape, into_shape)],
        grid=(12,),
        in_specs=[pl.BlockSpec((1, size, size), lambda t: (t % 2, t // 2, 0))],
        out_specs=[pl.BlockSpec((size, size), spot(n)) for n in range(3)],
        compiler_params=pltpu.CompilerParams(vmem_limit_bytes=48 * 2**20),
        name="widen_three",
    )(sums)


def widen_four(sums, shape, starts, part):
    rows, columns = shape
    qk, v, o = (start // part for start in starts)

    def kernel(qk_a, qk_b, v_a, v_b, o_ref, q_out, k_out, v_out, o_out):
        step = pl.program_id(0)
        o_out[...] = o_ref[0].astype(F32)
        for core in range(2):
            for pair, out, at in ((0, q_out, 0), (1, k_out, 2)):
                for x, ref in enumerate((qk_a, qk_b)):
                    spot = (2 * core + x) * part
                    source = (at + core) * part
                    out[:, spot : spot + part] = ref[0, :, source : source + part].astype(F32)
        for high in range(2):

            @pl.when(step // 2 == high)
            def _():
                for core in range(2):
                    for x, ref in enumerate((v_a, v_b)):
                        spot = (2 * core + x) * part
                        source = (2 * high + core) * part
                        v_out[:, spot : spot + part] = ref[0, :, source : source + part].astype(F32)

    block = (1, part, columns)
    return pl.pallas_call(
        kernel,
        out_shape=[jax.ShapeDtypeStruct(shape, F32)] * 4,
        grid=(rows // part,),
        in_specs=[
            pl.BlockSpec(block, lambda i: (0, qk + i, 0)),
            pl.BlockSpec(block, lambda i: (1, qk + i, 0)),
            pl.BlockSpec(block, lambda i: (0, v + i % 2, 0)),
            pl.BlockSpec(block, lambda i: (1, v + i % 2, 0)),
            pl.BlockSpec(block, lambda i: (i % 2, o + i // 2, 0)),
        ],
        out_specs=[pl.BlockSpec((part, columns), lambda i: (i, 0))] * 4,
        compiler_params=pltpu.CompilerParams(vmem_limit_bytes=32 * 2**20),
        name="widen_four",
    )(sums, sums, sums, sums, sums)


def body(
    tokens,
    teacher,
    segments,
    valid_mask,
    query_weight,
    key_weight,
    value_weight,
    output_weight,
    gate_weight,
    up_weight,
    down_weight,
):
    rows = tokens.shape[0]
    cols = lax.axis_size("col")
    row = lax.axis_index("row")
    col = lax.axis_index("col")
    side = lax.axis_index("dp") % 2
    sides = [(i, i ^ 1) for i in range(lax.axis_size("dp"))]
    block = tokens.shape[1]
    half_width = block * cols
    wide = query_weight.shape[1] // 2
    units = gate_weight.shape[1] // 2
    part_units = units // 2
    part_wide = wide // 2
    tile = min(512, part_units)
    span = rows // 2
    own = span // 2
    first_row = row == 0
    where = jnp.stack([row, side]).astype(jnp.int32)
    tie = lax.optimization_barrier

    def swap(operand):
        return lax.ppermute(operand, "row", [(0, 1), (1, 0)])

    def cross(operand):
        return lax.ppermute(operand, "dp", sides)

    def gather_blocks(operand):
        if cols == 2:
            got = lax.ppermute(operand, "col", [(0, 1), (1, 0)])
            return ordered(col == 0, operand, got, 1)
        return lax.all_gather(operand, "col", axis=1, tiled=True)

    def from_chips(sent):
        if cols == 2:
            return lax.ppermute(sent.astype(BF), "col", [(0, 1), (1, 0)])
        sent = sent.astype(F32)
        return lax.psum(sent, "col") - sent

    def both_cores(kept):
        return [kept, swap(swap_halves(kept, 1))]

    def from_cores(first, second):
        other = swap(swap_halves(jnp.concatenate([first, second], axis=0), 1))
        return [first, other[:own], second, other[own:]]

    def sum_cores(near, far):
        sent = jnp.concatenate([far[own:], near[own:]], axis=1).astype(BF)
        return jnp.concatenate([near[:own], far[:own]], axis=1) + swap(sent).astype(F32)

    def local_order(vector):
        pieces = []
        for j in range(2):
            piece = vector[j * span : (j + 1) * span]
            pieces.append(ordered(first_row, piece[:own], piece[own:], 0))
        return pieces

    blocks = []
    for j in range(2):
        piece = tokens[j * span : (j + 1) * span]
        blocks.append(gather_blocks(ordered(first_row, piece[:own], piece[own:], 0)))

    targets = []
    for j in range(2):
        piece = teacher[j * span : (j + 1) * span]
        piece = ordered(first_row, piece[:own], piece[own:], 0)
        targets.append((piece[:own], swap(piece[own:])))
    slices = [take(w, 1 - row, units, 1) for w in (gate_weight, up_weight)]
    blocks[0], slices, targets = tie((blocks[0], slices, targets))

    def columns_of(core):
        return jnp.concatenate(
            [take(w, core, wide, 1) for w in (query_weight, key_weight, value_weight)], axis=1
        )

    qkv_own, qkv_got = columns_of(row), swap(columns_of(1 - row))
    out_own = take(output_weight, row, wide, 0)
    out_got = swap(take(output_weight, 1 - row, wide, 0))
    weights = (gate_weight, up_weight, down_weight)

    validity = valid_mask.astype(F32)
    token_total = jnp.sum(validity).reshape(1, 1)
    hops = [(axis, 1 << k) for axis in ("dp", "row", "col") for k in range(10)]
    hops = [(axis, step) for axis, step in hops if step < lax.axis_size(axis)]
    token_hops = [h for h in hops if h[0] == "dp"]
    segs = local_order(segments)
    places = local_order(jnp.arange(rows, dtype=jnp.int32))
    valids = [v[:own, None] for v in local_order(validity)]
    tables = [rope_tables(p) for p in places]
    spot_cols = [jnp.stack([g, p], axis=1) for g, p in zip(segs, places)]
    spot_rows = [
        jnp.stack([jnp.concatenate(segs[: j + 1]), jnp.concatenate(places[: j + 1])])
        for j in range(2)
    ]

    inputs, first_stats, low_first = [], [], []
    query_heads, key_heads, value_heads = [], [], []
    attended, logsums = [], []

    def first_norm(j, half):
        whole = jnp.concatenate([half, swap(swap_halves(half, 0))], axis=1)
        whole_f = whole.astype(F32)
        average, factor = moments(whole_f)
        inputs.append(whole[:own])
        first_stats.append((average[:own], factor[:own]))
        low_first.append(((whole_f - average) * factor).astype(BF))
        return low_first[j]

    def attention(j, operand):
        out = jax.ShapeDtypeStruct((span, wide), BF)
        q, k, v, heads, logsum, kept, sent = in_vmem(
            attention_kernel,
            "attention",
            [out] * 4
            + [
                jax.ShapeDtypeStruct((span, wide), F32),
                jax.ShapeDtypeStruct((own, 2 * half_width), F32),
                jax.ShapeDtypeStruct((own, 2 * half_width), BF),
            ],
            [operand, qkv_own, qkv_got, out_own, out_got, *tables[j], spot_cols[j], spot_rows[j]]
            + [x for pair in zip(key_heads, value_heads) for x in pair],
        )
        query_heads.append(q)
        key_heads.append(k)
        value_heads.append(v)
        attended.append(heads)
        logsums.append(logsum)
        return kept, sent

    hidden, second_stats, low_second = [], [], []

    def second_norm(j, part, got):
        hidden.append(inputs[j].astype(F32) + (part + got.astype(F32)))
        average, factor = moments(hidden[j])
        second_stats.append((average, factor))
        low_second.append(both_cores(((hidden[j] - average) * factor).astype(BF)))
        return low_second[j]

    saved, acts, act_gives = [], [], []

    def forward(operand, received):
        return feed_forward(False, where, operand, (), weights, received, units, tile)

    def after_forward(j, raw):
        gate_out, up_out, act_keep, act_give, kept, sent = raw
        saved.append((gate_out, up_out))
        acts.append(act_keep)
        act_gives.append(act_give)
        near, far = (t.astype(F32) for t in targets[j])
        minus = [jnp.where(col == b, near, 0.0) for b in range(cols)]
        minus += [jnp.where(col == b, far, 0.0) for b in range(cols)]
        part = kept + swap(sent).astype(F32) - jnp.concatenate(minus, axis=1)
        return part, (near, far)

    outputs, errors, grad_results, low_results = [], [], [], []

    def loss_of(j, part, got, targets):
        near, far = targets
        error = hidden[j] + (part + got.astype(F32))
        near_error = take(error[:, :half_width], col, block, 1)
        far_error = take(error[:, half_width:], col, block, 1)
        outputs.append(
            ordered(
                first_row,
                (near_error + near).astype(BF),
                swap((far_error + far).astype(BF)),
                0,
            )
        )
        errors.append(
            0.5 * jnp.sum(valids[j] * (near_error * near_error + far_error * far_error))
        )
        grad_results.append(scale * valids[j] * error)
        low_results.append(both_cores(grad_results[j].astype(BF)))
        return low_results[j]

    def backward(j, operand, received):
        return feed_forward(True, where, operand, saved[j], weights, received, units, tile)

    grad_hiddens, low_hiddens = [], []

    def second_norm_back(j, part, got):
        gradient = part + got.astype(F32)
        average, factor = second_stats[j]
        normed = (hidden[j] - average) * factor
        grad_hiddens.append(grad_results[j] + normalize_back(gradient, normed, factor))
        low_hiddens.append(both_cores(grad_hiddens[j].astype(BF)))
        return low_hiddens[j]

    def attention_back(j, operand, extra):
        first = jax.ShapeDtypeStruct((span, wide), F32)
        shapes = [jax.ShapeDtypeStruct((span, wide), BF), first, first]
        if j == 1:
            shapes = [jax.ShapeDtypeStruct((span, n * wide), BF) for n in (2, 3)]
        return in_vmem(
            attention_back_kernel,
            "attention_back",
            shapes,
            [
                *operand,
                out_own,
                out_got,
                *tables[j],
                spot_cols[j],
                spot_rows[j],
                logsums[j],
                query_heads[j],
                key_heads[j],
                value_heads[j],
                *extra,
            ],
        )

    def joined(pair):
        return pair[0] + swap(pair[1]).astype(F32)

    part_a = joined(attention(0, first_norm(0, blocks[0])))
    operand = first_norm(1, blocks[1])
    operand, part_a, low, token_total, core, slices = tie(
        (operand, part_a, part_a.astype(BF), token_total, 1 - row, slices)
    )
    got_a = from_chips(low)
    token_total = hop(token_total, *token_hops[0])
    pair = attention(1, operand)
    received = (
        swap(slices[0]),
        swap(slices[1]),
        swap(take(down_weight, core, units, 0)),
    )
    pair, got_a, token_total, received = tie((pair, got_a, token_total, received))
    part_b = joined(pair)
    two_a = second_norm(0, part_a, got_a)
    two_a, part_b, low, mine, token_total = tie(
        (two_a, part_b, part_b.astype(BF), two_a[0], token_total)
    )
    token_total = hop(token_total, *token_hops[1])
    got_b, cross_two_a = from_chips(low), cross(mine)
    raw = forward(two_a, received)
    raw, got_b, cross_two_a, token_total = tie((raw, got_b, cross_two_a, token_total))
    part_a, targets_a = after_forward(0, raw)
    two_b = second_norm(1, part_b, got_b)
    two_b, part_a, low, mine, token_total = tie(
        (two_b, part_a, part_a.astype(BF), two_b[0], token_total)
    )
    for step in token_hops[2:]:
        token_total = hop(token_total, *step)
    got_a, cross_two_b = from_chips(low), cross(mine)
    raw = forward(two_b, received)
    raw, got_a, cross_two_b, token_total = tie((raw, got_a, cross_two_b, token_total))
    scale = (rows * lax.axis_size("dp")) / token_total
    part_b, targets_b = after_forward(1, raw)
    low_a = loss_of(0, part_a, got_a, targets_a)
    low_a, part_b, low, mine = tie((low_a, part_b, part_b.astype(BF), act_gives[0]))
    got_b, cross_act_a = from_chips(low), cross(mine)
    raw = backward(0, low_a, received)
    raw, got_b, cross_act_a = tie((raw, got_b, cross_act_a))
    ups_a, part_a = raw[:4], joined(raw[4:])
    low_b = loss_of(1, part_b, got_b, targets_b)
    low_b, part_a, low, mine, error_sum = tie(
        (
            low_b,
            part_a,
            part_a.astype(BF),
            act_gives[1],
            (errors[0] + errors[1]).reshape(1, 1),
        )
    )
    error_sum = hop(error_sum, *hops[0])
    got_a, cross_act_b = from_chips(low), cross(mine)
    raw = backward(1, low_b, received)
    raw, got_a, cross_act_b, error_sum = tie((raw, got_a, cross_act_b, error_sum))
    ups_b, part_b = raw[:4], joined(raw[4:])
    hidden_a = second_norm_back(0, part_a, got_a)
    hidden_a, part_b, low, mine = tie((hidden_a, part_b, part_b.astype(BF), low_a[0]))
    error_sum = hop(error_sum, *hops[1])
    got_b, cross_low_a = from_chips(low), cross(mine)
    parts = attention_back(0, hidden_a, [])
    parts, got_b, cross_low_a, error_sum = tie((parts, got_b, cross_low_a, error_sum))
    hidden_b = second_norm_back(1, part_b, got_b)
    hidden_b, parts, mine, error_sum = tie((hidden_b, parts, low_b[0], error_sum))
    error_sum = hop(error_sum, *hops[2])
    cross_low_b = cross(mine)
    first_back, back_b = attention_back(
        1, hidden_b, [key_heads[0], value_heads[0], *tables[0], *parts[1:]]
    )
    first_back, back_b, cross_low_b, error_sum = tie(
        (first_back, back_b, cross_low_b, error_sum)
    )
    backs = [jnp.concatenate([parts[0], first_back], axis=1), back_b]
    gate_gives = [u[1] for u in (ups_a, ups_b)]
    up_gives = [u[3] for u in (ups_a, ups_b)]

    def split_rows(full):
        half = full.shape[0] // 2
        return full[:half], swap(full[half:])

    def split_cols(full):
        half = full.shape[1] // 2
        return full[:, :half], swap(full[:, half:])

    def together(lefts, rights):
        return jnp.concatenate(lefts, axis=0), jnp.concatenate(rights, axis=0)

    def product(lefts, rights):
        return contract_rows(lefts, rights).astype(BF)

    hiddens = together(attended, [*hidden_a, *hidden_b])
    firsts = together(low_first, backs)
    downs = together(
        [*acts, cross_act_a, cross_act_b], [*low_a, *low_b, *from_cores(cross_low_a, cross_low_b)]
    )
    downs, gate_gives, error_sum = tie((downs, gate_gives, error_sum))
    cross_gate_a, cross_gate_b = (cross(g) for g in gate_gives)
    for step in hops[3:]:
        error_sum = hop(error_sum, *step)
    grad_down = product(*downs)
    grad_down, backs = tie((grad_down, backs))
    ends = [jax.ShapeDtypeStruct((own, 2 * half_width), t) for t in (F32, BF)]
    raw = in_vmem(
        last_kernel, "first_norm_back", ends * 2, [*backs, qkv_own, qkv_got], flops=4000
    )
    raw, grad_down, cross_gate_a, cross_gate_b, up_gives, error_sum = tie(
        (raw, grad_down, cross_gate_a, cross_gate_b, up_gives, error_sum)
    )
    last_parts = [joined(raw[:2]), joined(raw[2:])]
    down_pair = split_cols(grad_down)
    firsts, up_gives = tie((firsts, up_gives))
    cross_up_a, cross_up_b = (cross(g) for g in up_gives)
    grad_qkv = product(*firsts)
    grad_qkv, hiddens, twos = tie(
        (
            grad_qkv,
            hiddens,
            ([*two_a, *two_b], [cross_two_a, cross_two_b], [ups_a[0], ups_b[0]]),
        )
    )
    qkv_pair = split_rows(grad_qkv)
    out_pair = split_cols(product(*hiddens))
    gates = [*twos[2], cross_gate_a, cross_gate_b]
    twos = [*twos[0], *from_cores(*twos[1])]
    gates = together(twos, gates)
    gates, qkv_pair, out_pair, cross_up_a, cross_up_b = tie(
        (gates, qkv_pair, out_pair, cross_up_a, cross_up_b)
    )
    grad_gate = product(*gates)
    gate_pair = split_rows(grad_gate)
    up_pair = split_rows(
        product(*together(twos, [ups_a[2], ups_b[2], cross_up_a, cross_up_b]))
    )

    def halves(pair, which):
        three = [
            ordered(
                first_row,
                *(take(p[:, i * wide : (i + 1) * wide], which, part_wide, 1) for p in pair),
                1,
            )
            for i in range(3)
        ]
        return [pack(jnp.concatenate(three[:2], axis=1), half_width), pack(three[2], half_width)]

    pieces, spots, starts = [], [], []
    total = 0
    out_mine = [take(p, side, part_wide, 0) for p in out_pair]
    out_give = [take(p, 1 - side, part_wide, 0) for p in out_pair]
    for pair in (down_pair, gate_pair, up_pair, out_mine):
        packed = [pack(p, half_width) for p in pair]
        size = packed[0].shape[0]
        pieces += packed
        spots += [
            lambda r, total=total, size=size: total + r * size,
            lambda r, total=total, size=size: total + (1 - r) * size,
        ]
        starts.append((total, size))
        total += 2 * size
    for packed in halves(qkv_pair, side):
        size = packed.shape[0]
        pieces.append(packed)
        spots.append(lambda r, total=total: total + 0 * r)
        starts.append((total, size))
        total += size
    gives = [pack(p, half_width) for p in out_give] + halves(qkv_pair, 1 - side)
    last_gots = [from_chips(p) for p in last_parts]
    sums = line_sum(pieces, spots, gives, chunk=min(256, total // 8))
    sums, last_parts, last_gots = tie((sums, last_parts, last_gots))

    if cols == 2 and part_units == half_width:
        grad_down, grad_gate, grad_up = widen_three(
            sums, down_weight.shape, gate_weight.shape, half_width
        )
        grad_query, grad_key, grad_value, grad_output = widen_four(
            sums, query_weight.shape, [starts[n][0] for n in (4, 5, 3)], part_wide
        )
    else:

        def blocks_of(which, columns):
            start, size = starts[which]
            return [
                unpack(sums[x, start + s * size : start + (s + 1) * size], columns)
                for s in range(2)
                for x in range(2)
            ]

        grad_down = jnp.concatenate(blocks_of(0, half_width), axis=0).astype(F32)
        grad_gate = jnp.concatenate(blocks_of(1, part_units), axis=1).astype(F32)
        grad_up = jnp.concatenate(blocks_of(2, part_units), axis=1).astype(F32)
        grad_output = jnp.concatenate(blocks_of(3, half_width), axis=0).astype(F32)
        three = [[], [], []]
        qk, v = (
            [unpack(sums[x, starts[n][0] : starts[n][0] + starts[n][1]], k * part_wide) for x in range(2)]
            for n, k in ((4, 4), (5, 2))
        )
        for s in range(2):
            for x in range(2):
                at = s * part_wide
                three[0].append(qk[x][:, at : at + part_wide])
                three[1].append(qk[x][:, 2 * part_wide + at : 2 * part_wide + at + part_wide])
                three[2].append(v[x][:, at : at + part_wide])
        grad_query, grad_key, grad_value = (
            jnp.concatenate(t, axis=1).astype(F32) for t in three
        )

    grad_tokens = []
    for j in range(2):
        gradient = last_parts[j] + last_gots[j].astype(F32)
        average, factor = first_stats[j]
        normed = (inputs[j].astype(F32) - average) * factor
        grads = grad_hiddens[j] + normalize_back(gradient, normed, factor)
        near = take(grads[:, :half_width], col, block, 1)
        far = take(grads[:, half_width:], col, block, 1)
        grad_tokens.append(ordered(first_row, near, swap(far), 0))
    loss_value = (error_sum / token_total)[0, 0]
    return (
        jnp.concatenate(outputs, axis=0),
        loss_value,
        jnp.concatenate(grad_tokens, axis=0),
        grad_query,
        grad_key,
        grad_value,
        grad_output,
        grad_gate,
        grad_up,
        grad_down,
    )


def solution(mesh):
    features = P("dp", ("row", "col"))
    into, back = P("row", "col"), P("col", "row")
    in_specs = (features, features, P("dp"), P("dp"), into, into, into, back, into, into, back)
    out_specs = (features, P(), features, into, into, into, back, into, into, back)
    return jax.shard_map(body, mesh=mesh, in_specs=in_specs, out_specs=out_specs, check_vma=False)
```

```python
import functools
import math

import jax
import jax.numpy as jnp
from jax import lax
from jax.experimental import pallas as pl
from jax.experimental.pallas import tpu as pltpu
from jax.sharding import PartitionSpec as P

D = 2048
HEAD = 128
LEN = 1024
EPS = 1e-05
THETA = 10000.0
NEG = -1e30

BF = jnp.bfloat16
F32 = jnp.float32


def rope_tables(places):
    half_width = HEAD // 2
    frequency = jnp.exp(
        jnp.arange(half_width).astype(F32) * (-2.0 * math.log(THETA) / HEAD)
    )
    angles = places.astype(F32)[:, None] * frequency[None, :]
    cosine, sine_table = jnp.cos(angles), jnp.sin(angles)
    return (
        jnp.concatenate([cosine, cosine], axis=1),
        jnp.concatenate([-sine_table, sine_table], axis=1),
    )


def dot(left, right):
    return jnp.dot(left, right, preferred_element_type=F32)


def contract_rows(left, right):
    return lax.dot_general(left, right, (((0,), (0,)), ((), ())), preferred_element_type=F32)


def contract_cols(left, right):
    return lax.dot_general(left, right, (((1,), (1,)), ((), ())), preferred_element_type=F32)


def take(operand, index, size, axis):
    return lax.dynamic_slice_in_dim(operand, index * size, size, axis)


def swap_halves(operand, axis):
    half = operand.shape[axis] // 2
    return jnp.concatenate(
        [
            lax.slice_in_dim(operand, half, 2 * half, axis=axis),
            lax.slice_in_dim(operand, 0, half, axis=axis),
        ],
        axis=axis,
    )


def ordered(first, mine, other, axis):
    return jnp.concatenate(
        [jnp.where(first, mine, other), jnp.where(first, other, mine)], axis=axis
    )


def add_low(left, right):
    return (left.astype(F32) + right.astype(F32)).astype(BF)


MESH = pl.DeviceIdType.MESH


def line_kernel(sizes, spots, given, chunk, lag, ahead, deep, *refs):
    count = len(sizes)
    pieces, gives = refs[:count], refs[count : count + given]
    out = refs[count + given]
    held, got_in, got_mid, got_give, load, send_in, send_mid, send_out, send_side, in_sem, mid_sem, out_sem, side_sem, keep, send_give, give_sem = refs[count + given + 1:]
    places = lax.axis_size("dp") // 2
    dp = lax.axis_index("dp")
    row = lax.axis_index("row")
    col = lax.axis_index("col")
    place, side = dp // 2, dp % 2
    half = places // 2
    low = place < half
    depth = jnp.where(low, place, places - 1 - place)
    is_mid = depth == half - 1
    is_end = depth == 0
    to_in = jnp.where(low, place + 1, place - 1)
    to_out = jnp.where(low, place - 1, place + 1)
    inner = (to_in * 2 + side, row, col)
    outer = (jnp.clip(to_out, 0, places - 1) * 2 + side, row, col)
    other = (dp + 1 - 2 * side, row, col)
    total_rows = held.shape[0]
    steps = total_rows // chunk
    base = total_rows - sum(sizes[count - given :])
    first = base // chunk

    loads = []
    for i in range(count):
        rows = sizes[i]
        at = pl.multiple_of(spots[i](row), 16)
        loads.append(pltpu.make_async_copy(pieces[i], held.at[pl.ds(at, rows)], load.at[i]))
        loads[-1].start()

    barrier = pltpu.get_barrier_semaphore()
    pl.semaphore_signal(barrier, inc=1, device_id=inner, device_id_type=MESH)
    pl.semaphore_signal(barrier, inc=1, device_id=other, device_id_type=MESH)

    @pl.when(jnp.logical_not(is_end))
    def _():
        pl.semaphore_signal(barrier, inc=1, device_id=outer, device_id_type=MESH)
        pl.semaphore_wait(barrier, 3)

    @pl.when(is_end)
    def _():
        pl.semaphore_wait(barrier, 2)

    given_copies = []
    for i in range(given):
        spot = pl.multiple_of(spots[count - given + i](row) - base, 16)
        given_copies.append(
            pltpu.make_async_remote_copy(
                src_ref=gives[i], dst_ref=got_give.at[pl.ds(spot, sizes[count - given + i])],
                send_sem=send_give.at[i], recv_sem=give_sem.at[i],
                device_id=other, device_id_type=MESH))
        given_copies[-1].start()
    for copy in loads:
        copy.wait()

    def add_given(t):
        @pl.when(t == first)
        def _():
            for copy in given_copies:
                copy.wait()

        @pl.when(t >= first)
        def _():
            held[at(t)] = (
                held[at(t)].astype(F32) + got_give[at(t - first)].astype(F32)
            ).astype(BF)

    def at(t):
        return pl.ds(pl.multiple_of(t * chunk, chunk), chunk)

    def inward(t):
        return pltpu.make_async_remote_copy(
            src_ref=held.at[at(t)], dst_ref=got_in.at[at(t)], send_sem=send_in.at[t],
            recv_sem=in_sem.at[t], device_id=inner, device_id_type=MESH)

    def middle(t):
        return pltpu.make_async_remote_copy(
            src_ref=held.at[at(t)], dst_ref=got_mid.at[at(t)], send_sem=send_mid.at[t],
            recv_sem=mid_sem.at[t], device_id=inner, device_id_type=MESH)

    def outward(t, source):
        return pltpu.make_async_remote_copy(
            src_ref=source, dst_ref=out.at[side, at(t)], send_sem=send_out.at[t],
            recv_sem=out_sem.at[t], device_id=outer, device_id_type=MESH)

    def across(t, source):
        return pltpu.make_async_remote_copy(
            src_ref=source, dst_ref=out.at[side, at(t)], send_sem=send_side.at[t],
            recv_sem=side_sem.at[t], device_id=other, device_id_type=MESH)

    def store(t):
        return pltpu.make_async_copy(got_in.at[at(t)], out.at[side, at(t)], keep.at[t])

    def mid_loop(t, _):
        @pl.when(t < steps)
        def _():
            add_given(t)

            @pl.when(jnp.logical_not(is_end))
            def _():
                inward(t).wait_recv()
                held[at(t)] = (held[at(t)].astype(F32) + got_in[at(t)].astype(F32)).astype(BF)
            @pl.when(t >= deep)
            def _():
                middle(t - deep).wait_send()
            middle(t).start()

        @pl.when(t >= ahead)
        def _():
            u = t - ahead
            middle(u).wait_recv()
            got_in[at(u)] = (held[at(u)].astype(F32) + got_mid[at(u)].astype(F32)).astype(BF)
            store(u).start()
            @pl.when(u >= deep)
            def _():
                @pl.when(jnp.logical_not(is_end))
                def _():
                    outward(u - deep, got_in.at[at(u)]).wait_send()
                across(u - deep, got_in.at[at(u)]).wait_send()
            @pl.when(jnp.logical_not(is_end))
            def _():
                outward(u, got_in.at[at(u)]).start()
            across(u, got_in.at[at(u)]).start()
        return 0

    def far_loop(t, _):
        @pl.when(t < steps)
        def _():
            add_given(t)

            @pl.when(jnp.logical_not(is_end))
            def _():
                inward(t).wait_recv()
                held[at(t)] = (held[at(t)].astype(F32) + got_in[at(t)].astype(F32)).astype(BF)
            @pl.when(t >= deep)
            def _():
                inward(t - deep).wait_send()
            inward(t).start()

        @pl.when(t >= lag)
        def _():
            u = t - lag
            outward(u, out.at[side, at(u)]).wait_recv()
            @pl.when(u >= deep)
            def _():
                @pl.when(jnp.logical_not(is_end))
                def _():
                    outward(u - deep, out.at[side, at(u)]).wait_send()
                across(u - deep, out.at[side, at(u)]).wait_send()
            @pl.when(jnp.logical_not(is_end))
            def _():
                outward(u, out.at[side, at(u)]).start()
            across(u, out.at[side, at(u)]).start()
        return 0

    @pl.when(is_mid)
    def _():
        lax.fori_loop(0, steps + ahead, mid_loop, 0)
        def finish(t, _):
            store(t).wait()
            across(t, got_in.at[at(t)]).wait_recv()
            @pl.when(t >= steps - deep)
            def _():
                middle(t).wait_send()
                across(t, got_in.at[at(t)]).wait_send()
                @pl.when(jnp.logical_not(is_end))
                def _():
                    outward(t, got_in.at[at(t)]).wait_send()
            return 0
        lax.fori_loop(0, steps, finish, 0)

    @pl.when(jnp.logical_not(is_mid))
    def _():
        lax.fori_loop(0, steps + lag, far_loop, 0)
        def finish(t, _):
            across(t, out.at[side, at(t)]).wait_recv()
            @pl.when(t >= steps - deep)
            def _():
                inward(t).wait_send()
                across(t, out.at[side, at(t)]).wait_send()
                @pl.when(jnp.logical_not(is_end))
                def _():
                    outward(t, out.at[side, at(t)]).wait_send()
            return 0
        lax.fori_loop(0, steps, finish, 0)


def line_sum(pieces, spots, gives, chunk, lag=8, ahead=2, deep=2):
    sizes = [p.shape[0] for p in pieces]
    rows, width = sum(sizes), pieces[0].shape[1]
    steps = rows // chunk
    given_rows = sum(g.shape[0] for g in gives)
    dma = pltpu.SemaphoreType.DMA
    return pl.pallas_call(
        functools.partial(line_kernel, sizes, spots, len(gives), chunk, lag, ahead, deep),
        out_shape=jax.ShapeDtypeStruct((2, rows, width), BF),
        in_specs=[pl.BlockSpec(memory_space=pl.ANY)] * (len(pieces) + len(gives)),
        out_specs=pl.BlockSpec(memory_space=pl.ANY),
        scratch_shapes=[pltpu.VMEM((rows, width), BF)] * 3
        + [pltpu.VMEM((given_rows, width), BF)]
        + [dma((len(pieces),))]
        + [dma((steps,))] * 9
        + [dma((len(gives),))] * 2,
        compiler_params=pltpu.CompilerParams(
            collective_id=0, has_side_effects=True, vmem_limit_bytes=58 * 2**20
        ),
        name="line_sum",
    )(*pieces, *gives)


def pack(operand, width):
    rows, columns = operand.shape
    if columns == width:
        return operand
    if columns > width:
        return jnp.concatenate(
            [operand[:, i : i + width] for i in range(0, columns, width)], axis=0
        )
    times = width // columns
    step = rows // times
    return jnp.concatenate([operand[i * step : (i + 1) * step] for i in range(times)], axis=1)


def unpack(operand, columns):
    rows, width = operand.shape
    if columns == width:
        return operand
    if columns > width:
        step = rows * width // columns
        return jnp.concatenate(
            [operand[i * step : (i + 1) * step] for i in range(columns // width)], axis=1
        )
    return jnp.concatenate(
        [operand[:, i : i + columns] for i in range(0, width, columns)], axis=0
    )


def hop(operand, axis, step):
    size = lax.axis_size(axis)
    return operand + lax.ppermute(operand, axis, [(i, i ^ step) for i in range(size)])


def turned(operand, cosine, sine_table):
    return operand * cosine + pltpu.roll(operand, HEAD // 2, 1) * sine_table


def allowed_pairs(spot_col, spot_row):
    return (spot_col[:, 0:1] == spot_row[0:1, :]) & (spot_row[1:2, :] <= spot_col[:, 1:2])


def attention_kernel(
    x_ref, own_ref, got_ref, out_own, out_got, cos_ref, sin_ref, col_ref, row_ref, *refs
):
    earlier, (q_out, k_out, v_out, att_out, lse_out, kept, sent) = refs[:-7], refs[-7:]
    half = x_ref.shape[1] // 2
    wide = out_own.shape[0]
    own = kept.shape[0]
    near, far = x_ref[:, :half], x_ref[:, half:]
    cosine, sine_table = cos_ref[...], sin_ref[...]
    for which, out in enumerate((q_out, k_out, v_out)):
        at = slice(which * wide, (which + 1) * wide)
        raw = dot(near, own_ref[:, at]) + dot(far, got_ref[:, at])
        for h in range(wide // HEAD):
            head = slice(h * HEAD, (h + 1) * HEAD)
            value = raw[:, head]
            if which < 2:
                value = turned(value, cosine, sine_table)
            out[:, head] = value.astype(BF)
    allowed = allowed_pairs(col_ref[...], row_ref[...])
    for h in range(wide // HEAD):
        head = slice(h * HEAD, (h + 1) * HEAD)
        keys, values = k_out[:, head], v_out[:, head]
        if earlier:
            keys = jnp.concatenate([earlier[0][:, head], keys], axis=0)
            values = jnp.concatenate([earlier[1][:, head], values], axis=0)
        scores = contract_cols(q_out[:, head], keys) * (1.0 / math.sqrt(HEAD))
        scores = jnp.where(allowed, scores, NEG)
        row_max = jnp.max(scores, axis=-1, keepdims=True)
        shares = jnp.exp(scores - row_max)
        totals = jnp.sum(shares, axis=-1, keepdims=True)
        shares = (shares / totals).astype(BF)
        att_out[:, head] = dot(shares, values).astype(BF)
        lse_out[:, head] = jnp.broadcast_to(row_max + jnp.log(totals), (2 * own, HEAD))
    near, far = dot(att_out[...], out_own[...]), dot(att_out[...], out_got[...])
    kept[:, :half] = near[:own]
    kept[:, half:] = far[:own]
    sent[:, :half] = far[own:].astype(BF)
    sent[:, half:] = near[own:].astype(BF)


def attention_back_kernel(
    own_rows, other_rows, out_own, out_got, cos_ref, sin_ref, col_ref, row_ref,
    lse_ref, q_ref, k_ref, v_ref, *refs
):
    span, wide = q_ref.shape
    g_ref = jnp.concatenate([own_rows[...], other_rows[...]], axis=0)
    half = g_ref.shape[1] // 2
    factor = 1.0 / math.sqrt(HEAD)
    cosine, sine_table = cos_ref[...], -sin_ref[...]
    grads = contract_cols(g_ref[:, :half], out_own[...])
    grads = (grads + contract_cols(g_ref[:, half:], out_got[...])).astype(BF)
    allowed = allowed_pairs(col_ref[...], row_ref[...])
    last = len(refs) > 3
    for h in range(wide // HEAD):
        head = slice(h * HEAD, (h + 1) * HEAD)
        queries, gradient = q_ref[:, head], grads[:, head]
        keys, values = k_ref[:, head], v_ref[:, head]
        if last:
            keys = jnp.concatenate([refs[0][:, head], keys], axis=0)
            values = jnp.concatenate([refs[1][:, head], values], axis=0)
        scores = jnp.where(allowed, contract_cols(queries, keys) * factor, NEG)
        shares = jnp.exp(scores - lse_ref[:, h * HEAD : h * HEAD + 1])
        grad_shares = contract_cols(gradient, values)
        centre = jnp.sum(shares * grad_shares, axis=-1, keepdims=True)
        grad_scores = (shares * (grad_shares - centre)).astype(BF)
        grad_q = turned(dot(grad_scores, keys) * factor, cosine, sine_table)
        grad_k = contract_rows(grad_scores, queries) * factor
        grad_v = contract_rows(shares.astype(BF), gradient)
        if not last:
            q_out, k_out, v_out = refs
            q_out[:, head] = grad_q.astype(BF)
            k_out[:, head] = grad_k
            v_out[:, head] = grad_v
        else:
            cos_first, sin_first, k_part, v_part, first_out, back_out = refs[2:]
            back_out[:, head] = grad_q.astype(BF)
            at = slice(wide + h * HEAD, wide + (h + 1) * HEAD)
            back_out[:, at] = turned(grad_k[span:], cosine, sine_table).astype(BF)
            first = grad_k[:span] + k_part[:, head]
            first_out[:, head] = turned(first, cos_first[...], -sin_first[...]).astype(BF)
            at = slice(2 * wide + h * HEAD, 2 * wide + (h + 1) * HEAD)
            back_out[:, at] = grad_v[span:].astype(BF)
            at = slice(wide + h * HEAD, wide + (h + 1) * HEAD)
            first_out[:, at] = (grad_v[:span] + v_part[:, head]).astype(BF)


def last_kernel(a_ref, b_ref, own_ref, got_ref, kept_a, sent_a, kept_b, sent_b):
    half = own_ref.shape[0]
    own = kept_a.shape[0]
    for ref, kept, sent in ((a_ref, kept_a, sent_a), (b_ref, kept_b, sent_b)):
        near, far = contract_cols(ref[...], own_ref[...]), contract_cols(ref[...], got_ref[...])
        kept[:, :half] = near[:own]
        kept[:, half:] = far[:own]
        sent[:, :half] = far[own:].astype(BF)
        sent[:, half:] = near[own:].astype(BF)


def in_vmem(kernel, name, out_shape, operands, flops=8 * 10**9):
    return pl.pallas_call(
        kernel,
        out_shape=out_shape,
        in_specs=[pl.BlockSpec(memory_space=pltpu.VMEM)] * len(operands),
        out_specs=[pl.BlockSpec(memory_space=pltpu.VMEM)] * len(out_shape),
        compiler_params=pltpu.CompilerParams(vmem_limit_bytes=52 * 2**20),
        cost_estimate=pl.CostEstimate(
            flops=flops, bytes_accessed=flops // 400, transcendentals=flops // 4000
        ),
        name=name,
    )(*operands)


def moments(operand):
    average = jnp.mean(operand, axis=-1, keepdims=True)
    centre = operand - average
    factor = lax.rsqrt(jnp.mean(centre * centre, axis=-1, keepdims=True) + EPS)
    return average, factor


def normalize_back(gradient, normed, factor):
    mean = jnp.mean(gradient, axis=-1, keepdims=True)
    crossed = jnp.mean(gradient * normed, axis=-1, keepdims=True)
    return factor * (gradient - mean - normed * crossed)


def feed_forward_kernel(
    r_ref, own_rows, other_rows, gate_own, gate_got, up_own, up_got, down_own, down_got,
    gate_out, up_out, act_keep, act_give, kept, sent, total, x_ref, *, side_steps,
):
    step, last = pl.program_id(0), pl.num_programs(0) - 1
    half = x_ref.shape[1] // 2
    own = kept.shape[0]

    @pl.when(step == 0)
    def _():
        x_ref[:own] = own_rows[...]
        x_ref[own:] = other_rows[...]

    near, far = x_ref[:, :half], x_ref[:, half:]
    gate = dot(near, gate_own[...]) + dot(far, gate_got[...])
    up = dot(near, up_own[...]) + dot(far, up_got[...])
    gate_out[...] = gate
    up_out[...] = up
    act = (gate * jax.nn.sigmoid(gate) * up).astype(BF)
    mine = step // side_steps == r_ref[1]

    @pl.when(mine)
    def _():
        act_keep[...] = act

    @pl.when(jnp.logical_not(mine))
    def _():
        act_give[...] = act

    near, far = dot(act, down_own[...]), dot(act, down_got[...])

    @pl.when(step == 0)
    def _():
        total[:, :half] = near
        total[:, half:] = far

    @pl.when(step > 0)
    def _():
        total[:, :half] += near
        total[:, half:] += far

    @pl.when(step == last)
    def _():
        kept[...] = total[:own]
        sent[:, :half] = total[own:, half:].astype(BF)
        sent[:, half:] = total[own:, :half].astype(BF)


def feed_forward_back_kernel(
    r_ref, own_rows, other_rows, gate_ref, up_ref,
    gate_own, gate_got, up_own, up_got, down_own, down_got,
    gate_keep, gate_give, up_keep, up_give, kept, sent, total, g_ref, *, side_steps,
):
    step, last = pl.program_id(0), pl.num_programs(0) - 1
    half = g_ref.shape[1] // 2
    own = kept.shape[0]

    @pl.when(step == 0)
    def _():
        g_ref[:own] = own_rows[...]
        g_ref[own:] = other_rows[...]

    grad = contract_cols(g_ref[:, :half], down_own[...]) + contract_cols(
        g_ref[:, half:], down_got[...]
    )
    gate, up = gate_ref[...], up_ref[...]
    sigmoid = jax.nn.sigmoid(gate)
    gate_back = (grad * up * sigmoid * (1.0 + gate * (1.0 - sigmoid))).astype(BF)
    up_back = (grad * gate * sigmoid).astype(BF)
    mine = step // side_steps == r_ref[1]

    @pl.when(mine)
    def _():
        gate_keep[...] = gate_back
        up_keep[...] = up_back

    @pl.when(jnp.logical_not(mine))
    def _():
        gate_give[...] = gate_back
        up_give[...] = up_back

    near = contract_cols(gate_back, gate_own[...]) + contract_cols(up_back, up_own[...])
    far = contract_cols(gate_back, gate_got[...]) + contract_cols(up_back, up_got[...])

    @pl.when(step == 0)
    def _():
        total[:, :half] = near
        total[:, half:] = far

    @pl.when(step > 0)
    def _():
        total[:, :half] += near
        total[:, half:] += far

    @pl.when(step == last)
    def _():
        kept[...] = total[:own]
        sent[:, :half] = total[own:, half:].astype(BF)
        sent[:, half:] = total[own:, :half].astype(BF)


def feed_forward(back, where, operand, saved, weights, got, units, tile):
    own, width = operand[0].shape
    half, span, steps = width // 2, 2 * own, units // tile
    side_steps = steps // 2
    gate, up, down = weights
    gate_got, up_got, down_got = got

    def mine(i, r):
        return (0, jnp.clip(i - r[1] * side_steps, 0, side_steps - 1))

    def other(i, r):
        return (0, jnp.clip(i - (1 - r[1]) * side_steps, 0, side_steps - 1))

    whole = pl.BlockSpec((own, width), lambda i, r: (0, 0))
    wide = pl.BlockSpec((span, tile), lambda i, r: (0, i))
    into_own = pl.BlockSpec((half, tile), lambda i, r: (0, r[0] * steps + i))
    into_got = pl.BlockSpec((half, tile), lambda i, r: (0, i))
    back_own = pl.BlockSpec((tile, half), lambda i, r: (r[0] * steps + i, 0))
    back_got = pl.BlockSpec((tile, half), lambda i, r: (i, 0))
    weight_specs = [into_own, into_got, into_own, into_got, back_own, back_got]
    keep, give = pl.BlockSpec((span, tile), mine), pl.BlockSpec((span, tile), other)
    ends = [pl.BlockSpec((own, width), lambda i, r: (0, 0))] * 2
    part = jax.ShapeDtypeStruct((span, units // 2), BF)
    full = jax.ShapeDtypeStruct((span, units), F32)
    end_shapes = [
        jax.ShapeDtypeStruct((own, width), F32),
        jax.ShapeDtypeStruct((own, width), BF),
    ]
    if back:
        kernel = feed_forward_back_kernel
        in_specs = [whole, whole, wide, wide] + weight_specs
        out_specs = [keep, give, keep, give] + ends
        out_shape = [part] * 4 + end_shapes
    else:
        kernel = feed_forward_kernel
        in_specs = [whole, whole] + weight_specs
        out_specs = [wide, wide, keep, give] + ends
        out_shape = [full] * 2 + [part] * 2 + end_shapes
    return pl.pallas_call(
        functools.partial(kernel, side_steps=side_steps),
        out_shape=out_shape,
        grid_spec=pltpu.PrefetchScalarGridSpec(
            num_scalar_prefetch=1,
            grid=(steps,),
            in_specs=in_specs,
            out_specs=out_specs,
            scratch_shapes=[pltpu.VMEM((span, width), F32), pltpu.VMEM((span, width), BF)],
        ),
        compiler_params=pltpu.CompilerParams(vmem_limit_bytes=52 * 2**20),
        cost_estimate=pl.CostEstimate(
            flops=6 * span * width * units,
            bytes_accessed=6 * width * units + 12 * span * units,
            transcendentals=span * units,
        ),
        name="feed_forward_back" if back else "feed_forward",
    )(where, *operand, *saved, gate, gate_got, up, up_got, down, down_got)


def widen_three(sums, down_shape, into_shape, size):
    def kernel(in_ref, *outs):
        for n, out in enumerate(outs):

            @pl.when(pl.program_id(0) // 4 == n)
            def _():
                out[...] = in_ref[0].astype(F32)

    def spot(n):
        if n == 0:
            return lambda t: (jnp.clip(t, 0, 3), 0)
        return lambda t: (0, jnp.clip(t - 4 * n, 0, 3))

    return pl.pallas_call(
        kernel,
        out_shape=[jax.ShapeDtypeStruct(x, F32) for x in (down_shape, into_shape, into_shape)],
        grid=(12,),
        in_specs=[pl.BlockSpec((1, size, size), lambda t: (t % 2, t // 2, 0))],
        out_specs=[pl.BlockSpec((size, size), spot(n)) for n in range(3)],
        compiler_params=pltpu.CompilerParams(vmem_limit_bytes=48 * 2**20),
        name="widen_three",
    )(sums)


def widen_four(sums, shape, starts, part):
    rows, columns = shape
    qk, v, o = (start // part for start in starts)

    def kernel(qk_a, qk_b, v_a, v_b, o_ref, q_out, k_out, v_out, o_out):
        step = pl.program_id(0)
        o_out[...] = o_ref[0].astype(F32)
        for core in range(2):
            for pair, out, at in ((0, q_out, 0), (1, k_out, 2)):
                for x, ref in enumerate((qk_a, qk_b)):
                    spot = (2 * core + x) * part
                    source = (at + core) * part
                    out[:, spot : spot + part] = ref[0, :, source : source + part].astype(F32)
        for high in range(2):

            @pl.when(step // 2 == high)
            def _():
                for core in range(2):
                    for x, ref in enumerate((v_a, v_b)):
                        spot = (2 * core + x) * part
                        source = (2 * high + core) * part
                        v_out[:, spot : spot + part] = ref[0, :, source : source + part].astype(F32)

    block = (1, part, columns)
    return pl.pallas_call(
        kernel,
        out_shape=[jax.ShapeDtypeStruct(shape, F32)] * 4,
        grid=(rows // part,),
        in_specs=[
            pl.BlockSpec(block, lambda i: (0, qk + i, 0)),
            pl.BlockSpec(block, lambda i: (1, qk + i, 0)),
            pl.BlockSpec(block, lambda i: (0, v + i % 2, 0)),
            pl.BlockSpec(block, lambda i: (1, v + i % 2, 0)),
            pl.BlockSpec(block, lambda i: (i % 2, o + i // 2, 0)),
        ],
        out_specs=[pl.BlockSpec((part, columns), lambda i: (i, 0))] * 4,
        compiler_params=pltpu.CompilerParams(vmem_limit_bytes=32 * 2**20),
        name="widen_four",
    )(sums, sums, sums, sums, sums)


def body(
    tokens,
    teacher,
    segments,
    valid_mask,
    query_weight,
    key_weight,
    value_weight,
    output_weight,
    gate_weight,
    up_weight,
    down_weight,
):
    rows = tokens.shape[0]
    cols = lax.axis_size("col")
    row = lax.axis_index("row")
    col = lax.axis_index("col")
    side = lax.axis_index("dp") % 2
    sides = [(i, i ^ 1) for i in range(lax.axis_size("dp"))]
    block = tokens.shape[1]
    half_width = block * cols
    wide = query_weight.shape[1] // 2
    units = gate_weight.shape[1] // 2
    part_units = units // 2
    part_wide = wide // 2
    tile = min(512, part_units)
    span = rows // 2
    own = span // 2
    first_row = row == 0
    where = jnp.stack([row, side]).astype(jnp.int32)
    tie = lax.optimization_barrier

    def swap(operand):
        return lax.ppermute(operand, "row", [(0, 1), (1, 0)])

    def cross(operand):
        return lax.ppermute(operand, "dp", sides)

    def gather_blocks(operand):
        if cols == 2:
            got = lax.ppermute(operand, "col", [(0, 1), (1, 0)])
            return ordered(col == 0, operand, got, 1)
        return lax.all_gather(operand, "col", axis=1, tiled=True)

    def from_chips(sent):
        if cols == 2:
            return lax.ppermute(sent.astype(BF), "col", [(0, 1), (1, 0)])
        sent = sent.astype(F32)
        return lax.psum(sent, "col") - sent

    def both_cores(kept):
        return [kept, swap(swap_halves(kept, 1))]

    def from_cores(first, second):
        other = swap(swap_halves(jnp.concatenate([first, second], axis=0), 1))
        return [first, other[:own], second, other[own:]]

    def sum_cores(near, far):
        sent = jnp.concatenate([far[own:], near[own:]], axis=1).astype(BF)
        return jnp.concatenate([near[:own], far[:own]], axis=1) + swap(sent).astype(F32)

    def local_order(vector):
        pieces = []
        for j in range(2):
            piece = vector[j * span : (j + 1) * span]
            pieces.append(ordered(first_row, piece[:own], piece[own:], 0))
        return pieces

    blocks = []
    for j in range(2):
        piece = tokens[j * span : (j + 1) * span]
        blocks.append(gather_blocks(ordered(first_row, piece[:own], piece[own:], 0)))

    targets = []
    for j in range(2):
        piece = teacher[j * span : (j + 1) * span]
        piece = ordered(first_row, piece[:own], piece[own:], 0)
        targets.append((piece[:own], swap(piece[own:])))
    slices = [take(w, 1 - row, units, 1) for w in (gate_weight, up_weight)]
    blocks[0], slices, targets = tie((blocks[0], slices, targets))

    def columns_of(core):
        return jnp.concatenate(
            [take(w, core, wide, 1) for w in (query_weight, key_weight, value_weight)], axis=1
        )

    qkv_own, qkv_got = columns_of(row), swap(columns_of(1 - row))
    out_own = take(output_weight, row, wide, 0)
    out_got = swap(take(output_weight, 1 - row, wide, 0))
    weights = (gate_weight, up_weight, down_weight)

    validity = valid_mask.astype(F32)
    token_total = jnp.sum(validity).reshape(1, 1)
    hops = [(axis, 1 << k) for axis in ("dp", "row", "col") for k in range(10)]
    hops = [(axis, step) for axis, step in hops if step < lax.axis_size(axis)]
    token_hops = [h for h in hops if h[0] == "dp"]
    segs = local_order(segments)
    places = local_order(jnp.arange(rows, dtype=jnp.int32))
    valids = [v[:own, None] for v in local_order(validity)]
    tables = [rope_tables(p) for p in places]
    spot_cols = [jnp.stack([g, p], axis=1) for g, p in zip(segs, places)]
    spot_rows = [
        jnp.stack([jnp.concatenate(segs[: j + 1]), jnp.concatenate(places[: j + 1])])
        for j in range(2)
    ]

    inputs, first_stats, low_first = [], [], []
    query_heads, key_heads, value_heads = [], [], []
    attended, logsums = [], []

    def first_norm(j, half):
        whole = jnp.concatenate([half, swap(swap_halves(half, 0))], axis=1)
        whole_f = whole.astype(F32)
        average, factor = moments(whole_f)
        inputs.append(whole[:own])
        first_stats.append((average[:own], factor[:own]))
        low_first.append(((whole_f - average) * factor).astype(BF))
        return low_first[j]

    def attention(j, operand):
        out = jax.ShapeDtypeStruct((span, wide), BF)
        q, k, v, heads, logsum, kept, sent = in_vmem(
            attention_kernel,
            "attention",
            [out] * 4
            + [
                jax.ShapeDtypeStruct((span, wide), F32),
                jax.ShapeDtypeStruct((own, 2 * half_width), F32),
                jax.ShapeDtypeStruct((own, 2 * half_width), BF),
            ],
            [operand, qkv_own, qkv_got, out_own, out_got, *tables[j], spot_cols[j], spot_rows[j]]
            + [x for pair in zip(key_heads, value_heads) for x in pair],
        )
        query_heads.append(q)
        key_heads.append(k)
        value_heads.append(v)
        attended.append(heads)
        logsums.append(logsum)
        return kept, sent

    hidden, second_stats, low_second = [], [], []

    def second_norm(j, part, got):
        hidden.append(inputs[j].astype(F32) + (part + got.astype(F32)))
        average, factor = moments(hidden[j])
        second_stats.append((average, factor))
        low_second.append(both_cores(((hidden[j] - average) * factor).astype(BF)))
        return low_second[j]

    saved, acts, act_gives = [], [], []

    def forward(operand, received):
        return feed_forward(False, where, operand, (), weights, received, units, tile)

    def after_forward(j, raw):
        gate_out, up_out, act_keep, act_give, kept, sent = raw
        saved.append((gate_out, up_out))
        acts.append(act_keep)
        act_gives.append(act_give)
        near, far = (t.astype(F32) for t in targets[j])
        minus = [jnp.where(col == b, near, 0.0) for b in range(cols)]
        minus += [jnp.where(col == b, far, 0.0) for b in range(cols)]
        part = kept + swap(sent).astype(F32) - jnp.concatenate(minus, axis=1)
        return part, (near, far)

    outputs, errors, grad_results, low_results = [], [], [], []

    def loss_of(j, part, got, targets):
        near, far = targets
        error = hidden[j] + (part + got.astype(F32))
        near_error = take(error[:, :half_width], col, block, 1)
        far_error = take(error[:, half_width:], col, block, 1)
        outputs.append(
            ordered(
                first_row,
                (near_error + near).astype(BF),
                swap((far_error + far).astype(BF)),
                0,
            )
        )
        errors.append(
            0.5 * jnp.sum(valids[j] * (near_error * near_error + far_error * far_error))
        )
        grad_results.append(scale * valids[j] * error)
        low_results.append(both_cores(grad_results[j].astype(BF)))
        return low_results[j]

    def backward(j, operand, received):
        return feed_forward(True, where, operand, saved[j], weights, received, units, tile)

    grad_hiddens, low_hiddens = [], []

    def second_norm_back(j, part, got):
        gradient = part + got.astype(F32)
        average, factor = second_stats[j]
        normed = (hidden[j] - average) * factor
        grad_hiddens.append(grad_results[j] + normalize_back(gradient, normed, factor))
        low_hiddens.append(both_cores(grad_hiddens[j].astype(BF)))
        return low_hiddens[j]

    def attention_back(j, operand, extra):
        first = jax.ShapeDtypeStruct((span, wide), F32)
        shapes = [jax.ShapeDtypeStruct((span, wide), BF), first, first]
        if j == 1:
            shapes = [jax.ShapeDtypeStruct((span, n * wide), BF) for n in (2, 3)]
        return in_vmem(
            attention_back_kernel,
            "attention_back",
            shapes,
            [
                *operand,
                out_own,
                out_got,
                *tables[j],
                spot_cols[j],
                spot_rows[j],
                logsums[j],
                query_heads[j],
                key_heads[j],
                value_heads[j],
                *extra,
            ],
        )

    def joined(pair):
        return pair[0] + swap(pair[1]).astype(F32)

    part_a = joined(attention(0, first_norm(0, blocks[0])))
    operand = first_norm(1, blocks[1])
    operand, part_a, low, token_total, core, slices = tie(
        (operand, part_a, part_a.astype(BF), token_total, 1 - row, slices)
    )
    got_a = from_chips(low)
    token_total = hop(token_total, *token_hops[0])
    pair = attention(1, operand)
    received = (
        swap(slices[0]),
        swap(slices[1]),
        swap(take(down_weight, core, units, 0)),
    )
    pair, got_a, token_total, received = tie((pair, got_a, token_total, received))
    part_b = joined(pair)
    two_a = second_norm(0, part_a, got_a)
    two_a, part_b, low, mine, token_total = tie(
        (two_a, part_b, part_b.astype(BF), two_a[0], token_total)
    )
    token_total = hop(token_total, *token_hops[1])
    got_b, cross_two_a = from_chips(low), cross(mine)
    raw = forward(two_a, received)
    raw, got_b, cross_two_a, token_total = tie((raw, got_b, cross_two_a, token_total))
    part_a, targets_a = after_forward(0, raw)
    two_b = second_norm(1, part_b, got_b)
    two_b, part_a, low, mine, token_total = tie(
        (two_b, part_a, part_a.astype(BF), two_b[0], token_total)
    )
    for step in token_hops[2:]:
        token_total = hop(token_total, *step)
    got_a, cross_two_b = from_chips(low), cross(mine)
    raw = forward(two_b, received)
    raw, got_a, cross_two_b, token_total = tie((raw, got_a, cross_two_b, token_total))
    scale = (rows * lax.axis_size("dp")) / token_total
    part_b, targets_b = after_forward(1, raw)
    low_a = loss_of(0, part_a, got_a, targets_a)
    low_a, part_b, low, mine = tie((low_a, part_b, part_b.astype(BF), act_gives[0]))
    got_b, cross_act_a = from_chips(low), cross(mine)
    raw = backward(0, low_a, received)
    raw, got_b, cross_act_a = tie((raw, got_b, cross_act_a))
    ups_a, part_a = raw[:4], joined(raw[4:])
    low_b = loss_of(1, part_b, got_b, targets_b)
    low_b, part_a, low, mine, error_sum = tie(
        (
            low_b,
            part_a,
            part_a.astype(BF),
            act_gives[1],
            (errors[0] + errors[1]).reshape(1, 1),
        )
    )
    error_sum = hop(error_sum, *hops[0])
    got_a, cross_act_b = from_chips(low), cross(mine)
    raw = backward(1, low_b, received)
    raw, got_a, cross_act_b, error_sum = tie((raw, got_a, cross_act_b, error_sum))
    ups_b, part_b = raw[:4], joined(raw[4:])
    hidden_a = second_norm_back(0, part_a, got_a)
    hidden_a, part_b, low, mine = tie((hidden_a, part_b, part_b.astype(BF), low_a[0]))
    got_b, cross_low_a = from_chips(low), cross(mine)
    parts = attention_back(0, hidden_a, [])
    parts, got_b, cross_low_a, error_sum = tie((parts, got_b, cross_low_a, error_sum))
    hidden_b = second_norm_back(1, part_b, got_b)
    hidden_b, parts, mine, error_sum = tie((hidden_b, parts, low_b[0], error_sum))
    cross_low_b = cross(mine)
    first_back, back_b = attention_back(
        1, hidden_b, [key_heads[0], value_heads[0], *tables[0], *parts[1:]]
    )
    first_back, back_b, cross_low_b, error_sum = tie(
        (first_back, back_b, cross_low_b, error_sum)
    )
    backs = [jnp.concatenate([parts[0], first_back], axis=1), back_b]
    gate_gives = [u[1] for u in (ups_a, ups_b)]
    up_gives = [u[3] for u in (ups_a, ups_b)]

    def split_rows(full):
        half = full.shape[0] // 2
        return full[:half], swap(full[half:])

    def split_cols(full):
        half = full.shape[1] // 2
        return full[:, :half], swap(full[:, half:])

    def together(lefts, rights):
        return jnp.concatenate(lefts, axis=0), jnp.concatenate(rights, axis=0)

    def product(lefts, rights):
        return contract_rows(lefts, rights).astype(BF)

    hiddens = together(attended, [*hidden_a, *hidden_b])
    firsts = together(low_first, backs)
    downs = together(
        [*acts, cross_act_a, cross_act_b], [*low_a, *low_b, *from_cores(cross_low_a, cross_low_b)]
    )
    downs, gate_gives, error_sum = tie((downs, gate_gives, error_sum))
    cross_gate_a, cross_gate_b = (cross(g) for g in gate_gives)
    for step in hops[1:]:
        error_sum = hop(error_sum, *step)
    grad_down = product(*downs)
    grad_down, backs = tie((grad_down, backs))
    ends = [jax.ShapeDtypeStruct((own, 2 * half_width), t) for t in (F32, BF)]
    raw = in_vmem(
        last_kernel, "first_norm_back", ends * 2, [*backs, qkv_own, qkv_got], flops=4000
    )
    raw, grad_down, cross_gate_a, cross_gate_b, up_gives, error_sum = tie(
        (raw, grad_down, cross_gate_a, cross_gate_b, up_gives, error_sum)
    )
    last_parts = [joined(raw[:2]), joined(raw[2:])]
    down_pair = split_cols(grad_down)
    firsts, up_gives = tie((firsts, up_gives))
    cross_up_a, cross_up_b = (cross(g) for g in up_gives)
    grad_qkv = product(*firsts)
    grad_qkv, hiddens, twos = tie(
        (
            grad_qkv,
            hiddens,
            ([*two_a, *two_b], [cross_two_a, cross_two_b], [ups_a[0], ups_b[0]]),
        )
    )
    qkv_pair = split_rows(grad_qkv)
    out_pair = split_cols(product(*hiddens))
    gates = [*twos[2], cross_gate_a, cross_gate_b]
    twos = [*twos[0], *from_cores(*twos[1])]
    gates = together(twos, gates)
    gates, qkv_pair, out_pair, cross_up_a, cross_up_b = tie(
        (gates, qkv_pair, out_pair, cross_up_a, cross_up_b)
    )
    grad_gate = product(*gates)
    gate_pair = split_rows(grad_gate)
    up_pair = split_rows(
        product(*together(twos, [ups_a[2], ups_b[2], cross_up_a, cross_up_b]))
    )

    def halves(pair, which):
        three = [
            ordered(
                first_row,
                *(take(p[:, i * wide : (i + 1) * wide], which, part_wide, 1) for p in pair),
                1,
            )
            for i in range(3)
        ]
        return [pack(jnp.concatenate(three[:2], axis=1), half_width), pack(three[2], half_width)]

    pieces, spots, starts = [], [], []
    total = 0
    out_mine = [take(p, side, part_wide, 0) for p in out_pair]
    out_give = [take(p, 1 - side, part_wide, 0) for p in out_pair]
    for pair in (down_pair, gate_pair, up_pair, out_mine):
        packed = [pack(p, half_width) for p in pair]
        size = packed[0].shape[0]
        pieces += packed
        spots += [
            lambda r, total=total, size=size: total + r * size,
            lambda r, total=total, size=size: total + (1 - r) * size,
        ]
        starts.append((total, size))
        total += 2 * size
    for packed in halves(qkv_pair, side):
        size = packed.shape[0]
        pieces.append(packed)
        spots.append(lambda r, total=total: total + 0 * r)
        starts.append((total, size))
        total += size
    gives = [pack(p, half_width) for p in out_give] + halves(qkv_pair, 1 - side)
    last_gots = [from_chips(p) for p in last_parts]
    sums = line_sum(pieces, spots, gives, chunk=min(256, total // 8))
    sums, last_parts, last_gots = tie((sums, last_parts, last_gots))

    if cols == 2 and part_units == half_width:
        grad_down, grad_gate, grad_up = widen_three(
            sums, down_weight.shape, gate_weight.shape, half_width
        )
        grad_query, grad_key, grad_value, grad_output = widen_four(
            sums, query_weight.shape, [starts[n][0] for n in (4, 5, 3)], part_wide
        )
    else:

        def blocks_of(which, columns):
            start, size = starts[which]
            return [
                unpack(sums[x, start + s * size : start + (s + 1) * size], columns)
                for s in range(2)
                for x in range(2)
            ]

        grad_down = jnp.concatenate(blocks_of(0, half_width), axis=0).astype(F32)
        grad_gate = jnp.concatenate(blocks_of(1, part_units), axis=1).astype(F32)
        grad_up = jnp.concatenate(blocks_of(2, part_units), axis=1).astype(F32)
        grad_output = jnp.concatenate(blocks_of(3, half_width), axis=0).astype(F32)
        three = [[], [], []]
        qk, v = (
            [unpack(sums[x, starts[n][0] : starts[n][0] + starts[n][1]], k * part_wide) for x in range(2)]
            for n, k in ((4, 4), (5, 2))
        )
        for s in range(2):
            for x in range(2):
                at = s * part_wide
                three[0].append(qk[x][:, at : at + part_wide])
                three[1].append(qk[x][:, 2 * part_wide + at : 2 * part_wide + at + part_wide])
                three[2].append(v[x][:, at : at + part_wide])
        grad_query, grad_key, grad_value = (
            jnp.concatenate(t, axis=1).astype(F32) for t in three
        )

    grad_tokens = []
    for j in range(2):
        gradient = last_parts[j] + last_gots[j].astype(F32)
        average, factor = first_stats[j]
        normed = (inputs[j].astype(F32) - average) * factor
        grads = grad_hiddens[j] + normalize_back(gradient, normed, factor)
        near = take(grads[:, :half_width], col, block, 1)
        far = take(grads[:, half_width:], col, block, 1)
        grad_tokens.append(ordered(first_row, near, swap(far), 0))
    loss_value = (error_sum / token_total)[0, 0]
    return (
        jnp.concatenate(outputs, axis=0),
        loss_value,
        jnp.concatenate(grad_tokens, axis=0),
        grad_query,
        grad_key,
        grad_value,
        grad_output,
        grad_gate,
        grad_up,
        grad_down,
    )


def solution(mesh):
    features = P("dp", ("row", "col"))
    into, back = P("row", "col"), P("col", "row")
    in_specs = (features, features, P("dp"), P("dp"), into, into, into, back, into, into, back)
    out_specs = (features, P(), features, into, into, into, back, into, into, back)
    return jax.shard_map(body, mesh=mesh, in_specs=in_specs, out_specs=out_specs, check_vma=False)
```
